128 devices in a mesh: dp: 4 (over z_lo, core), ctx: 32 (over y, x, z_hi).
Axes of the slice: x: 4, y: 4, z: 4 (z_hi: 2, z_lo: 2; z = z_hi * 2 + z_lo), core: 2. Of those that a mesh axis runs over, the one named last changes fastest.
Arguments:
- tokens_in: bfloat16 [4, 4096, 1536], P('dp', 'ctx'), may hold values from -6 to 6
- qkv_weight: bfloat16 [2048, 1536], P(('dp', 'ctx')), may hold values from -0.21875 to 0.21875
- qkv_bias: bfloat16 [2048], P(('dp', 'ctx')), may hold values from -3 to 3
- out_weight: bfloat16 [1536, 1536], P(('dp', 'ctx')), may hold values from -0.625 to 0.625
- norm_gains: bfloat16 [2, 1536], P(None, ('dp', 'ctx')), may hold values from 0.099609375 to 1.8984375
- gate_weight: bfloat16 [8960, 1536], P(('dp', 'ctx')), may hold values from -0.15625 to 0.15625
- up_weight: bfloat16 [8960, 1536], P(('dp', 'ctx')), may hold values from -0.15625 to 0.15625
- down_weight: bfloat16 [8960, 1536], P(('dp', 'ctx')), may hold values from -0.125 to 0.125
- doc_ids: int32 [4, 4096], P('dp'), may hold values from 0 to 2, as said below
- cotangent: bfloat16 [4, 4096, 1536], P('dp', 'ctx'), may hold values from -6 to 6
Outputs:
- layer_out: bfloat16 [4, 4096, 1536], P('dp', 'ctx')
- input_grad: float32 [4, 4096, 1536], P('dp', 'ctx')
- qkv_weight_grad: float32 [2048, 1536], P(('dp', 'ctx'))
- qkv_bias_grad: float32 [2048], P(('dp', 'ctx'))
- out_weight_grad: float32 [1536, 1536], P(('dp', 'ctx'))
- norm_gains_grad: float32 [2, 1536], P(None, ('dp', 'ctx'))
- gate_weight_grad: float32 [8960, 1536], P(('dp', 'ctx'))
- up_weight_grad: float32 [8960, 1536], P(('dp', 'ctx'))
- down_weight_grad: float32 [8960, 1536], P(('dp', 'ctx'))
The draws below stay inside these ranges and needn't reach their ends.
Inputs may be any that keep to these rules, and one draw needn't show every extreme that they name: `doc_ids`: in every sequence the ids never fall and take exactly the values 0, 1, 2; document 1 begins within the first half of 128 tokens and ends within the last half of 128 tokens; documents 0 and 2 are not empty.
All inputs are finite; a program needn't handle non-finite values.
Results may differ from the reference program's by a relative error of at most 0.033.
Values may be sent and summed in bfloat16 or wider, within the bound.
A program may use at most 512 MiB of HBM per device.

```python
import jax
import jax.numpy as jnp
from jax import lax

D = 1536
H = 12
KVH = 2
HD = 128
FF = 8960
TOK_DEV = 128
SEQS = 4
LEN = 4096
KEY_BLOCK = 512
HQ = 1536
QKV = 2048


def draw_doc_ids(key, part):
    key = jax.random.fold_in(key, 7)
    first_key, last_key = jax.random.split(key)
    begin = jax.random.randint(first_key, (SEQS, 1), 1, TOK_DEV // 2 + 1)
    finish = jax.random.randint(last_key, (SEQS, 1), LEN - TOK_DEV // 2, LEN)
    index = jnp.arange(LEN, dtype=jnp.int32)[None, :]
    return (index >= begin).astype(jnp.int32) + (index >= finish).astype(jnp.int32)


def steps_of(key, extent, pieces, low, top_value):
    factor_of, own = 1.0, jax.random.fold_in(key, 6)
    for dim, shards_of in pieces:
        steps = jnp.exp(jax.random.uniform(jax.random.fold_in(own, dim), (shards_of,), jnp.float32, low / len(pieces), top_value / len(pieces)))
        factor_of = factor_of * jnp.repeat(steps, extent[dim] // shards_of).reshape([-1 if axis == dim else 1 for axis in range(len(extent))])
    return factor_of


def centred(rng, dims, width, bound, pieces=(), kind=jnp.bfloat16):
    level = steps_of(rng, dims, pieces, -0.22, 0.18) if pieces else 1.0
    values = jax.random.normal(rng, dims, jnp.float32) * width * level
    return jnp.minimum(jnp.maximum(values, -bound), bound).astype(kind)


def setup_inputs(seed: int = 0) -> dict:
    arg_keys = jax.random.split(jax.random.key(seed), 11)
    return {
        "tokens_in": centred(arg_keys[0], (SEQS, LEN, D), 1.0, 6.0, ((0, 4), (1, 32))),
        "qkv_weight": centred(arg_keys[1], (QKV, D), (D // 2) ** -0.5, 0.21875, ((0, 128),)),
        "qkv_bias": centred(arg_keys[2], (QKV,), 0.5, 3.0, ((0, 128),)),
        "out_weight": centred(arg_keys[3], (HQ, D), (HQ // 16) ** -0.5, 0.625, ((0, 128),)),
        "norm_gains": jnp.clip(1.0 + 0.18 * jax.random.normal(arg_keys[4], (2, D), jnp.float32), 0.099609375, 1.8984375).astype(jnp.bfloat16),
        "gate_weight": centred(arg_keys[5], (FF, D), D ** -0.5, 0.15625, ((0, 128),)),
        "up_weight": centred(arg_keys[6], (FF, D), D ** -0.5, 0.15625, ((0, 128),)),
        "down_weight": centred(arg_keys[7], (FF, D), (FF // 4) ** -0.5, 0.125, ((0, 128),)),
        "doc_ids": draw_doc_ids(jax.random.fold_in(arg_keys[10], 71), 0),
        "cotangent": centred(arg_keys[9], (SEQS, LEN, D), 1.0, 6.0, ((0, 4), (1, 32))),
    }


@jax.custom_vjp
def low(v):
    return lax.optimization_barrier(v.astype(jnp.bfloat16)).astype(jnp.float32)

@jax.custom_vjp
def low_back(v):
    return v

def low_keep(v):
    return (low(v), None)

def low_pass(kept, grad):
    return (grad,)

def back_keep(v):
    return (v, None)

def back_low(kept, grad):
    return (low(grad),)
low.defvjp(low_keep, low_pass)
low_back.defvjp(back_keep, back_low)
norm_eps = 1e-06
rope_base = 1000000.0
doc_kinds = 3
highest = lax.Precision.HIGHEST

def positions_of(documents):
    index = jnp.arange(documents.shape[0], dtype=jnp.int32)
    kinds = jnp.arange(doc_kinds, dtype=jnp.int32)
    counts = lax.optimization_barrier(jnp.sum((documents[None, :] == kinds[:, None]).astype(jnp.int32), axis=1))
    starts = jnp.cumsum(counts) - counts
    first = lax.optimization_barrier(jnp.sum(jnp.where(documents[:, None] == kinds[None, :], starts[None, :], 0), axis=1))
    return (index - first).astype(jnp.int32)

def rope_tables(position):
    half = HD // 2
    inverse = rope_base ** (-(jnp.arange(half, dtype=jnp.float32) * 2.0 / HD))
    angle = position.astype(jnp.float32)[:, None] * inverse[None, :]
    angle = jnp.concatenate([angle, angle], axis=1)
    return (jnp.cos(angle), jnp.sin(angle))

def rotate(vector, cosine, sine):
    half = vector.shape[-1] // 2
    turned = jnp.concatenate([-vector[..., half:], vector[..., :half]], axis=-1)
    return vector * cosine[:, None, :] + turned * sine[:, None, :]

def rms_norm(vector, gain):
    factor = lax.rsqrt(lax.optimization_barrier(jnp.mean(vector * vector, axis=-1, keepdims=True)) + norm_eps)
    return vector * factor * gain

def layer(inputs, qkv_weight, qkv_bias, out_weight, norm_gains, gate_weight, up_weight, down_weight, cosine, sine, documents):
    length = inputs.shape[0]
    normed_one = low(rms_norm(inputs, norm_gains[0]))
    qkv = low_back(jnp.dot(normed_one, qkv_weight.T, precision=highest) + qkv_bias)
    queries = low(rotate(qkv[:, :HQ].reshape(length, H, HD), cosine, sine)).reshape(length, KVH, H // KVH, HD)
    keys_rot = low(rotate(qkv[:, HQ:HQ + KVH * HD].reshape(length, KVH, HD), cosine, sine))
    values = low(qkv[:, HQ + KVH * HD:].reshape(length, KVH, HD))
    index = jnp.arange(length, dtype=jnp.int32)
    scale = HD ** (-0.5)

    def attend_block(start):
        query_block = lax.dynamic_slice_in_dim(queries, start, KEY_BLOCK, 0)
        rows = start + jnp.arange(KEY_BLOCK, dtype=jnp.int32)
        row_docs = lax.dynamic_slice_in_dim(documents, start, KEY_BLOCK, 0)
        scores = low_back(jnp.einsum('qkgd,skd->kgqs', query_block, keys_rot, precision=highest) * scale)
        allowed = (index[None, :] <= rows[:, None]) & (documents[None, :] == row_docs[:, None])
        masked = jnp.where(allowed, scores, -1e+30)
        top_score = lax.optimization_barrier(jnp.max(masked, axis=-1, keepdims=True))
        expo = jnp.exp(masked - top_score)
        probs = low(expo / lax.optimization_barrier(jnp.sum(expo, axis=-1, keepdims=True)))
        return low(low_back(jnp.einsum('kgqs,skd->qkgd', probs, values, precision=highest)))
    starts = jnp.arange(0, length, KEY_BLOCK, dtype=jnp.int32)
    attended = lax.map(jax.checkpoint(attend_block), starts).reshape(length, HQ)
    middle = inputs + low_back(jnp.dot(attended, out_weight, precision=highest))
    normed_two = low(rms_norm(middle, norm_gains[1]))
    gate = low_back(jnp.dot(normed_two, gate_weight.T, precision=highest))
    upward = low_back(jnp.dot(normed_two, up_weight.T, precision=highest))
    hidden = low(jax.nn.silu(gate) * upward)
    return middle + low_back(jnp.dot(hidden, down_weight, precision=highest))

def reference(tokens_in, qkv_weight, qkv_bias, out_weight, norm_gains, gate_weight, up_weight, down_weight, doc_ids, cotangent):
    params = (qkv_weight.astype(jnp.float32), qkv_bias.astype(jnp.float32), out_weight.astype(jnp.float32), norm_gains.astype(jnp.float32), gate_weight.astype(jnp.float32), up_weight.astype(jnp.float32), down_weight.astype(jnp.float32))

    def one_sequence(carry, item):
        sequence, documents, cot_seq = item
        cosine, sine = rope_tables(positions_of(documents))

        def forward(inputs, w_qkv, b_qkv, w_out, gains, w_gate, w_up, w_down):
            return layer(inputs, w_qkv, b_qkv, w_out, gains, w_gate, w_up, w_down, cosine, sine, documents)
        result, pullback = jax.vjp(forward, sequence.astype(jnp.float32), *params)
        grads = pullback(cot_seq.astype(jnp.float32))
        updated = tuple((total + piece for total, piece in zip(carry, grads[1:])))
        return (updated, (result.astype(jnp.bfloat16), grads[0]))
    zeros = tuple((jnp.zeros(p.shape, jnp.float32) for p in params))
    totals, (layer_out, input_grad) = lax.scan(one_sequence, zeros, (tokens_in, doc_ids, cotangent))
    return (layer_out, input_grad, totals[0], totals[1], totals[2], totals[3], totals[4], totals[5], totals[6])
```

```python
import functools

import jax
import jax.numpy as jnp
from jax import lax
from jax.experimental import pallas as pl
from jax.experimental.pallas import tpu as pltpu
from jax.sharding import Mesh
from jax.sharding import PartitionSpec as P

H = 12
KVH = 2
HD = 128
HQ = 1536
D = 1536
TOK = 128
ROWS = 80

norm_eps = 1e-06
rope_base = 1000000.0
doc_kinds = 3

AXES = ("zl", "c", "y", "x", "zh")
SIZE = {"zl": 2, "c": 2, "y": 4, "x": 4, "zh": 2}
PARTS_OF = {"z": ("zl", "zh"), "x": ("x",), "y": ("y",), "c": ("c",), "zh": ("zh",)}
REACH = {"z": (1, 2, 3), "x": (1, 2, 3), "y": (1, 2, 3), "c": (1,), "zh": (1,)}
BF = jnp.bfloat16
F32 = jnp.float32
ANY = pl.BlockSpec(memory_space=pl.ANY)
VMEM = pl.BlockSpec(memory_space=pltpu.VMEM)


def here():
    return {a: lax.axis_index(a) for a in AXES}


def peer(me, axis, k):
    to = dict(me)
    if axis == "z":
        z = lax.rem(me["zh"] * 2 + me["zl"] + k, 4)
        to["zl"], to["zh"] = lax.rem(z, 2), lax.div(z, 2)
    else:
        to[axis] = lax.rem(me[axis] + k, SIZE[axis])
    return to


def device_id(at):
    return tuple(at[a] for a in AXES)


def place(dims, at, whole, tail=()):
    return tuple(slice(None) if d in whole else at[d] for d in dims) + tuple(tail)


class Links:
    def __init__(self, me, send, recv):
        self.me, self.send, self.recv, self.used = me, send, recv, 0

    def copy(self, src, dst, axis, k):
        i = self.used
        self.used += 1
        c = pltpu.make_async_remote_copy(
            src_ref=src,
            dst_ref=dst,
            send_sem=self.send.at[i],
            recv_sem=self.recv.at[i],
            device_id=device_id(peer(self.me, axis, k)),
            device_id_type=pl.DeviceIdType.MESH,
        )
        c.start()
        return c


def greet(me, axes):
    barrier = pltpu.get_barrier_semaphore()
    count = 0
    for axis in axes:
        for k in REACH[axis]:
            pl.semaphore_signal(
                barrier,
                inc=1,
                device_id=device_id(peer(me, axis, k)),
                device_id_type=pl.DeviceIdType.MESH,
            )
            count += 1
    pl.semaphore_wait(barrier, count)


def gather_stream(links, block, buf, dims, tail, order):
    me = links.me
    whole = ()
    for n, axis in enumerate(order):
        mine = place(dims, me, whole, tail)
        src = block if n == 0 else buf.at[mine]
        copies = [links.copy(src, buf.at[mine], axis, k) for k in REACH[axis]]
        yield
        for c in copies:
            c.wait()
        whole = whole + PARTS_OF[axis]


def run_streams(streams):
    live = list(streams)
    while live:
        live = [s for s in live if next(s, live) is not live]


def count_gather(orders):
    return sum(len(REACH[a]) for order in orders for a in order)


THIRDS = tuple((slice(None), slice(512 * i, 512 * (i + 1))) for i in range(3))
ORDERS = (("x", "y", "z"), ("y", "z", "x"), ("z", "x", "y"))
HALVES = tuple((slice(None), slice(768 * i, 768 * (i + 1))) for i in range(2))
FFN_ORDERS = (("y", "z"), ("z", "y"))
FFN_DIMS = ("zl", "y", "zh")
ROW_DIMS = ("x", "c")
KV_DIMS = ("y", "x", "zh")


def weights_kernel(*refs):
    qkv, out, gate, up, down, cot = refs[:6]
    qkv_all, out_all, gate_all, up_all, down_all, cot_all = refs[6:12]
    send, recv, local = refs[12:]
    me = here()
    links = Links(me, send, recv)
    own = []
    pairs = [
        (qkv, qkv_all, AXES),
        (out, out_all, AXES),
        (gate, gate_all, FFN_DIMS),
        (up, up_all, FFN_DIMS),
        (down, down_all, FFN_DIMS),
        (cot, cot_all, ROW_DIMS),
    ]
    for i, (a, b, dims) in enumerate(pairs):
        own.append(pltpu.make_async_copy(a, b.at[place(dims, me, ())], local.at[i]))
        own[-1].start()
    greet(me, ("x", "y", "z", "c"))
    for c in own:
        c.wait()
    streams = []
    for block, buf in ((qkv, qkv_all), (out, out_all)):
        for order, tail in zip(ORDERS, THIRDS, strict=True):
            streams.append(
                gather_stream(links, block.at[tail], buf, AXES, tail, order + ("c",))
            )
    streams.append(gather_stream(links, cot, cot_all, ROW_DIMS, (), ("x", "c")))
    for block, buf in ((gate, gate_all), (up, up_all), (down, down_all)):
        for order, tail in zip(FFN_ORDERS, HALVES, strict=True):
            streams.append(gather_stream(links, block.at[tail], buf, FFN_DIMS, tail, order))
    run_streams(streams)


def gather_weights(qkv, out, gate, up, down, cot):
    ffn = jax.ShapeDtypeStruct((2, 4, 2, ROWS, D), BF)
    every = jax.ShapeDtypeStruct((2, 2, 4, 4, 2, 16, D), BF)
    rows = jax.ShapeDtypeStruct((4, 2, TOK, D), BF)
    copies = 2 * count_gather([o + ("c",) for o in ORDERS]) + count_gather([("x", "c")])
    copies += 3 * count_gather(FFN_ORDERS)
    return pl.pallas_call(
        weights_kernel,
        out_shape=(every, every, ffn, ffn, ffn, rows),
        in_specs=[ANY] * 6,
        out_specs=(ANY,) * 6,
        scratch_shapes=[
            pltpu.SemaphoreType.DMA((copies,)),
            pltpu.SemaphoreType.DMA((copies,)),
            pltpu.SemaphoreType.DMA((6,)),
        ],
        compiler_params=pltpu.CompilerParams(collective_id=1, has_side_effects=True),
    )(qkv, out, gate, up, down, cot)


def keys_kernel(block, buf, send, recv, local):
    me = here()
    links = Links(me, send, recv)
    own = pltpu.make_async_copy(block, buf.at[place(KV_DIMS, me, ())], local)
    own.start()
    greet(me, ("zh", "x", "y"))
    own.wait()
    streams = []
    for half, order in enumerate((("zh", "x", "y"), ("zh", "y", "x"))):
        tail = (slice(None), slice(256 * half, 256 * (half + 1)))
        streams.append(gather_stream(links, block.at[tail], buf, KV_DIMS, tail, order))
    run_streams(streams)


def gather_keys(block):
    copies = 2 * count_gather([("zh", "x", "y")])
    return pl.pallas_call(
        keys_kernel,
        out_shape=jax.ShapeDtypeStruct((4, 4, 2, TOK, 512), BF),
        in_specs=[ANY],
        out_specs=ANY,
        scratch_shapes=[
            pltpu.SemaphoreType.DMA((copies,)),
            pltpu.SemaphoreType.DMA((copies,)),
            pltpu.SemaphoreType.DMA,
        ],
        compiler_params=pltpu.CompilerParams(collective_id=2, has_side_effects=True),
    )(block)


def rows_kernel(block, buf, send, recv, local):
    me = here()
    links = Links(me, send, recv)
    own = pltpu.make_async_copy(block, buf.at[place(ROW_DIMS, me, ())], local)
    own.start()
    greet(me, ("x", "c"))
    own.wait()
    run_streams([gather_stream(links, block, buf, ROW_DIMS, (), ("x", "c"))])


def gather_rows(block):
    copies = count_gather([("x", "c")])
    return pl.pallas_call(
        rows_kernel,
        out_shape=jax.ShapeDtypeStruct((4, 2, TOK, D), BF),
        in_specs=[ANY],
        out_specs=ANY,
        scratch_shapes=[
            pltpu.SemaphoreType.DMA((copies,)),
            pltpu.SemaphoreType.DMA((copies,)),
            pltpu.SemaphoreType.DMA,
        ],
        compiler_params=pltpu.CompilerParams(collective_id=3, has_side_effects=True),
    )(block)


def lead_of(dims):
    return tuple(SIZE[d] for d in dims)


def rest_of(dims, axis):
    return tuple(d for d in dims if d not in PARTS_OF[axis])


def scatter_scratch(dims, order, rows, cols):
    shapes = []
    for axis in order:
        dims = rest_of(dims, axis)
        shapes.append(pltpu.VMEM((len(REACH[axis]),) + lead_of(dims) + (rows, cols), BF))
        shapes.append(pltpu.VMEM(lead_of(dims) + (rows, cols), BF))
    return shapes


def sum_blocks(own, arrived, out, lead, rows, step):
    count = 1
    for n in lead:
        count *= n
    per = rows // step
    parts = arrived.shape[0]

    def body(i, carry):
        block, row = lax.div(i, per), lax.rem(i, per)
        index = []
        for n in reversed(lead):
            index.append(lax.rem(block, n))
            block = lax.div(block, n)
        at = tuple(reversed(index)) + (pl.ds(pl.multiple_of(row * step, step), step),)
        total = own[at].astype(F32)
        for p in range(parts):
            total = total + arrived[(p,) + at].astype(F32)
        out[at] = total.astype(out.dtype)
        return carry

    lax.fori_loop(0, count * per, body, 0)


def scatter_stream(links, local, source, dims, tail, order, scratch, out, rows, step):
    me = links.me
    now = None
    for n, axis in enumerate(order):
        arrived, own = scratch[2 * n], scratch[2 * n + 1]
        gone = PARTS_OF[axis]
        keep = tuple(d for d in dims if d not in gone)
        end = tail if n == 0 else ()
        base = source if n == 0 else now
        copies = []
        for k in REACH[axis]:
            to = peer(me, axis, k)
            src = base.at[place(dims, to, keep, end)]
            copies.append(links.copy(src, arrived.at[k - 1], axis, k))
        held = base.at[place(dims, me, keep, end)]
        if n == 0:
            mine = pltpu.make_async_copy(held, own, local)
            mine.start()
        yield
        if n == 0:
            mine.wait()
            held = own
        for c in copies:
            c.wait()
        target = out if n == len(order) - 1 else own
        sum_blocks(held, arrived, target, lead_of(keep), rows, step)
        now, dims = own, keep


def rows_scatter_kernel(first, second, out_a, out_b, send, recv, local, *scratch):
    me = here()
    links = Links(me, send, recv)
    greet(me, ("x", "c"))
    half = len(scratch) // 2
    run_streams(
        [
            scatter_stream(
                links, local.at[0], first, ROW_DIMS, (), ("c", "x"), scratch[:half], out_a, TOK, 16
            ),
            scatter_stream(
                links, local.at[1], second, ROW_DIMS, (), ("c", "x"), scratch[half:], out_b, TOK, 16
            ),
        ]
    )


def scatter_rows(first, second):
    copies = 2 * count_gather([("c", "x")])
    one = jax.ShapeDtypeStruct((TOK, D), F32)
    return pl.pallas_call(
        rows_scatter_kernel,
        out_shape=(one, one),
        in_specs=[ANY] * 2,
        out_specs=(VMEM,) * 2,
        scratch_shapes=[
            pltpu.SemaphoreType.DMA((copies,)),
            pltpu.SemaphoreType.DMA((copies,)),
            pltpu.SemaphoreType.DMA((2,)),
        ]
        + 2 * scatter_scratch(ROW_DIMS, ("c", "x"), TOK, D),
        compiler_params=pltpu.CompilerParams(
            collective_id=4, has_side_effects=True, vmem_limit_bytes=48 * 2**20
        ),
    )(first, second)


KV_ORDERS = (("y", "x", "zh"), ("x", "y", "zh"))


def keys_scatter_kernel(source, out, send, recv, local, *scratch):
    me = here()
    links = Links(me, send, recv)
    greet(me, ("zh", "x", "y"))
    streams = []
    for half, order in enumerate(KV_ORDERS):
        tail = (slice(None), slice(256 * half, 256 * (half + 1)))
        part = scratch[6 * half : 6 * half + 6]
        streams.append(
            scatter_stream(
                links, local.at[half], source, KV_DIMS, tail, order, part, out.at[half], TOK, 32
            )
        )
    run_streams(streams)


def scatter_keys(source):
    copies = count_gather(KV_ORDERS)
    return pl.pallas_call(
        keys_scatter_kernel,
        out_shape=jax.ShapeDtypeStruct((2, TOK, 256), F32),
        in_specs=[ANY],
        out_specs=VMEM,
        scratch_shapes=[
            pltpu.SemaphoreType.DMA((copies,)),
            pltpu.SemaphoreType.DMA((copies,)),
            pltpu.SemaphoreType.DMA((2,)),
        ]
        + [s for order in KV_ORDERS for s in scatter_scratch(KV_DIMS, order, TOK, 256)],
        compiler_params=pltpu.CompilerParams(
            collective_id=5, has_side_effects=True, vmem_limit_bytes=48 * 2**20
        ),
    )(source)


ALL_ORDERS = tuple(("c",) + o for o in ORDERS)


def weight_grads_kernel(*refs):
    sources, outs = refs[:5], refs[5:10]
    send, recv, local = refs[10:13]
    scratch = list(refs[13:])
    me = here()
    links = Links(me, send, recv)
    greet(me, ("x", "y", "z", "c"))
    streams = []
    used = 0
    for source, out in zip(sources[:2], outs[:2], strict=True):
        for order, tail in zip(ALL_ORDERS, THIRDS, strict=True):
            part, scratch = scratch[:8], scratch[8:]
            streams.append(
                scatter_stream(
                    links, local.at[used], source, AXES, tail, order, part, out.at[tail], 16, 16
                )
            )
            used += 1
    for source, out in zip(sources[2:], outs[2:], strict=True):
        for order, tail in zip(FFN_ORDERS, HALVES, strict=True):
            part, scratch = scratch[:4], scratch[4:]
            streams.append(
                scatter_stream(
                    links, local.at[used], source, FFN_DIMS, tail, order, part, out.at[tail], ROWS, 16
                )
            )
            used += 1
    run_streams(streams)


def scatter_weight_grads(qkv, out, gate, up, down):
    copies = 2 * count_gather(ALL_ORDERS) + 3 * count_gather(FFN_ORDERS)
    scratch = []
    for _ in range(2):
        for order in ALL_ORDERS:
            scratch += scatter_scratch(AXES, order, 16, 512)
    for _ in range(3):
        for order in FFN_ORDERS:
            scratch += scatter_scratch(FFN_DIMS, order, ROWS, 768)
    attn = jax.ShapeDtypeStruct((16, D), F32)
    ffn = jax.ShapeDtypeStruct((ROWS, D), F32)
    return pl.pallas_call(
        weight_grads_kernel,
        out_shape=(attn, attn, ffn, ffn, ffn),
        in_specs=[ANY] * 5,
        out_specs=(VMEM,) * 5,
        scratch_shapes=[
            pltpu.SemaphoreType.DMA((copies,)),
            pltpu.SemaphoreType.DMA((copies,)),
            pltpu.SemaphoreType.DMA((12,)),
        ]
        + scratch,
        compiler_params=pltpu.CompilerParams(
            collective_id=6, has_side_effects=True, vmem_limit_bytes=60 * 2**20
        ),
    )(qkv, out, gate, up, down)


def positions_of(documents):
    index = jnp.arange(documents.shape[0], dtype=jnp.int32)
    kinds = jnp.arange(doc_kinds, dtype=jnp.int32)
    counts = jnp.sum((documents[None, :] == kinds[:, None]).astype(jnp.int32), axis=1)
    starts = jnp.cumsum(counts) - counts
    first = jnp.sum(jnp.where(documents[:, None] == kinds[None, :], starts[None, :], 0), axis=1)
    return index - first


def rope_tables(position):
    half = HD // 2
    inverse = rope_base ** (-(jnp.arange(half, dtype=jnp.float32) * 2.0 / HD))
    angle = position.astype(jnp.float32)[:, None] * inverse[None, :]
    angle = jnp.concatenate([angle, angle], axis=1)
    return (jnp.cos(angle), jnp.sin(angle))


def rotate(vector, cosine, sine):
    half = vector.shape[-1] // 2
    turned = jnp.concatenate([-vector[..., half:], vector[..., :half]], axis=-1)
    return vector * cosine[:, None, :] + turned * sine[:, None, :]


def rotate_back(grad_in, cosine, sine):
    half = grad_in.shape[-1] // 2
    moved = grad_in * sine[:, None, :]
    turned = jnp.concatenate([moved[..., half:], -moved[..., :half]], axis=-1)
    return grad_in * cosine[:, None, :] + turned


def dot(a, b, dims):
    return lax.dot_general(a, b, ((dims[:1], dims[1:]), ((), ())), preferred_element_type=F32)


def local(
    tokens_in,
    qkv_weight,
    qkv_bias,
    out_weight,
    norm_gains,
    gate_weight,
    up_weight,
    down_weight,
    doc_ids,
    cotangent,
):
    block_index = lax.axis_index("y") * 8 + lax.axis_index("x") * 2 + lax.axis_index("zh")
    inputs = tokens_in[0].astype(F32)
    count = TOK
    documents = doc_ids[0]
    length = documents.shape[0]
    key_block = min(512, length)
    num_blocks = length // key_block
    groups = H // KVH
    scale = HD ** (-0.5)
    cot_low = cotangent[0]

    small = jnp.concatenate([qkv_bias, norm_gains.reshape(-1), jnp.zeros((D - 40,), BF)])[None]
    out_block = jnp.concatenate([out_weight, small, jnp.zeros((3, D), BF)], axis=0)
    pad = ((0, ROWS - gate_weight.shape[0]), (0, 0))
    qkv_all, out_all, gate_all_w, up_all_w, down_all_w, cot_rows = gather_weights(
        qkv_weight,
        out_block,
        jnp.pad(gate_weight, pad),
        jnp.pad(up_weight, pad),
        jnp.pad(down_weight, pad),
        cot_low,
    )
    w_qkv = qkv_all.reshape(2048, D)
    out_all = out_all.reshape(128, 16, D)
    w_out = out_all[:, :12].reshape(HQ, D)
    b_qkv = out_all[:, 12, :16].reshape(2048)
    gain_one = out_all[:, 12, 16:28].reshape(D).astype(F32)
    gain_two = out_all[:, 12, 28:40].reshape(D).astype(F32)
    w_gate = gate_all_w.reshape(-1, D)
    w_up = up_all_w.reshape(-1, D)
    w_down = down_all_w.reshape(-1, D)
    cot_rows = cot_rows.reshape(-1, D)

    first_row = block_index * count
    my_rows = first_row + jnp.arange(count, dtype=jnp.int32)
    my_docs = lax.dynamic_slice_in_dim(documents, first_row, count, 0)
    my_pos = lax.dynamic_slice_in_dim(positions_of(documents), first_row, count, 0)
    cosine, sine = rope_tables(my_pos)
    factor_one = lax.rsqrt(jnp.mean(inputs * inputs, axis=-1, keepdims=True) + norm_eps)
    normed_one = (inputs * factor_one * gain_one).astype(BF)
    qkv = dot(normed_one, w_qkv, (1, 1)) + b_qkv.astype(F32)
    queries = (
        rotate(qkv[:, :HQ].reshape(count, H, HD), cosine, sine)
        .astype(BF)
        .reshape(count, KVH, groups, HD)
    )
    keys_mine = rotate(qkv[:, HQ : HQ + KVH * HD].reshape(count, KVH, HD), cosine, sine).astype(BF)
    keys_values = gather_keys(
        jnp.concatenate(
            [keys_mine.reshape(count, KVH * HD), qkv[:, HQ + KVH * HD :].astype(BF)], axis=1
        )
    ).reshape(length, 2, KVH, HD)
    all_keys, all_values = keys_values[:, 0], keys_values[:, 1]
    row_limit = first_row + count

    def scores_of(start):
        key_part = lax.dynamic_slice_in_dim(all_keys, start, key_block, 0)
        raw = jnp.einsum("qkgd,skd->kgqs", queries, key_part, preferred_element_type=F32) * scale
        key_rows = start + jnp.arange(key_block, dtype=jnp.int32)
        key_docs = lax.dynamic_slice_in_dim(documents, start, key_block, 0)
        allowed = (key_rows[None, :] <= my_rows[:, None]) & (key_docs[None, :] == my_docs[:, None])
        return (raw, allowed)

    def stats_step(block_id, carry):
        start = block_id * key_block

        def stats_live(state):
            raw, allowed = scores_of(start)
            masked = jnp.where(allowed, raw, -1e30)
            new_top = jnp.maximum(state[0], jnp.max(masked, axis=-1))
            new_total = state[1] * jnp.exp(state[0] - new_top) + jnp.sum(
                jnp.exp(masked - new_top[..., None]), axis=-1
            )
            return (new_top, new_total)

        return lax.cond(start < row_limit, stats_live, lambda state: state, carry)

    stat_shape = (KVH, groups, count)
    top_score, total_exp = lax.fori_loop(
        0,
        num_blocks,
        stats_step,
        (jnp.full(stat_shape, -1e30, F32), jnp.zeros(stat_shape, F32)),
    )
    log_total = top_score + jnp.log(total_exp)

    def probs_of(start):
        raw, allowed = scores_of(start)
        return jnp.where(allowed, jnp.exp(raw - log_total[..., None]), 0.0)

    def attend_step(block_id, carry):
        start = block_id * key_block

        def attend_live(state):
            probs = probs_of(start).astype(BF)
            value_part = lax.dynamic_slice_in_dim(all_values, start, key_block, 0)
            return state + jnp.einsum(
                "kgqs,skd->qkgd", probs, value_part, preferred_element_type=F32
            )

        return lax.cond(start < row_limit, attend_live, lambda state: state, carry)

    attended = lax.fori_loop(
        0, num_blocks, attend_step, jnp.zeros((count, KVH, groups, HD), F32)
    )
    attended_low = attended.reshape(count, HQ).astype(BF)
    middle = inputs + dot(attended_low, w_out, (1, 0))
    factor_two = lax.rsqrt(jnp.mean(middle * middle, axis=-1, keepdims=True) + norm_eps)
    normed_two = (middle * factor_two * gain_two).astype(BF)

    rows_two = gather_rows(normed_two).reshape(-1, D)
    gate = dot(rows_two, w_gate, (1, 1))
    upward = dot(rows_two, w_up, (1, 1))
    hidden_grad = dot(cot_rows, w_down, (1, 1))
    sigma = jax.nn.sigmoid(gate)
    hidden = (gate * sigma * upward).astype(BF)
    gate_grad = (hidden_grad * upward * sigma * (1.0 + gate * (1.0 - sigma))).astype(BF)
    upward_grad = (hidden_grad * gate * sigma).astype(BF)
    ffn_part = dot(hidden, w_down, (1, 0)).astype(BF)
    grad_part = (dot(gate_grad, w_gate, (1, 0)) + dot(upward_grad, w_up, (1, 0))).astype(BF)
    ffn_total, normed_two_grad = scatter_rows(
        ffn_part.reshape(4, 2, TOK, D), grad_part.reshape(4, 2, TOK, D)
    )
    layer_out = (middle + ffn_total).astype(BF)

    cot_full = cot_low.astype(F32)
    scaled_two = gain_two * normed_two_grad
    gain_two_grad = jnp.sum(normed_two_grad * middle * factor_two, axis=0)
    middle_grad = (
        cot_full
        + factor_two * scaled_two
        - middle * factor_two**3 * jnp.mean(scaled_two * middle, axis=-1, keepdims=True)
    )
    branch_grad = middle_grad.astype(BF)
    attended_grad = dot(branch_grad, w_out, (1, 1)).astype(BF).reshape(count, KVH, groups, HD)
    delta = jnp.transpose(jnp.sum(attended_grad.astype(F32) * attended, axis=-1), (1, 2, 0))

    def grad_step(block_id, carry):
        start = block_id * key_block

        def grad_live(state):
            query_grad, key_grads, value_grads = state
            probs = probs_of(start)
            key_part = lax.dynamic_slice_in_dim(all_keys, start, key_block, 0)
            value_part = lax.dynamic_slice_in_dim(all_values, start, key_block, 0)
            prob_grad = jnp.einsum(
                "qkgd,skd->kgqs", attended_grad, value_part, preferred_element_type=F32
            )
            score_grad = (probs * (prob_grad - delta[..., None])).astype(BF)
            query_grad = query_grad + jnp.einsum(
                "kgqs,skd->qkgd", score_grad, key_part, preferred_element_type=F32
            )
            key_term = jnp.einsum(
                "kgqs,qkgd->skd", score_grad, queries, preferred_element_type=F32
            )
            value_term = jnp.einsum(
                "kgqs,qkgd->skd", probs.astype(BF), attended_grad, preferred_element_type=F32
            )
            key_grads = lax.dynamic_update_slice_in_dim(key_grads, key_term, start, 0)
            value_grads = lax.dynamic_update_slice_in_dim(value_grads, value_term, start, 0)
            return (query_grad, key_grads, value_grads)

        return lax.cond(start < row_limit, grad_live, lambda state: state, carry)

    grad_init = (
        jnp.zeros((count, KVH, groups, HD), F32),
        jnp.zeros((length, KVH, HD), F32),
        jnp.zeros((length, KVH, HD), F32),
    )
    query_grad, key_grads, value_grads = lax.fori_loop(0, num_blocks, grad_step, grad_init)
    kv_part = jnp.concatenate(
        [(key_grads * scale).astype(BF).reshape(length, 256), value_grads.astype(BF).reshape(length, 256)],
        axis=1,
    )
    kv_grad = scatter_keys(kv_part.reshape(4, 4, 2, TOK, 512))
    query_pre = rotate_back((query_grad * scale).reshape(count, H, HD), cosine, sine).reshape(
        count, HQ
    )
    key_pre = rotate_back(kv_grad[0].reshape(count, KVH, HD), cosine, sine).reshape(count, KVH * HD)
    qkv_grad = jnp.concatenate([query_pre, key_pre, kv_grad[1]], axis=1).astype(BF)
    normed_one_grad = dot(qkv_grad, w_qkv, (1, 0))
    scaled_one = gain_one * normed_one_grad
    gain_one_grad = jnp.sum(normed_one_grad * inputs * factor_one, axis=0)
    input_grad = (
        middle_grad
        + factor_one * scaled_one
        - inputs * factor_one**3 * jnp.mean(scaled_one * inputs, axis=-1, keepdims=True)
    )

    qkv_part = dot(qkv_grad, normed_one, (0, 0)).astype(BF)
    out_part = dot(attended_low, branch_grad, (0, 0)).astype(BF)
    bias_part = jnp.sum(qkv_grad.astype(F32), axis=0).astype(BF)
    small_part = jnp.concatenate(
        [
            bias_part.reshape(128, 16),
            gain_one_grad.astype(BF).reshape(128, 12),
            gain_two_grad.astype(BF).reshape(128, 12),
            jnp.zeros((128, D - 40), BF),
        ],
        axis=1,
    )
    out_part = jnp.concatenate(
        [out_part.reshape(128, 12, D), small_part[:, None], jnp.zeros((128, 3, D), BF)], axis=1
    )
    gate_part = dot(gate_grad, rows_two, (0, 0)).astype(BF)
    up_part = dot(upward_grad, rows_two, (0, 0)).astype(BF)
    down_part = dot(hidden, cot_rows, (0, 0)).astype(BF)
    lead = lead_of(AXES) + (16, D)
    ffn_lead = lead_of(FFN_DIMS) + (ROWS, D)
    qkv_sum, out_sum, gate_sum, up_sum, down_sum = scatter_weight_grads(
        qkv_part.reshape(lead),
        out_part.reshape(lead),
        gate_part.reshape(ffn_lead),
        up_part.reshape(ffn_lead),
        down_part.reshape(ffn_lead),
    )
    units = gate_weight.shape[0]
    return (
        layer_out[None],
        input_grad[None],
        qkv_sum,
        out_sum[12, :16],
        out_sum[:12],
        out_sum[12, 16:40].reshape(2, 12),
        gate_sum[:units],
        up_sum[:units],
        down_sum[:units],
    )


def solution(mesh):
    fine = Mesh(mesh.devices.reshape(tuple(SIZE[a] for a in AXES)), AXES)
    dp, ctx = ("zl", "c"), ("y", "x", "zh")
    in_specs = (
        P(dp, ctx, None),
        P(AXES, None),
        P(AXES),
        P(AXES, None),
        P(None, AXES),
        P(AXES, None),
        P(AXES, None),
        P(AXES, None),
        P(dp, None),
        P(dp, ctx, None),
    )
    out_specs = (
        P(dp, ctx, None),
        P(dp, ctx, None),
        P(AXES, None),
        P(AXES),
        P(AXES, None),
        P(None, AXES),
        P(AXES, None),
        P(AXES, None),
        P(AXES, None),
    )
    return jax.shard_map(local, mesh=fine, in_specs=in_specs, out_specs=out_specs, check_vma=False)
```

```python
import math

import jax
import jax.numpy as jnp
from jax import lax
from jax.experimental import pallas as pl
from jax.experimental.pallas import tpu as pltpu
from jax.sharding import Mesh
from jax.sharding import PartitionSpec as P

H = 12
KVH = 2
HD = 128
HQ = 1536
D = 1536
TOK = 128
ROWS = 80

norm_eps = 1e-06
rope_base = 1000000.0
doc_kinds = 3

AXES = ("zl", "c", "y", "x", "zh")
SIZE = {"zl": 2, "c": 2, "y": 4, "x": 4, "zh": 2}
PARTS_OF = {"z": ("zl", "zh"), "x": ("x",), "y": ("y",), "c": ("c",), "zh": ("zh",)}
REACH = {"z": (1, 2, 3), "x": (1, 2, 3), "y": (1, 2, 3), "c": (1,), "zh": (1,)}
BF = jnp.bfloat16
F32 = jnp.float32
ANY = pl.BlockSpec(memory_space=pl.ANY)
VMEM = pl.BlockSpec(memory_space=pltpu.VMEM)


def here():
    return {a: lax.axis_index(a) for a in AXES}


def peer(me, axis, k):
    to = dict(me)
    if axis == "z":
        z = lax.rem(me["zh"] * 2 + me["zl"] + k, 4)
        to["zl"], to["zh"] = lax.rem(z, 2), lax.div(z, 2)
    else:
        to[axis] = lax.rem(me[axis] + k, SIZE[axis])
    return to


def device_id(at):
    return tuple(at[a] for a in AXES)


def place(dims, at, whole, tail=()):
    return tuple(slice(None) if d in whole else at[d] for d in dims) + tuple(tail)


class Links:
    def __init__(self, me, send, recv):
        self.me, self.send, self.recv, self.used = me, send, recv, 0

    def copy(self, src, dst, axis, k):
        i = self.used
        self.used += 1
        c = pltpu.make_async_remote_copy(
            src_ref=src,
            dst_ref=dst,
            send_sem=self.send.at[i],
            recv_sem=self.recv.at[i],
            device_id=device_id(peer(self.me, axis, k)),
            device_id_type=pl.DeviceIdType.MESH,
        )
        c.start()
        return c


def greet(me, axes):
    barrier = pltpu.get_barrier_semaphore()
    count = 0
    for axis in axes:
        for k in REACH[axis]:
            pl.semaphore_signal(
                barrier,
                inc=1,
                device_id=device_id(peer(me, axis, k)),
                device_id_type=pl.DeviceIdType.MESH,
            )
            count += 1
    pl.semaphore_wait(barrier, count)


def gather_stream(links, block, buf, dims, tail, order):
    me = links.me
    whole = ()
    for n, axis in enumerate(order):
        mine = place(dims, me, whole, tail)
        src = block if n == 0 else buf.at[mine]
        copies = [links.copy(src, buf.at[mine], axis, k) for k in REACH[axis]]
        yield
        for c in copies:
            c.wait()
        whole = whole + PARTS_OF[axis]


def run_streams(streams):
    live = list(streams)
    while live:
        live = [s for s in live if next(s, live) is not live]


def step(streams):
    for s in streams:
        next(s, None)


def count_gather(orders):
    return sum(len(REACH[a]) for order in orders for a in order)


THIRDS = tuple((slice(None), slice(512 * i, 512 * (i + 1))) for i in range(3))
ORDERS = (("x", "y", "z"), ("y", "z", "x"), ("z", "x", "y"))
HALVES = tuple((slice(None), slice(768 * i, 768 * (i + 1))) for i in range(2))
FFN_ORDERS = (("y", "z"), ("z", "y"))
FFN_DIMS = ("zl", "y", "zh")
ROW_DIMS = ("x", "c")
KV_DIMS = ("y", "x", "zh")


def weights_kernel(qkv, out, small, qkv_all, out_all, small_all, send, recv, local):
    me = here()
    links = Links(me, send, recv)
    own = []
    pairs = ((qkv, qkv_all), (out, out_all), (small, small_all))
    for i, (a, b) in enumerate(pairs):
        own.append(pltpu.make_async_copy(a, b.at[place(AXES, me, ())], local.at[i]))
        own[-1].start()
    greet(me, ("x", "y", "z", "c"))
    for c in own:
        c.wait()
    streams = []
    for block, buf in pairs[:2]:
        for order, tail in zip(ORDERS, THIRDS, strict=True):
            streams.append(
                gather_stream(links, block.at[tail], buf, AXES, tail, order + ("c",))
            )
    streams.append(gather_stream(links, small, small_all, AXES, (), ORDERS[0] + ("c",)))
    run_streams(streams)


def gather_weights(qkv, out, small):
    every = jax.ShapeDtypeStruct(lead_of(AXES) + (16, D), BF)
    smalls = jax.ShapeDtypeStruct(lead_of(AXES) + (16, 128), BF)
    copies = 2 * count_gather([o + ("c",) for o in ORDERS]) + count_gather([ORDERS[0] + ("c",)])
    return pl.pallas_call(
        weights_kernel,
        out_shape=(every, every, smalls),
        in_specs=[ANY] * 3,
        out_specs=(ANY,) * 3,
        scratch_shapes=[
            pltpu.SemaphoreType.DMA((copies,)),
            pltpu.SemaphoreType.DMA((copies,)),
            pltpu.SemaphoreType.DMA((3,)),
        ],
        compiler_params=pltpu.CompilerParams(collective_id=1, has_side_effects=True),
    )(qkv, out, small)


GROUP = H // KVH
GQ = GROUP * TOK
KEYS = 512
SCALE = HD**-0.5
TO_LOG2 = SCALE * math.log2(math.e)


def head(h):
    return slice(128 * h, 128 * (h + 1))


def turned(v):
    return pltpu.roll(v, 64, 1)


def key_blocks():
    ctx = lax.axis_index("y") * 8 + lax.axis_index("x") * 2 + lax.axis_index("zh")
    return lax.div(ctx, 4) + 1, ctx * TOK


def key_block_of(ref, b, cols):
    return ref[lax.div(b, 2), pl.ds(lax.rem(b, 2) * 2, 2), :, :, cols].reshape(KEYS, HD)


def allowed_keys(b, first, row):
    key = b * KEYS + lax.broadcasted_iota(jnp.int32, (KEYS, GQ), 0)
    query = row + lax.rem(lax.broadcasted_iota(jnp.int32, (1, GQ), 1), TOK)
    return (key <= query) & (key >= first)


def mm(a, b, contract):
    return lax.dot_general(
        a, b, ((contract[:1], contract[1:]), ((), ())), preferred_element_type=F32
    )


def attend_group(g, kv, qs, first, row, blocks, acc, stats):
    acc[...] = jnp.zeros_like(acc)
    stats[0:1] = jnp.full((1, GQ), -1e30, F32)
    stats[1:2] = jnp.zeros((1, GQ), F32)

    def body(b, carry):
        keys = key_block_of(kv, b, head(g))
        values = key_block_of(kv, b, head(2 + g))
        raw = mm(keys, qs[g], (1, 1)) * TO_LOG2
        raw = jnp.where(allowed_keys(b, first, row), raw, -1e30)
        old = stats[0:1]
        top = jnp.maximum(old, jnp.max(raw, axis=0, keepdims=True))
        probs = jnp.exp2(raw - top)
        shrink = jnp.exp2(old - top)
        stats[0:1] = top
        stats[1:2] = stats[1:2] * shrink + jnp.sum(probs, axis=0, keepdims=True)
        acc[...] = acc[...] * shrink + mm(values.T, probs.astype(BF), (1, 0))
        return carry

    lax.fori_loop(0, blocks, body, 0)


def attend_kernel(*refs):
    qkv, cosine, sine, first_ref, spread, gate, up, down, cot = refs[:9]
    kv, queries, attended, slots, lse = refs[9:14]
    gate_all, up_all, down_all, cot_all = refs[14:18]
    block, qs, acc, stats, send, recv, local = refs[18:]
    me = here()
    links = Links(me, send, recv)
    own = []
    pairs = (
        (gate, gate_all, FFN_DIMS),
        (up, up_all, FFN_DIMS),
        (down, down_all, FFN_DIMS),
        (cot, cot_all, ROW_DIMS),
    )
    for i, (a, b, dims) in enumerate(pairs):
        own.append(pltpu.make_async_copy(a, b.at[place(dims, me, ())], local.at[i]))
        own[-1].start()
    cos, sin = cosine[...], sine[...]
    for g in range(KVH):
        part = qkv[:, head(H + g)]
        block[:, head(g)] = (part * cos + turned(part) * sin).astype(BF)
        block[:, head(2 + g)] = qkv[:, head(H + 2 + g)].astype(BF)
    own.append(pltpu.make_async_copy(block, kv.at[place(KV_DIMS, me, ())], local.at[4]))
    own[-1].start()
    greet(me, ("zh", "x", "y", "z", "c"))
    keys = []
    for half, order in enumerate((("zh", "x", "y"), ("zh", "y", "x"))):
        tail = (slice(None), slice(256 * half, 256 * (half + 1)))
        keys.append(gather_stream(links, block.at[tail], kv, KV_DIMS, tail, order))
    weights = []
    for a, b, _ in pairs[:3]:
        for order, tail in zip(FFN_ORDERS, HALVES, strict=True):
            weights.append(gather_stream(links, a.at[tail], b, FFN_DIMS, tail, order))
    rows = [gather_stream(links, cot, cot_all, ROW_DIMS, (), ("x", "c"))]
    step(keys)
    step(weights)
    for c in own:
        c.wait()
    step(keys)
    for h in range(H):
        part = qkv[:, head(h)]
        turned_q = (part * cos + turned(part) * sin).astype(BF)
        queries[:, head(h)] = turned_q
        qs[h // GROUP, (h % GROUP) * TOK : (h % GROUP + 1) * TOK, :] = turned_q
    step(keys)
    step(weights)
    step(rows)
    step(keys)
    blocks, row = key_blocks()
    first = first_ref[0:1]
    for g in range(KVH):
        attend_group(g, kv, qs, first, row, blocks, acc, stats)
        total = stats[1:2]
        lse[g] = jnp.broadcast_to(stats[0:1] + jnp.log2(total), (8, GQ))
        acc[...] = acc[...] / total
        for i in range(GROUP):
            attended[:, head(GROUP * g + i)] = acc[:, head(i)].T
        step(rows)
    for i in range(4):
        part = attended[:, 384 * i : 384 * (i + 1)].astype(BF)
        slots[:, 512 * i : 512 * (i + 1)] = mm(part, spread[...], (1, 0)).astype(BF)
    step(rows)
    step(weights)


def attend(qkv, cosine, sine, first, spread, gate, up, down, cot):
    ffn = jax.ShapeDtypeStruct(lead_of(FFN_DIMS) + (ROWS, D), BF)
    rows = jax.ShapeDtypeStruct(lead_of(ROW_DIMS) + (TOK, D), BF)
    copies = count_gather([("zh", "x", "y"), ("zh", "y", "x"), ("x", "c")])
    copies += 3 * count_gather(FFN_ORDERS)
    return pl.pallas_call(
        attend_kernel,
        out_shape=(
            jax.ShapeDtypeStruct(lead_of(KV_DIMS) + (TOK, 512), BF),
            jax.ShapeDtypeStruct((TOK, HQ), BF),
            jax.ShapeDtypeStruct((TOK, HQ), F32),
            jax.ShapeDtypeStruct((TOK, 2048), BF),
            jax.ShapeDtypeStruct((KVH, 8, GQ), F32),
            ffn,
            ffn,
            ffn,
            rows,
        ),
        in_specs=[VMEM] * 5 + [ANY] * 4,
        out_specs=(VMEM,) * 5 + (ANY,) * 4,
        scratch_shapes=[
            pltpu.VMEM((TOK, 512), BF),
            pltpu.VMEM((KVH, GQ, HD), BF),
            pltpu.VMEM((HD, GQ), F32),
            pltpu.VMEM((8, GQ), F32),
            pltpu.SemaphoreType.DMA((copies,)),
            pltpu.SemaphoreType.DMA((copies,)),
            pltpu.SemaphoreType.DMA((5,)),
        ],
        compiler_params=pltpu.CompilerParams(
            collective_id=2, has_side_effects=True, vmem_limit_bytes=48 * 2**20
        ),
    )(qkv, cosine, sine, first, spread, gate, up, down, cot)


def grad_group(g, kv, qs, gs, lse, delta, first, row, blocks, query_grad, kv_grad):
    query_grad[...] = jnp.zeros_like(query_grad)

    def body(b, carry):
        at = (lax.div(b, 2), pl.ds(lax.rem(b, 2) * 2, 2), slice(None), slice(None))
        keys = key_block_of(kv, b, head(g))
        values = key_block_of(kv, b, head(2 + g))
        raw = mm(keys, qs[g], (1, 1)) * TO_LOG2
        probs = jnp.where(allowed_keys(b, first, row), jnp.exp2(raw - lse), 0.0)
        prob_grad = mm(values, gs[g], (1, 1))
        score_grad = (probs * (prob_grad - delta)).astype(BF)
        key_term = mm(score_grad, qs[g], (1, 0)) * SCALE
        value_term = mm(probs.astype(BF), gs[g], (1, 0))
        kv_grad[at + (head(g),)] = key_term.astype(BF).reshape(2, 2, TOK, HD)
        kv_grad[at + (head(2 + g),)] = value_term.astype(BF).reshape(2, 2, TOK, HD)
        query_grad[...] += mm(keys.T, score_grad, (1, 0))
        return carry

    lax.fori_loop(0, blocks, body, 0)


FIRST_STAGE = (("y",), ("z",))
LAST_STAGE = (("z",), ("y",))


def attend_back_kernel(*refs):
    kv, queries, attended, grad_slots, lse, first_ref, cosine, sine, spread = refs[:9]
    parts = refs[9:12]
    qkv_grad = refs[12]
    sums = refs[13:19]
    qs, gs, delta, query_grad, kv_grad, kv_out, send, recv, local = refs[19:28]
    scratch = refs[28:]
    me = here()
    links = Links(me, send, recv)
    greet(me, ("zh", "x", "y", "z"))
    weights = []
    for i in range(6):
        order, tail = FIRST_STAGE[i % 2], HALVES[i % 2]
        weights.append(
            scatter_stream(
                links, local.at[i], parts[i // 2], FFN_DIMS, tail, order, scratch[2 * i : 2 * i + 2], sums[i], ROWS, 16
            )
        )
    step(weights)
    blocks, row = key_blocks()
    first = first_ref[0:1]
    for i in range(4):
        part = mm(grad_slots[:, 512 * i : 512 * (i + 1)], spread[...], (1, 1))
        for j in range(3):
            h = 3 * i + j
            one = part[:, head(j)]
            gs[h // GROUP, (h % GROUP) * TOK : (h % GROUP + 1) * TOK, :] = one.astype(BF)
            both = (one * attended[:, head(h)]).T
            delta[h // GROUP : h // GROUP + 1, head(h % GROUP)] = jnp.sum(
                both, axis=0, keepdims=True
            )
            qs[h // GROUP, (h % GROUP) * TOK : (h % GROUP + 1) * TOK, :] = queries[:, head(h)]

    def clear(b, carry):
        at = (lax.div(b, 2), pl.ds(lax.rem(b, 2) * 2, 2))
        kv_grad[at] = jnp.zeros((2, 2, TOK, 512), BF)
        return carry

    lax.fori_loop(blocks, 8, clear, 0)
    cos, sin = cosine[...], sine[...]
    for g in range(KVH):
        grad_group(
            g, kv, qs, gs, lse[g, 0:1], delta[g : g + 1], first, row, blocks, query_grad, kv_grad
        )
        for i in range(GROUP):
            one = query_grad[:, head(i)].T * SCALE
            qkv_grad[:, head(GROUP * g + i)] = (one * cos - turned(one) * sin).astype(BF)
    keys = []
    for half, order in enumerate(KV_ORDERS):
        tail = (slice(None), slice(256 * half, 256 * (half + 1)))
        part = scratch[12 + 6 * half : 18 + 6 * half]
        keys.append(
            scatter_stream(links, None, kv_grad, KV_DIMS, tail, order, part, kv_out.at[half], TOK, 32)
        )
    step(keys)
    step(keys)
    step(keys)
    step(keys)
    for g in range(KVH):
        one = kv_out[0, :, head(g)]
        qkv_grad[:, head(H + g)] = (one * cos - turned(one) * sin).astype(BF)
        qkv_grad[:, head(H + 2 + g)] = kv_out[1, :, head(g)].astype(BF)
    step(weights)


def attend_back(kv, queries, attended, grad_slots, lse, first, cosine, sine, spread, parts):
    copies = count_gather(KV_ORDERS) + 3 * count_gather(FIRST_STAGE)
    scratch, sums = [], []
    for _ in range(3):
        for order in FIRST_STAGE:
            scratch += scatter_scratch(FFN_DIMS, order, ROWS, 768)
            sums.append(
                jax.ShapeDtypeStruct(lead_of(rest_of(FFN_DIMS, order[0])) + (ROWS, 768), BF)
            )
    for order in KV_ORDERS:
        scratch += scatter_scratch(KV_DIMS, order, TOK, 256)
    return pl.pallas_call(
        attend_back_kernel,
        out_shape=(jax.ShapeDtypeStruct((TOK, 2048), BF),) + tuple(sums),
        in_specs=[VMEM] * 9 + [ANY] * 3,
        out_specs=(VMEM,) * 7,
        scratch_shapes=[
            pltpu.VMEM((KVH, GQ, HD), BF),
            pltpu.VMEM((KVH, GQ, HD), BF),
            pltpu.VMEM((8, GQ), F32),
            pltpu.VMEM((HD, GQ), F32),
            pltpu.VMEM(lead_of(KV_DIMS) + (TOK, 512), BF),
            pltpu.VMEM((2, TOK, 256), F32),
            pltpu.SemaphoreType.DMA((copies,)),
            pltpu.SemaphoreType.DMA((copies,)),
            pltpu.SemaphoreType.DMA((6,)),
        ]
        + scratch,
        compiler_params=pltpu.CompilerParams(
            collective_id=5, has_side_effects=True, vmem_limit_bytes=60 * 2**20
        ),
    )(kv, queries, attended, grad_slots, lse, first, cosine, sine, spread, *parts)


def rows_kernel(block, buf, send, recv, local):
    me = here()
    links = Links(me, send, recv)
    own = pltpu.make_async_copy(block, buf.at[place(ROW_DIMS, me, ())], local)
    own.start()
    greet(me, ("x", "c"))
    own.wait()
    run_streams([gather_stream(links, block, buf, ROW_DIMS, (), ("x", "c"))])


def gather_rows(block):
    copies = count_gather([("x", "c")])
    return pl.pallas_call(
        rows_kernel,
        out_shape=jax.ShapeDtypeStruct((4, 2, TOK, D), BF),
        in_specs=[ANY],
        out_specs=ANY,
        scratch_shapes=[
            pltpu.SemaphoreType.DMA((copies,)),
            pltpu.SemaphoreType.DMA((copies,)),
            pltpu.SemaphoreType.DMA,
        ],
        compiler_params=pltpu.CompilerParams(collective_id=3, has_side_effects=True),
    )(block)


def lead_of(dims):
    return tuple(SIZE[d] for d in dims)


def rest_of(dims, axis):
    return tuple(d for d in dims if d not in PARTS_OF[axis])


def scatter_scratch(dims, order, rows, cols):
    shapes = []
    for axis in order:
        dims = rest_of(dims, axis)
        shapes.append(pltpu.VMEM((len(REACH[axis]),) + lead_of(dims) + (rows, cols), BF))
        shapes.append(pltpu.VMEM(lead_of(dims) + (rows, cols), BF))
    return shapes


def sum_blocks(own, arrived, out, lead, rows, step):
    count = 1
    for n in lead:
        count *= n
    per = rows // step
    parts = arrived.shape[0]

    def body(i, carry):
        block, row = lax.div(i, per), lax.rem(i, per)
        index = []
        for n in reversed(lead):
            index.append(lax.rem(block, n))
            block = lax.div(block, n)
        at = tuple(reversed(index)) + (pl.ds(pl.multiple_of(row * step, step), step),)
        total = own[at].astype(F32)
        for p in range(parts):
            total = total + arrived[(p,) + at].astype(F32)
        out[at] = total.astype(out.dtype)
        return carry

    lax.fori_loop(0, count * per, body, 0)


def scatter_stream(links, local, source, dims, tail, order, scratch, out, rows, step):
    me = links.me
    now = None
    for n, axis in enumerate(order):
        arrived, own = scratch[2 * n], scratch[2 * n + 1]
        gone = PARTS_OF[axis]
        keep = tuple(d for d in dims if d not in gone)
        end = tail if n == 0 else ()
        base = source if n == 0 else now
        copies = []
        for k in REACH[axis]:
            to = peer(me, axis, k)
            src = base.at[place(dims, to, keep, end)]
            copies.append(links.copy(src, arrived.at[k - 1], axis, k))
        held = base.at[place(dims, me, keep, end)]
        staged = n == 0 and local is not None
        if staged:
            mine = pltpu.make_async_copy(held, own, local)
            mine.start()
        yield
        if staged:
            mine.wait()
            held = own
        for c in copies:
            c.wait()
        target = out if n == len(order) - 1 else own
        sum_blocks(held, arrived, target, lead_of(keep), rows, step)
        now, dims = own, keep


def rows_scatter_kernel(first, second, out_a, out_b, send, recv, local, *scratch):
    me = here()
    links = Links(me, send, recv)
    greet(me, ("x", "c"))
    half = len(scratch) // 2
    run_streams(
        [
            scatter_stream(
                links, local.at[0], first, ROW_DIMS, (), ("c", "x"), scratch[:half], out_a, TOK, 16
            ),
            scatter_stream(
                links, local.at[1], second, ROW_DIMS, (), ("c", "x"), scratch[half:], out_b, TOK, 16
            ),
        ]
    )


def scatter_rows(first, second):
    copies = 2 * count_gather([("c", "x")])
    one = jax.ShapeDtypeStruct((TOK, D), F32)
    return pl.pallas_call(
        rows_scatter_kernel,
        out_shape=(one, one),
        in_specs=[ANY] * 2,
        out_specs=(VMEM,) * 2,
        scratch_shapes=[
            pltpu.SemaphoreType.DMA((copies,)),
            pltpu.SemaphoreType.DMA((copies,)),
            pltpu.SemaphoreType.DMA((2,)),
        ]
        + 2 * scatter_scratch(ROW_DIMS, ("c", "x"), TOK, D),
        compiler_params=pltpu.CompilerParams(
            collective_id=4, has_side_effects=True, vmem_limit_bytes=48 * 2**20
        ),
    )(first, second)


KV_ORDERS = (("y", "x", "zh"), ("x", "y", "zh"))
ALL_ORDERS = tuple(("c",) + o for o in ORDERS)


def weight_grads_kernel(*refs):
    qkv, out, small = refs[:3]
    parts = refs[3:9]
    qkv_out, out_out, small_out = refs[9:12]
    ffn_outs = refs[12:15]
    send, recv, local = refs[15:18]
    scratch = list(refs[18:])
    me = here()
    links = Links(me, send, recv)
    greet(me, ("x", "y", "z", "c"))
    streams = []

    def add(source, dims, order, tail, target, rows):
        n = 2 * len(order)
        part = [scratch.pop(0) for _ in range(n)]
        streams.append(
            scatter_stream(
                links, local.at[len(streams)], source, dims, tail, order, part, target, rows, 16
            )
        )

    for source, target in ((qkv, qkv_out), (out, out_out)):
        for order, tail in zip(ALL_ORDERS, THIRDS, strict=True):
            add(source, AXES, order, tail, target.at[tail], 16)
    add(small, AXES, ALL_ORDERS[0], (), small_out, 16)
    for i, source in enumerate(parts):
        order = LAST_STAGE[i % 2]
        dims = rest_of(FFN_DIMS, FIRST_STAGE[i % 2][0])
        add(source, dims, order, (), ffn_outs[i // 2].at[HALVES[i % 2]], ROWS)
    run_streams(streams)


def scatter_weight_grads(qkv, out, small, parts):
    copies = 2 * count_gather(ALL_ORDERS) + count_gather(ALL_ORDERS[:1])
    copies += 3 * count_gather(LAST_STAGE)
    scratch = []
    for _ in range(2):
        for order in ALL_ORDERS:
            scratch += scatter_scratch(AXES, order, 16, 512)
    scratch += scatter_scratch(AXES, ALL_ORDERS[0], 16, 128)
    for i in range(6):
        scratch += scatter_scratch(
            rest_of(FFN_DIMS, FIRST_STAGE[i % 2][0]), LAST_STAGE[i % 2], ROWS, 768
        )
    attn = jax.ShapeDtypeStruct((16, D), F32)
    ffn = jax.ShapeDtypeStruct((ROWS, D), F32)
    return pl.pallas_call(
        weight_grads_kernel,
        out_shape=(attn, attn, jax.ShapeDtypeStruct((16, 128), F32), ffn, ffn, ffn),
        in_specs=[ANY] * 9,
        out_specs=(VMEM,) * 6,
        scratch_shapes=[
            pltpu.SemaphoreType.DMA((copies,)),
            pltpu.SemaphoreType.DMA((copies,)),
            pltpu.SemaphoreType.DMA((13,)),
        ]
        + scratch,
        compiler_params=pltpu.CompilerParams(
            collective_id=6, has_side_effects=True, vmem_limit_bytes=60 * 2**20
        ),
    )(qkv, out, small, *parts)


def positions_of(documents):
    index = jnp.arange(documents.shape[0], dtype=jnp.int32)
    kinds = jnp.arange(doc_kinds, dtype=jnp.int32)
    counts = jnp.sum((documents[None, :] == kinds[:, None]).astype(jnp.int32), axis=1)
    starts = jnp.cumsum(counts) - counts
    first = jnp.sum(jnp.where(documents[:, None] == kinds[None, :], starts[None, :], 0), axis=1)
    return index - first


def rope_tables(position):
    half = HD // 2
    inverse = rope_base ** (-(jnp.arange(half, dtype=jnp.float32) * 2.0 / HD))
    angle = position.astype(jnp.float32)[:, None] * inverse[None, :]
    angle = jnp.concatenate([angle, angle], axis=1)
    return (jnp.cos(angle), jnp.sin(angle))


def dot(a, b, dims):
    return lax.dot_general(a, b, ((dims[:1], dims[1:]), ((), ())), preferred_element_type=F32)


def local(
    tokens_in,
    qkv_weight,
    qkv_bias,
    out_weight,
    norm_gains,
    gate_weight,
    up_weight,
    down_weight,
    doc_ids,
    cotangent,
):
    block_index = lax.axis_index("y") * 8 + lax.axis_index("x") * 2 + lax.axis_index("zh")
    inputs = tokens_in[0].astype(F32)
    documents = doc_ids[0]
    cot_low = cotangent[0]

    small = jnp.concatenate([qkv_bias, norm_gains.reshape(-1)])[None]
    small = jnp.pad(small, ((0, 15), (0, 128 - small.shape[1])))
    units, out_rows = gate_weight.shape[0], out_weight.shape[0]
    qkv_all, out_all, small_all = gather_weights(
        qkv_weight, jnp.pad(out_weight, ((0, 16 - out_rows), (0, 0))), small
    )
    w_qkv = qkv_all.reshape(2048, D)
    w_out = out_all.reshape(2048, D)
    small_all = small_all.reshape(128, 16, 128)[:, 0]
    b_qkv = small_all[:, :16].reshape(2048).astype(F32)
    gain_one = small_all[:, 16:28].reshape(D).astype(F32)
    gain_two = small_all[:, 28:40].reshape(D).astype(F32)
    feature = lax.broadcasted_iota(jnp.int32, (384, 512), 0)
    slot = lax.broadcasted_iota(jnp.int32, (384, 512), 1)
    spread = (slot == feature // out_rows * 16 + feature % out_rows).astype(BF)

    first_row = block_index * TOK
    my_pos = lax.dynamic_slice_in_dim(positions_of(documents), first_row, TOK, 0)
    cosine, sine = rope_tables(my_pos)
    sine = jnp.concatenate([-sine[:, : HD // 2], sine[:, HD // 2 :]], axis=1)
    first = first_row + jnp.arange(TOK, dtype=jnp.int32) - my_pos
    first = jnp.broadcast_to(jnp.tile(first, GROUP)[None], (8, GQ))

    factor_one = lax.rsqrt(jnp.mean(inputs * inputs, axis=-1, keepdims=True) + norm_eps)
    normed_one = (inputs * factor_one * gain_one).astype(BF)
    qkv = dot(normed_one, w_qkv, (1, 1)) + b_qkv
    pad = ((0, ROWS - units), (0, 0))
    kv, queries, attended, slots, lse, w_gate, w_up, w_down, cot_rows = attend(
        qkv,
        cosine,
        sine,
        first,
        spread,
        jnp.pad(gate_weight, pad),
        jnp.pad(up_weight, pad),
        jnp.pad(down_weight, pad),
        cot_low,
    )
    w_gate, w_up, w_down = (w.reshape(-1, D) for w in (w_gate, w_up, w_down))
    cot_rows = cot_rows.reshape(-1, D)
    middle = inputs + dot(slots, w_out, (1, 0))
    factor_two = lax.rsqrt(jnp.mean(middle * middle, axis=-1, keepdims=True) + norm_eps)
    normed_two = (middle * factor_two * gain_two).astype(BF)

    rows_two = gather_rows(normed_two).reshape(-1, D)
    gate = dot(rows_two, w_gate, (1, 1))
    upward = dot(rows_two, w_up, (1, 1))
    hidden_grad = dot(cot_rows, w_down, (1, 1))
    sigma = jax.nn.sigmoid(gate)
    hidden = (gate * sigma * upward).astype(BF)
    gate_grad = (hidden_grad * upward * sigma * (1.0 + gate * (1.0 - sigma))).astype(BF)
    upward_grad = (hidden_grad * gate * sigma).astype(BF)
    ffn_part = dot(hidden, w_down, (1, 0)).astype(BF)
    grad_part = (dot(gate_grad, w_gate, (1, 0)) + dot(upward_grad, w_up, (1, 0))).astype(BF)
    rows_lead = lead_of(ROW_DIMS) + (TOK, D)
    ffn_total, normed_two_grad = scatter_rows(
        ffn_part.reshape(rows_lead), grad_part.reshape(rows_lead)
    )
    layer_out = (middle + ffn_total).astype(BF)

    cot_full = cot_low.astype(F32)
    scaled_two = gain_two * normed_two_grad
    gain_two_grad = jnp.sum(normed_two_grad * middle * factor_two, axis=0)
    middle_grad = (
        cot_full
        + factor_two * scaled_two
        - middle * factor_two**3 * jnp.mean(scaled_two * middle, axis=-1, keepdims=True)
    )
    branch_grad = middle_grad.astype(BF)
    grad_slots = dot(branch_grad, w_out, (1, 1)).astype(BF)
    ffn_lead = lead_of(FFN_DIMS) + (ROWS, D)
    parts = tuple(
        dot(a, b, (0, 0)).astype(BF).reshape(ffn_lead)
        for a, b in ((gate_grad, rows_two), (upward_grad, rows_two), (hidden, cot_rows))
    )
    qkv_grad, *parts = attend_back(
        kv, queries, attended, grad_slots, lse, first, cosine, sine, spread, parts
    )
    normed_one_grad = dot(qkv_grad, w_qkv, (1, 0))
    scaled_one = gain_one * normed_one_grad
    gain_one_grad = jnp.sum(normed_one_grad * inputs * factor_one, axis=0)
    input_grad = (
        middle_grad
        + factor_one * scaled_one
        - inputs * factor_one**3 * jnp.mean(scaled_one * inputs, axis=-1, keepdims=True)
    )

    lead = lead_of(AXES)
    qkv_part = dot(qkv_grad, normed_one, (0, 0)).astype(BF)
    out_part = dot(slots, branch_grad, (0, 0)).astype(BF)
    bias_part = jnp.sum(qkv_grad.astype(F32), axis=0)
    small_part = jnp.concatenate(
        [
            bias_part.reshape(128, 16),
            gain_one_grad.reshape(128, 12),
            gain_two_grad.reshape(128, 12),
        ],
        axis=1,
    ).astype(BF)
    small_part = jnp.pad(small_part[:, None], ((0, 0), (0, 15), (0, 88)))
    qkv_sum, out_sum, small_sum, gate_sum, up_sum, down_sum = scatter_weight_grads(
        qkv_part.reshape(lead + (16, D)),
        out_part.reshape(lead + (16, D)),
        small_part.reshape(lead + (16, 128)),
        parts,
    )
    return (
        layer_out[None],
        input_grad[None],
        qkv_sum,
        small_sum[0, :16],
        out_sum[:out_rows],
        small_sum[0, 16:40].reshape(2, 12),
        gate_sum[:units],
        up_sum[:units],
        down_sum[:units],
    )


def solution(mesh):
    fine = Mesh(mesh.devices.reshape(tuple(SIZE[a] for a in AXES)), AXES)
    dp, ctx = ("zl", "c"), ("y", "x", "zh")
    in_specs = (
        P(dp, ctx, None),
        P(AXES, None),
        P(AXES),
        P(AXES, None),
        P(None, AXES),
        P(AXES, None),
        P(AXES, None),
        P(AXES, None),
        P(dp, None),
        P(dp, ctx, None),
    )
    out_specs = (
        P(dp, ctx, None),
        P(dp, ctx, None),
        P(AXES, None),
        P(AXES),
        P(AXES, None),
        P(None, AXES),
        P(AXES, None),
        P(AXES, None),
        P(AXES, None),
    )
    return jax.shard_map(local, mesh=fine, in_specs=in_specs, out_specs=out_specs, check_vma=False)
```

```python
import math

import jax
import jax.numpy as jnp
from jax import lax
from jax.experimental import pallas as pl
from jax.experimental.pallas import tpu as pltpu
from jax.sharding import Mesh
from jax.sharding import PartitionSpec as P

H = 12
KVH = 2
HD = 128
HQ = 1536
D = 1536
TOK = 128
ROWS = 80

norm_eps = 1e-06
rope_base = 1000000.0
doc_kinds = 3

AXES = ("zl", "c", "y", "x", "zh")
SIZE = {"zl": 2, "c": 2, "y": 4, "x": 4, "zh": 2}
PARTS_OF = {"z": ("zl", "zh"), "x": ("x",), "y": ("y",), "c": ("c",), "zh": ("zh",)}
REACH = {"z": (1, 2, 3), "x": (1, 2, 3), "y": (1, 2, 3), "c": (1,), "zh": (1,)}
BF = jnp.bfloat16
F32 = jnp.float32
ANY = pl.BlockSpec(memory_space=pl.ANY)
VMEM = pl.BlockSpec(memory_space=pltpu.VMEM)


def here():
    return {a: lax.axis_index(a) for a in AXES}


def peer(me, axis, k):
    to = dict(me)
    if axis == "z":
        z = lax.rem(me["zh"] * 2 + me["zl"] + k, 4)
        to["zl"], to["zh"] = lax.rem(z, 2), lax.div(z, 2)
    else:
        to[axis] = lax.rem(me[axis] + k, SIZE[axis])
    return to


def device_id(at):
    return tuple(at[a] for a in AXES)


def place(dims, at, whole, tail=()):
    return tuple(slice(None) if d in whole else at[d] for d in dims) + tuple(tail)


class Links:
    def __init__(self, me, send, recv):
        self.me, self.send, self.recv, self.used = me, send, recv, 0

    def copy(self, src, dst, axis, k):
        i = self.used
        self.used += 1
        c = pltpu.make_async_remote_copy(
            src_ref=src,
            dst_ref=dst,
            send_sem=self.send.at[i],
            recv_sem=self.recv.at[i],
            device_id=device_id(peer(self.me, axis, k)),
            device_id_type=pl.DeviceIdType.MESH,
        )
        c.start()
        return c


def greet(me, axes):
    barrier = pltpu.get_barrier_semaphore()
    count = 0
    for axis in axes:
        for k in REACH[axis]:
            pl.semaphore_signal(
                barrier,
                inc=1,
                device_id=device_id(peer(me, axis, k)),
                device_id_type=pl.DeviceIdType.MESH,
            )
            count += 1
    pl.semaphore_wait(barrier, count)


def halves_of(tail, cols):
    rows = tail[:-1] if tail else (slice(None),)
    start = tail[-1].start if tail else 0
    cut = cols // 2
    return tuple(rows + (slice(start + cut * i, start + cut * (i + 1)),) for i in range(2))


def gather_stream(links, block, buf, dims, tail, order):
    me = links.me
    whole = ()
    cols = block.shape[-1]
    for n, axis in enumerate(order):
        mine = place(dims, me, whole, tail)
        src = block if n == 0 else buf.at[mine]
        near = (1, 3) if len(REACH[axis]) == 3 else (1,)
        copies = [links.copy(src, buf.at[mine], axis, k) for k in near]
        yield
        for c in copies:
            c.wait()
        if len(near) == 2:
            copies = []
            for k, half in zip(near, halves_of(tail, cols), strict=True):
                theirs = buf.at[place(dims, peer(me, axis, 4 - k), whole, half)]
                copies.append(links.copy(theirs, theirs, axis, k))
            yield
            for c in copies:
                c.wait()
        whole = whole + PARTS_OF[axis]


def run_streams(streams):
    live = list(streams)
    while live:
        live = [s for s in live if next(s, live) is not live]


def step(streams):
    for s in streams:
        next(s, None)


def count_gather(orders):
    return sum((1, 4)[len(REACH[a]) // 3] for order in orders for a in order)


def count_scatter(orders):
    return sum(len(REACH[a]) for order in orders for a in order)


THIRDS = tuple((slice(None), slice(512 * i, 512 * (i + 1))) for i in range(3))
ORDERS = (("x", "y", "z"), ("y", "z", "x"), ("z", "x", "y"))
HALVES = tuple((slice(None), slice(768 * i, 768 * (i + 1))) for i in range(2))
FFN_ORDERS = (("y", "z"), ("z", "y"))
FFN_DIMS = ("zl", "y", "zh")
ROW_DIMS = ("x", "c")
KV_DIMS = ("y", "x", "zh")


def weights_kernel(qkv, out, small, qkv_all, out_all, small_all, send, recv, local):
    me = here()
    links = Links(me, send, recv)
    own = []
    pairs = ((qkv, qkv_all), (out, out_all), (small, small_all))
    for i, (a, b) in enumerate(pairs):
        own.append(pltpu.make_async_copy(a, b.at[place(AXES, me, ())], local.at[i]))
        own[-1].start()
    greet(me, ("x", "y", "z", "c"))
    for c in own:
        c.wait()
    streams = []
    for block, buf in pairs[:2]:
        for order, tail in zip(ORDERS, THIRDS, strict=True):
            streams.append(
                gather_stream(links, block.at[tail], buf, AXES, tail, order + ("c",))
            )
    streams.append(gather_stream(links, small, small_all, AXES, (), ORDERS[0] + ("c",)))
    run_streams(streams)


def gather_weights(qkv, out, small):
    every = jax.ShapeDtypeStruct(lead_of(AXES) + (16, D), BF)
    smalls = jax.ShapeDtypeStruct(lead_of(AXES) + (16, 256), BF)
    copies = 2 * count_gather([o + ("c",) for o in ORDERS]) + count_gather([ORDERS[0] + ("c",)])
    return pl.pallas_call(
        weights_kernel,
        out_shape=(every, every, smalls),
        in_specs=[ANY] * 3,
        out_specs=(ANY,) * 3,
        scratch_shapes=[
            pltpu.SemaphoreType.DMA((copies,)),
            pltpu.SemaphoreType.DMA((copies,)),
            pltpu.SemaphoreType.DMA((3,)),
        ],
        compiler_params=pltpu.CompilerParams(collective_id=1, has_side_effects=True),
    )(qkv, out, small)


def lead_of(dims):
    return tuple(SIZE[d] for d in dims)


def rest_of(dims, axis):
    return tuple(d for d in dims if d not in PARTS_OF[axis])


def scatter_scratch(dims, order, rows, cols):
    shapes = []
    for axis in order:
        dims = rest_of(dims, axis)
        shapes.append(pltpu.VMEM((len(REACH[axis]),) + lead_of(dims) + (rows, cols), BF))
        shapes.append(pltpu.VMEM(lead_of(dims) + (rows, cols), BF))
    return shapes


def sum_blocks(own, arrived, out, lead, rows, step):
    count = 1
    for n in lead:
        count *= n
    per = rows // step
    parts = arrived.shape[0]

    def body(i, carry):
        block, row = lax.div(i, per), lax.rem(i, per)
        index = []
        for n in reversed(lead):
            index.append(lax.rem(block, n))
            block = lax.div(block, n)
        at = tuple(reversed(index)) + (pl.ds(pl.multiple_of(row * step, step), step),)
        total = own[at].astype(F32)
        for p in range(parts):
            total = total + arrived[(p,) + at].astype(F32)
        out[at] = total.astype(out.dtype)
        return carry

    lax.fori_loop(0, count * per, body, 0)


def scatter_stream(links, local, source, dims, tail, order, scratch, out, rows, step):
    me = links.me
    now = None
    for n, axis in enumerate(order):
        arrived, own = scratch[2 * n], scratch[2 * n + 1]
        gone = PARTS_OF[axis]
        keep = tuple(d for d in dims if d not in gone)
        end = tail if n == 0 else ()
        base = source if n == 0 else now
        copies = []
        for k in REACH[axis]:
            to = peer(me, axis, k)
            src = base.at[place(dims, to, keep, end)]
            copies.append(links.copy(src, arrived.at[k - 1], axis, k))
        held = base.at[place(dims, me, keep, end)]
        staged = n == 0 and local is not None
        if staged:
            mine = pltpu.make_async_copy(held, own, local)
            mine.start()
        yield
        if staged:
            mine.wait()
            held = own
        for c in copies:
            c.wait()
        target = out if n == len(order) - 1 else own
        sum_blocks(held, arrived, target, lead_of(keep), rows, step)
        now, dims = own, keep


FIRST_STAGE = (("y",), ("z",))
LAST_STAGE = (("z",), ("y",))
KV_ORDERS = (("y", "x", "zh"), ("x", "y", "zh"))
ALL_ORDERS = tuple(("c",) + o for o in ORDERS)


def first_stage_scratch():
    scratch, sums = [], []
    for order in FIRST_STAGE:
        scratch += scatter_scratch(FFN_DIMS, order, ROWS, 768)
        sums.append(jax.ShapeDtypeStruct(lead_of(rest_of(FFN_DIMS, order[0])) + (ROWS, 768), BF))
    return scratch, sums


def first_stage(links, local, used, part, sums, scratch):
    return [
        scatter_stream(
            links,
            local.at[used + i],
            part,
            FFN_DIMS,
            HALVES[i],
            FIRST_STAGE[i],
            scratch[2 * i : 2 * i + 2],
            sums[i],
            ROWS,
            16,
        )
        for i in range(2)
    ]


def rows_scatter_kernel(rows, part, out, sum_a, sum_b, send, recv, local, *scratch):
    me = here()
    links = Links(me, send, recv)
    greet(me, ("x", "y", "z", "c"))
    streams = [
        scatter_stream(links, local.at[2], rows, ROW_DIMS, (), ("c", "x"), scratch[4:], out, TOK, 16)
    ]
    weights = first_stage(links, local, 0, part, (sum_a, sum_b), scratch[:4])
    step(streams)
    step(weights)
    run_streams(streams)
    step(weights)


def scatter_rows(rows, part):
    copies = count_scatter([("c", "x")]) + count_scatter(FIRST_STAGE)
    scratch, sums = first_stage_scratch()
    return pl.pallas_call(
        rows_scatter_kernel,
        out_shape=(jax.ShapeDtypeStruct((TOK, D), F32),) + tuple(sums),
        in_specs=[ANY] * 2,
        out_specs=(VMEM,) * 3,
        scratch_shapes=[
            pltpu.SemaphoreType.DMA((copies,)),
            pltpu.SemaphoreType.DMA((copies,)),
            pltpu.SemaphoreType.DMA((3,)),
        ]
        + scratch
        + scatter_scratch(ROW_DIMS, ("c", "x"), TOK, D),
        compiler_params=pltpu.CompilerParams(
            collective_id=4, has_side_effects=True, vmem_limit_bytes=48 * 2**20
        ),
    )(rows, part)


GROUP = H // KVH
GQ = GROUP * TOK
KEYS = 512
SCALE = HD**-0.5
TO_LOG2 = SCALE * math.log2(math.e)


def head(h):
    return slice(128 * h, 128 * (h + 1))


def turned(v):
    return pltpu.roll(v, 64, 1)


def key_blocks():
    ctx = lax.axis_index("y") * 8 + lax.axis_index("x") * 2 + lax.axis_index("zh")
    return lax.div(ctx, 4) + 1, ctx * TOK


def key_block_of(ref, b, cols):
    return ref[lax.div(b, 2), pl.ds(lax.rem(b, 2) * 2, 2), :, :, cols].reshape(KEYS, HD)


def allowed_keys(b, first, row):
    key = b * KEYS + lax.broadcasted_iota(jnp.int32, (KEYS, GQ), 0)
    query = row + lax.rem(lax.broadcasted_iota(jnp.int32, (1, GQ), 1), TOK)
    return (key <= query) & (key >= first)


def mm(a, b, contract):
    return lax.dot_general(
        a, b, ((contract[:1], contract[1:]), ((), ())), preferred_element_type=F32
    )


def attend_group(g, kv, qs, first, row, blocks, acc, stats):
    acc[...] = jnp.zeros_like(acc)
    stats[0:1] = jnp.full((1, GQ), -1e30, F32)
    stats[1:2] = jnp.zeros((1, GQ), F32)

    def body(b, carry):
        keys = key_block_of(kv, b, head(g))
        values = key_block_of(kv, b, head(2 + g))
        raw = mm(keys, qs[g], (1, 1)) * TO_LOG2
        raw = jnp.where(allowed_keys(b, first, row), raw, -1e30)
        old = stats[0:1]
        top = jnp.maximum(old, jnp.max(raw, axis=0, keepdims=True))
        probs = jnp.exp2(raw - top)
        shrink = jnp.exp2(old - top)
        stats[0:1] = top
        stats[1:2] = stats[1:2] * shrink + jnp.sum(probs, axis=0, keepdims=True)
        acc[...] = acc[...] * shrink + mm(values.T, probs.astype(BF), (1, 0))
        return carry

    lax.fori_loop(0, blocks, body, 0)


def attend_kernel(*refs):
    qkv, cosine, sine, first_ref, spread, tokens, gain = refs[:7]
    gate, up, down, cot, w_out_hbm = refs[7:12]
    kv, queries, attended, slots, lse, middle = refs[12:18]
    gate_all, up_all, down_all, cot_all, rows_all = refs[18:23]
    block, qs, acc, stats, w_out, normed, send, recv, local = refs[23:]
    me = here()
    links = Links(me, send, recv)
    own = []
    pairs = (
        (gate, gate_all, FFN_DIMS),
        (up, up_all, FFN_DIMS),
        (down, down_all, FFN_DIMS),
        (cot, cot_all, ROW_DIMS),
    )
    for i, (a, b, dims) in enumerate(pairs):
        own.append(pltpu.make_async_copy(a, b.at[place(dims, me, ())], local.at[i]))
        own[-1].start()
    cos, sin = cosine[...], sine[...]
    for g in range(KVH):
        part = qkv[:, head(H + g)]
        block[:, head(g)] = (part * cos + turned(part) * sin).astype(BF)
        block[:, head(2 + g)] = qkv[:, head(H + 2 + g)].astype(BF)
    own.append(pltpu.make_async_copy(block, kv.at[place(KV_DIMS, me, ())], local.at[4]))
    own[-1].start()
    fetch = pltpu.make_async_copy(w_out_hbm, w_out, local.at[5])
    fetch.start()
    greet(me, ("zh", "x", "y", "z", "c"))
    keys = []
    for half, order in enumerate((("zh", "x", "y"), ("zh", "y", "x"))):
        tail = (slice(None), slice(256 * half, 256 * (half + 1)))
        keys.append(gather_stream(links, block.at[tail], kv, KV_DIMS, tail, order))
    weights = []
    for a, b, _ in pairs[:3]:
        for order, tail in zip(FFN_ORDERS, HALVES, strict=True):
            weights.append(gather_stream(links, a.at[tail], b, FFN_DIMS, tail, order))
    cots = [gather_stream(links, cot, cot_all, ROW_DIMS, (), ("x", "c"))]
    step(keys)
    step(weights)
    for c in own:
        c.wait()
    step(keys)
    for h in range(H):
        part = qkv[:, head(h)]
        turned_q = (part * cos + turned(part) * sin).astype(BF)
        queries[:, head(h)] = turned_q
        qs[h // GROUP, (h % GROUP) * TOK : (h % GROUP + 1) * TOK, :] = turned_q
    step(keys)
    step(weights)
    step(keys)
    step(weights)
    step(keys)
    step(cots)
    step(keys)
    blocks, row = key_blocks()
    first = first_ref[0:1]
    for g in range(KVH):
        attend_group(g, kv, qs, first, row, blocks, acc, stats)
        total = stats[1:2]
        lse[g] = jnp.broadcast_to(stats[0:1] + jnp.log2(total), (8, GQ))
        acc[...] = acc[...] / total
        for i in range(GROUP):
            attended[:, head(GROUP * g + i)] = acc[:, head(i)].T
        step(cots)
    for i in range(4):
        part = attended[:, 384 * i : 384 * (i + 1)].astype(BF)
        slots[:, 512 * i : 512 * (i + 1)] = mm(part, spread[...], (1, 0)).astype(BF)
    fetch.wait()
    square = jnp.zeros((TOK, 1), F32)
    for i in range(3):
        cols = slice(512 * i, 512 * (i + 1))
        part = tokens[:, cols].astype(F32) + mm(slots[...], w_out[:, cols], (1, 0))
        middle[:, cols] = part
        square = square + jnp.sum(part * part, axis=1, keepdims=True)
    factor = lax.rsqrt(square / D + norm_eps)
    normed[...] = (middle[...] * factor * gain[0:1]).astype(BF)
    keep = pltpu.make_async_copy(normed, rows_all.at[place(ROW_DIMS, me, ())], local.at[6])
    keep.start()
    rows = [gather_stream(links, normed, rows_all, ROW_DIMS, (), ("x", "c"))]
    step(rows)
    step(weights)
    step(cots)
    step(rows)
    keep.wait()
    step(rows)
    step(rows)
    step(weights)


def attend(qkv, cosine, sine, first, spread, tokens, gain, gate, up, down, cot, w_out):
    ffn = jax.ShapeDtypeStruct(lead_of(FFN_DIMS) + (ROWS, D), BF)
    rows = jax.ShapeDtypeStruct(lead_of(ROW_DIMS) + (TOK, D), BF)
    copies = count_gather([("zh", "x", "y"), ("zh", "y", "x"), ("x", "c"), ("x", "c")])
    copies += 3 * count_gather(FFN_ORDERS)
    return pl.pallas_call(
        attend_kernel,
        out_shape=(
            jax.ShapeDtypeStruct(lead_of(KV_DIMS) + (TOK, 512), BF),
            jax.ShapeDtypeStruct((TOK, HQ), BF),
            jax.ShapeDtypeStruct((TOK, HQ), F32),
            jax.ShapeDtypeStruct((TOK, 2048), BF),
            jax.ShapeDtypeStruct((KVH, 8, GQ), F32),
            jax.ShapeDtypeStruct((TOK, D), F32),
            ffn,
            ffn,
            ffn,
            rows,
            rows,
        ),
        in_specs=[VMEM] * 7 + [ANY] * 5,
        out_specs=(VMEM,) * 6 + (ANY,) * 5,
        scratch_shapes=[
            pltpu.VMEM((TOK, 512), BF),
            pltpu.VMEM((KVH, GQ, HD), BF),
            pltpu.VMEM((HD, GQ), F32),
            pltpu.VMEM((8, GQ), F32),
            pltpu.VMEM((2048, D), BF),
            pltpu.VMEM((TOK, D), BF),
            pltpu.SemaphoreType.DMA((copies,)),
            pltpu.SemaphoreType.DMA((copies,)),
            pltpu.SemaphoreType.DMA((7,)),
        ],
        compiler_params=pltpu.CompilerParams(
            collective_id=2, has_side_effects=True, vmem_limit_bytes=48 * 2**20
        ),
    )(qkv, cosine, sine, first, spread, tokens, gain, gate, up, down, cot, w_out)


def grad_group(g, kv, qs, gs, lse, delta, first, row, blocks, query_grad, kv_grad):
    query_grad[...] = jnp.zeros_like(query_grad)

    def body(b, carry):
        at = (lax.div(b, 2), pl.ds(lax.rem(b, 2) * 2, 2), slice(None), slice(None))
        keys = key_block_of(kv, b, head(g))
        values = key_block_of(kv, b, head(2 + g))
        raw = mm(keys, qs[g], (1, 1)) * TO_LOG2
        probs = jnp.where(allowed_keys(b, first, row), jnp.exp2(raw - lse), 0.0)
        prob_grad = mm(values, gs[g], (1, 1))
        score_grad = (probs * (prob_grad - delta)).astype(BF)
        key_term = mm(score_grad, qs[g], (1, 0)) * SCALE
        value_term = mm(probs.astype(BF), gs[g], (1, 0))
        kv_grad[at + (head(g),)] = key_term.astype(BF).reshape(2, 2, TOK, HD)
        kv_grad[at + (head(2 + g),)] = value_term.astype(BF).reshape(2, 2, TOK, HD)
        query_grad[...] += mm(keys.T, score_grad, (1, 0))
        return carry

    lax.fori_loop(0, blocks, body, 0)


def attend_back_kernel(*refs):
    kv, queries, attended, grad_slots, lse, first_ref, cosine, sine, spread = refs[:9]
    gate_part, up_part, out_part, ffn_rows = refs[9:13]
    qkv_grad = refs[13]
    sums = refs[14:18]
    out_grad, ffn_total = refs[18:20]
    qs, gs, delta, query_grad, kv_grad, kv_out, send, recv, local = refs[20:29]
    scratch = list(refs[29:])

    def take(n):
        return [scratch.pop(0) for _ in range(n)]

    me = here()
    links = Links(me, send, recv)
    greet(me, ("zh", "x", "y", "z", "c"))
    weights = first_stage(links, local, 0, gate_part, sums[:2], take(4))
    weights += first_stage(links, local, 2, up_part, sums[2:], take(4))
    outs = []
    for i in range(3):
        outs.append(
            scatter_stream(
                links, local.at[4 + i], out_part, AXES, THIRDS[i], ALL_ORDERS[i], take(8), out_grad.at[THIRDS[i]], 16, 16
            )
        )
    rows = [
        scatter_stream(
            links, local.at[7], ffn_rows, ROW_DIMS, (), ("c", "x"), take(4), ffn_total, TOK, 16
        )
    ]
    step(weights)
    step(rows)
    step(outs)
    blocks, row = key_blocks()
    first = first_ref[0:1]
    for i in range(4):
        part = mm(grad_slots[:, 512 * i : 512 * (i + 1)], spread[...], (1, 1))
        for j in range(3):
            h = 3 * i + j
            one = part[:, head(j)]
            gs[h // GROUP, (h % GROUP) * TOK : (h % GROUP + 1) * TOK, :] = one.astype(BF)
            both = (one * attended[:, head(h)]).T
            delta[h // GROUP : h // GROUP + 1, head(h % GROUP)] = jnp.sum(
                both, axis=0, keepdims=True
            )
            qs[h // GROUP, (h % GROUP) * TOK : (h % GROUP + 1) * TOK, :] = queries[:, head(h)]

    def clear(b, carry):
        at = (lax.div(b, 2), pl.ds(lax.rem(b, 2) * 2, 2))
        kv_grad[at] = jnp.zeros((2, 2, TOK, 512), BF)
        return carry

    lax.fori_loop(blocks, 8, clear, 0)
    cos, sin = cosine[...], sine[...]
    for g in range(KVH):
        grad_group(
            g, kv, qs, gs, lse[g, 0:1], delta[g : g + 1], first, row, blocks, query_grad, kv_grad
        )
        for i in range(GROUP):
            one = query_grad[:, head(i)].T * SCALE
            qkv_grad[:, head(GROUP * g + i)] = (one * cos - turned(one) * sin).astype(BF)
    keys = []
    for half, order in enumerate(KV_ORDERS):
        tail = (slice(None), slice(256 * half, 256 * (half + 1)))
        keys.append(
            scatter_stream(
                links, None, kv_grad, KV_DIMS, tail, order, take(6), kv_out.at[half], TOK, 32
            )
        )
    step(keys)
    step(outs)
    step(rows)
    step(keys)
    step(outs)
    step(keys)
    step(outs)
    step(keys)
    for g in range(KVH):
        one = kv_out[0, :, head(g)]
        qkv_grad[:, head(H + g)] = (one * cos - turned(one) * sin).astype(BF)
        qkv_grad[:, head(H + 2 + g)] = kv_out[1, :, head(g)].astype(BF)
    step(rows)
    step(outs)
    step(weights)


def attend_back(
    kv, queries, attended, grad_slots, lse, first, cosine, sine, spread, gate_part, up_part, out_part, ffn_rows
):
    copies = count_scatter(KV_ORDERS) + 2 * count_scatter(FIRST_STAGE)
    copies += count_scatter(ALL_ORDERS) + count_scatter([("c", "x")])
    scratch, sums = [], []
    for _ in range(2):
        more, results = first_stage_scratch()
        scratch += more
        sums += results
    for order in ALL_ORDERS:
        scratch += scatter_scratch(AXES, order, 16, 512)
    scratch += scatter_scratch(ROW_DIMS, ("c", "x"), TOK, D)
    for order in KV_ORDERS:
        scratch += scatter_scratch(KV_DIMS, order, TOK, 256)
    return pl.pallas_call(
        attend_back_kernel,
        out_shape=(
            jax.ShapeDtypeStruct((TOK, 2048), BF),
            *sums,
            jax.ShapeDtypeStruct((16, D), F32),
            jax.ShapeDtypeStruct((TOK, D), F32),
        ),
        in_specs=[VMEM] * 9 + [ANY] * 4,
        out_specs=(VMEM,) * 7,
        scratch_shapes=[
            pltpu.VMEM((KVH, GQ, HD), BF),
            pltpu.VMEM((KVH, GQ, HD), BF),
            pltpu.VMEM((8, GQ), F32),
            pltpu.VMEM((HD, GQ), F32),
            pltpu.VMEM(lead_of(KV_DIMS) + (TOK, 512), BF),
            pltpu.VMEM((2, TOK, 256), F32),
            pltpu.SemaphoreType.DMA((copies,)),
            pltpu.SemaphoreType.DMA((copies,)),
            pltpu.SemaphoreType.DMA((8,)),
        ]
        + scratch,
        compiler_params=pltpu.CompilerParams(
            collective_id=5, has_side_effects=True, vmem_limit_bytes=60 * 2**20
        ),
    )(kv, queries, attended, grad_slots, lse, first, cosine, sine, spread, gate_part, up_part, out_part, ffn_rows)


def weight_grads_kernel(*refs):
    qkv, small = refs[:2]
    parts = refs[2:8]
    qkv_out, small_out = refs[8:10]
    ffn_outs = refs[10:13]
    send, recv, local = refs[13:16]
    scratch = list(refs[16:])
    me = here()
    links = Links(me, send, recv)
    greet(me, ("x", "y", "z", "c"))
    streams = []

    def add(source, dims, order, tail, target, rows):
        n = 2 * len(order)
        part = [scratch.pop(0) for _ in range(n)]
        streams.append(
            scatter_stream(
                links, local.at[len(streams)], source, dims, tail, order, part, target, rows, 16
            )
        )

    for order, tail in zip(ALL_ORDERS, THIRDS, strict=True):
        add(qkv, AXES, order, tail, qkv_out.at[tail], 16)
    add(small, AXES, ALL_ORDERS[0], (), small_out, 16)
    for i, source in enumerate(parts):
        order = LAST_STAGE[i % 2]
        dims = rest_of(FFN_DIMS, FIRST_STAGE[i % 2][0])
        add(source, dims, order, (), ffn_outs[i // 2].at[HALVES[i % 2]], ROWS)
    run_streams(streams)


def scatter_weight_grads(qkv, small, parts):
    copies = count_scatter(ALL_ORDERS) + count_scatter(ALL_ORDERS[:1])
    copies += 3 * count_scatter(LAST_STAGE)
    scratch = []
    for order in ALL_ORDERS:
        scratch += scatter_scratch(AXES, order, 16, 512)
    scratch += scatter_scratch(AXES, ALL_ORDERS[0], 16, 128)
    for i in range(6):
        scratch += scatter_scratch(
            rest_of(FFN_DIMS, FIRST_STAGE[i % 2][0]), LAST_STAGE[i % 2], ROWS, 768
        )
    ffn = jax.ShapeDtypeStruct((ROWS, D), F32)
    return pl.pallas_call(
        weight_grads_kernel,
        out_shape=(
            jax.ShapeDtypeStruct((16, D), F32),
            jax.ShapeDtypeStruct((16, 128), F32),
            ffn,
            ffn,
            ffn,
        ),
        in_specs=[ANY] * 8,
        out_specs=(VMEM,) * 5,
        scratch_shapes=[
            pltpu.SemaphoreType.DMA((copies,)),
            pltpu.SemaphoreType.DMA((copies,)),
            pltpu.SemaphoreType.DMA((10,)),
        ]
        + scratch,
        compiler_params=pltpu.CompilerParams(
            collective_id=6, has_side_effects=True, vmem_limit_bytes=60 * 2**20
        ),
    )(qkv, small, *parts)


def positions_of(documents):
    index = jnp.arange(documents.shape[0], dtype=jnp.int32)
    kinds = jnp.arange(doc_kinds, dtype=jnp.int32)
    counts = jnp.sum((documents[None, :] == kinds[:, None]).astype(jnp.int32), axis=1)
    starts = jnp.cumsum(counts) - counts
    first = jnp.sum(jnp.where(documents[:, None] == kinds[None, :], starts[None, :], 0), axis=1)
    return index - first


def rope_tables(position):
    half = HD // 2
    inverse = rope_base ** (-(jnp.arange(half, dtype=jnp.float32) * 2.0 / HD))
    angle = position.astype(jnp.float32)[:, None] * inverse[None, :]
    angle = jnp.concatenate([angle, angle], axis=1)
    return (jnp.cos(angle), jnp.sin(angle))


def dot(a, b, dims):
    return lax.dot_general(a, b, ((dims[:1], dims[1:]), ((), ())), preferred_element_type=F32)


def local(
    tokens_in,
    qkv_weight,
    qkv_bias,
    out_weight,
    norm_gains,
    gate_weight,
    up_weight,
    down_weight,
    doc_ids,
    cotangent,
):
    block_index = lax.axis_index("y") * 8 + lax.axis_index("x") * 2 + lax.axis_index("zh")
    inputs = tokens_in[0].astype(F32)
    documents = doc_ids[0]
    cot_low = cotangent[0]

    small = jnp.concatenate([qkv_bias, norm_gains.reshape(-1)])[None]
    small = jnp.pad(small, ((0, 15), (0, 256 - small.shape[1])))
    units, out_rows = gate_weight.shape[0], out_weight.shape[0]
    qkv_all, out_all, small_all = gather_weights(
        qkv_weight, jnp.pad(out_weight, ((0, 16 - out_rows), (0, 0))), small
    )
    w_qkv = qkv_all.reshape(2048, D)
    w_out = out_all.reshape(2048, D)
    small_all = small_all.reshape(128, 16, 256)[:, 0]
    b_qkv = small_all[:, :16].reshape(2048).astype(F32)
    gain_one = small_all[:, 16:28].reshape(D).astype(F32)
    gain_two = small_all[:, 28:40].reshape(D).astype(F32)
    feature = lax.broadcasted_iota(jnp.int32, (384, 512), 0)
    slot = lax.broadcasted_iota(jnp.int32, (384, 512), 1)
    spread = (slot == feature // out_rows * 16 + feature % out_rows).astype(BF)

    first_row = block_index * TOK
    my_pos = lax.dynamic_slice_in_dim(positions_of(documents), first_row, TOK, 0)
    cosine, sine = rope_tables(my_pos)
    sine = jnp.concatenate([-sine[:, : HD // 2], sine[:, HD // 2 :]], axis=1)
    first = first_row + jnp.arange(TOK, dtype=jnp.int32) - my_pos
    first = jnp.broadcast_to(jnp.tile(first, GROUP)[None], (8, GQ))

    factor_one = lax.rsqrt(jnp.mean(inputs * inputs, axis=-1, keepdims=True) + norm_eps)
    normed_one = (inputs * factor_one * gain_one).astype(BF)
    qkv = dot(normed_one, w_qkv, (1, 1)) + b_qkv
    pad = ((0, ROWS - units), (0, 0))
    kv, queries, attended, slots, lse, middle, w_gate, w_up, w_down, cot_rows, rows_two = attend(
        qkv,
        cosine,
        sine,
        first,
        spread,
        tokens_in[0],
        jnp.broadcast_to(gain_two[None], (8, D)),
        jnp.pad(gate_weight, pad),
        jnp.pad(up_weight, pad),
        jnp.pad(down_weight, pad),
        cot_low,
        w_out,
    )
    w_gate, w_up, w_down = (w.reshape(-1, D) for w in (w_gate, w_up, w_down))
    cot_rows, rows_two = cot_rows.reshape(-1, D), rows_two.reshape(-1, D)
    factor_two = lax.rsqrt(jnp.mean(middle * middle, axis=-1, keepdims=True) + norm_eps)

    gate = dot(rows_two, w_gate, (1, 1))
    upward = dot(rows_two, w_up, (1, 1))
    hidden_grad = dot(cot_rows, w_down, (1, 1))
    sigma = jax.nn.sigmoid(gate)
    hidden = (gate * sigma * upward).astype(BF)
    gate_grad = (hidden_grad * upward * sigma * (1.0 + gate * (1.0 - sigma))).astype(BF)
    upward_grad = (hidden_grad * gate * sigma).astype(BF)
    ffn_part = dot(hidden, w_down, (1, 0)).astype(BF)
    grad_part = (dot(gate_grad, w_gate, (1, 0)) + dot(upward_grad, w_up, (1, 0))).astype(BF)
    ffn_lead = lead_of(FFN_DIMS) + (ROWS, D)
    gate_part, up_part, down_part = (
        dot(a, b, (0, 0)).astype(BF).reshape(ffn_lead)
        for a, b in ((gate_grad, rows_two), (upward_grad, rows_two), (hidden, cot_rows))
    )
    rows_lead = lead_of(ROW_DIMS) + (TOK, D)
    normed_two_grad, *down_sums = scatter_rows(grad_part.reshape(rows_lead), down_part)

    cot_full = cot_low.astype(F32)
    scaled_two = gain_two * normed_two_grad
    gain_two_grad = jnp.sum(normed_two_grad * middle * factor_two, axis=0)
    middle_grad = (
        cot_full
        + factor_two * scaled_two
        - middle * factor_two**3 * jnp.mean(scaled_two * middle, axis=-1, keepdims=True)
    )
    branch_grad = middle_grad.astype(BF)
    grad_slots = dot(branch_grad, w_out, (1, 1)).astype(BF)
    out_part = dot(slots, branch_grad, (0, 0)).astype(BF)
    lead = lead_of(AXES)
    qkv_grad, *parts, out_sum, ffn_total = attend_back(
        kv,
        queries,
        attended,
        grad_slots,
        lse,
        first,
        cosine,
        sine,
        spread,
        gate_part,
        up_part,
        out_part.reshape(lead + (16, D)),
        ffn_part.reshape(rows_lead),
    )
    layer_out = (middle + ffn_total).astype(BF)
    normed_one_grad = dot(qkv_grad, w_qkv, (1, 0))
    scaled_one = gain_one * normed_one_grad
    gain_one_grad = jnp.sum(normed_one_grad * inputs * factor_one, axis=0)
    input_grad = (
        middle_grad
        + factor_one * scaled_one
        - inputs * factor_one**3 * jnp.mean(scaled_one * inputs, axis=-1, keepdims=True)
    )

    qkv_part = dot(qkv_grad, normed_one, (0, 0)).astype(BF)
    bias_part = jnp.sum(qkv_grad.astype(F32), axis=0)
    small_part = jnp.concatenate(
        [
            bias_part.reshape(128, 16),
            gain_one_grad.reshape(128, 12),
            gain_two_grad.reshape(128, 12),
        ],
        axis=1,
    ).astype(BF)
    small_part = jnp.pad(small_part[:, None], ((0, 0), (0, 15), (0, 88)))
    qkv_sum, small_sum, gate_sum, up_sum, down_sum = scatter_weight_grads(
        qkv_part.reshape(lead + (16, D)),
        small_part.reshape(lead + (16, 128)),
        (*parts, *down_sums),
    )
    return (
        layer_out[None],
        input_grad[None],
        qkv_sum,
        small_sum[0, :16],
        out_sum[:out_rows],
        small_sum[0, 16:40].reshape(2, 12),
        gate_sum[:units],
        up_sum[:units],
        down_sum[:units],
    )


def solution(mesh):
    fine = Mesh(mesh.devices.reshape(tuple(SIZE[a] for a in AXES)), AXES)
    dp, ctx = ("zl", "c"), ("y", "x", "zh")
    in_specs = (
        P(dp, ctx, None),
        P(AXES, None),
        P(AXES),
        P(AXES, None),
        P(None, AXES),
        P(AXES, None),
        P(AXES, None),
        P(AXES, None),
        P(dp, None),
        P(dp, ctx, None),
    )
    out_specs = (
        P(dp, ctx, None),
        P(dp, ctx, None),
        P(AXES, None),
        P(AXES),
        P(AXES, None),
        P(None, AXES),
        P(AXES, None),
        P(AXES, None),
        P(AXES, None),
    )
    return jax.shard_map(local, mesh=fine, in_specs=in_specs, out_specs=out_specs, check_vma=False)
```

```python
import math

import jax
import jax.numpy as jnp
from jax import lax
from jax.experimental import pallas as pl
from jax.experimental.pallas import tpu as pltpu
from jax.sharding import Mesh
from jax.sharding import PartitionSpec as P

H = 12
KVH = 2
HD = 128
HQ = 1536
D = 1536
TOK = 128
ROWS = 80

norm_eps = 1e-06
rope_base = 1000000.0
doc_kinds = 3

AXES = ("zl", "c", "y", "x", "zh")
SIZE = {"zl": 2, "c": 2, "y": 4, "x": 4, "zh": 2}
PARTS_OF = {"z": ("zl", "zh"), "x": ("x",), "y": ("y",), "c": ("c",), "zh": ("zh",)}
REACH = {"z": (1, 2, 3), "x": (1, 2, 3), "y": (1, 2, 3), "c": (1,), "zh": (1,)}
BF = jnp.bfloat16
F32 = jnp.float32
ANY = pl.BlockSpec(memory_space=pl.ANY)
VMEM = pl.BlockSpec(memory_space=pltpu.VMEM)


def here():
    return {a: lax.axis_index(a) for a in AXES}


def peer(me, axis, k):
    to = dict(me)
    if axis == "z":
        z = lax.rem(me["zh"] * 2 + me["zl"] + k, 4)
        to["zl"], to["zh"] = lax.rem(z, 2), lax.div(z, 2)
    else:
        to[axis] = lax.rem(me[axis] + k, SIZE[axis])
    return to


def device_id(at):
    return tuple(at[a] for a in AXES)


def place(dims, at, whole, tail=()):
    return tuple(slice(None) if d in whole else at[d] for d in dims) + tuple(tail)


class Links:
    def __init__(self, me, send, recv):
        self.me, self.send, self.recv, self.used = me, send, recv, 0

    def copy(self, src, dst, axis, k):
        i = self.used
        self.used += 1
        c = pltpu.make_async_remote_copy(
            src_ref=src,
            dst_ref=dst,
            send_sem=self.send.at[i],
            recv_sem=self.recv.at[i],
            device_id=device_id(peer(self.me, axis, k)),
            device_id_type=pl.DeviceIdType.MESH,
        )
        c.start()
        return c


def greet(me, axes):
    barrier = pltpu.get_barrier_semaphore()
    count = 0
    for axis in axes:
        for k in REACH[axis]:
            pl.semaphore_signal(
                barrier,
                inc=1,
                device_id=device_id(peer(me, axis, k)),
                device_id_type=pl.DeviceIdType.MESH,
            )
            count += 1
    pl.semaphore_wait(barrier, count)


def halves_of(tail, cols):
    rows = tail[:-1] if tail else (slice(None),)
    start = tail[-1].start if tail else 0
    cut = cols // 2
    return tuple(rows + (slice(start + cut * i, start + cut * (i + 1)),) for i in range(2))


def gather_stream(links, block, buf, dims, tail, order):
    me = links.me
    whole = ()
    cols = block.shape[-1]
    for n, axis in enumerate(order):
        direct = axis.endswith("!")
        axis = axis.rstrip("!")
        mine = place(dims, me, whole, tail)
        src = block if n == 0 else buf.at[mine]
        ring = len(REACH[axis]) == 3 and not direct
        near = (1, 3) if ring else REACH[axis]
        copies = [links.copy(src, buf.at[mine], axis, k) for k in near]
        yield
        for c in copies:
            c.wait()
        if ring:
            copies = []
            for k, half in zip(near, halves_of(tail, cols), strict=True):
                theirs = buf.at[place(dims, peer(me, axis, 4 - k), whole, half)]
                copies.append(links.copy(theirs, theirs, axis, k))
            yield
            for c in copies:
                c.wait()
        whole = whole + PARTS_OF[axis]


def run_streams(streams):
    live = list(streams)
    while live:
        live = [s for s in live if next(s, live) is not live]


def step(streams):
    for s in streams:
        next(s, None)


def count_gather(orders):
    return sum({"c": 1, "zh": 1}.get(a, 3 if "!" in a else 4) for order in orders for a in order)


def count_scatter(orders):
    return sum(len(REACH[a]) for order in orders for a in order)


THIRDS = tuple((slice(None), slice(512 * i, 512 * (i + 1))) for i in range(3))
ORDERS = (("x", "y", "z"), ("y", "z", "x"), ("z", "x", "y"))
HALVES = tuple((slice(None), slice(768 * i, 768 * (i + 1))) for i in range(2))
FFN_ORDERS = (("y", "z"), ("z", "y"))
FFN_DIMS = ("zl", "y", "zh")
ROW_DIMS = ("x", "c")
KV_DIMS = ("y", "x", "zh")


def lead_of(dims):
    return tuple(SIZE[d] for d in dims)


def rest_of(dims, axis):
    return tuple(d for d in dims if d not in PARTS_OF[axis])


def scatter_scratch(dims, order, rows, cols):
    shapes = []
    for axis in order:
        dims = rest_of(dims, axis)
        shapes.append(pltpu.VMEM((len(REACH[axis]),) + lead_of(dims) + (rows, cols), BF))
        shapes.append(pltpu.VMEM(lead_of(dims) + (rows, cols), BF))
    return shapes


def sum_blocks(own, arrived, out, lead, rows, step):
    count = 1
    for n in lead:
        count *= n
    per = rows // step
    parts = arrived.shape[0]

    def body(i, carry):
        block, row = lax.div(i, per), lax.rem(i, per)
        index = []
        for n in reversed(lead):
            index.append(lax.rem(block, n))
            block = lax.div(block, n)
        at = tuple(reversed(index)) + (pl.ds(pl.multiple_of(row * step, step), step),)
        total = own[at].astype(F32)
        for p in range(parts):
            total = total + arrived[(p,) + at].astype(F32)
        out[at] = total.astype(out.dtype)
        return carry

    lax.fori_loop(0, count * per, body, 0)


def scatter_stream(links, local, source, dims, tail, order, scratch, out, rows, step):
    me = links.me
    now = None
    for n, axis in enumerate(order):
        arrived, own = scratch[2 * n], scratch[2 * n + 1]
        gone = PARTS_OF[axis]
        keep = tuple(d for d in dims if d not in gone)
        end = tail if n == 0 else ()
        base = source if n == 0 else now
        copies = []
        for k in REACH[axis]:
            to = peer(me, axis, k)
            src = base.at[place(dims, to, keep, end)]
            copies.append(links.copy(src, arrived.at[k - 1], axis, k))
        held = base.at[place(dims, me, keep, end)]
        staged = n == 0 and local is not None
        if staged:
            mine = pltpu.make_async_copy(held, own, local)
            mine.start()
        yield
        if staged:
            mine.wait()
            held = own
        for c in copies:
            c.wait()
        target = out if n == len(order) - 1 else own
        sum_blocks(held, arrived, target, lead_of(keep), rows, step)
        now, dims = own, keep


FIRST_STAGE = (("y",), ("z",))
LAST_STAGE = (("z",), ("y",))
KV_ORDERS = (("y", "x", "zh"), ("x", "y", "zh"))
ALL_ORDERS = tuple(("c",) + o for o in ORDERS)


def first_stage_scratch():
    scratch, sums = [], []
    for order in FIRST_STAGE:
        scratch += scatter_scratch(FFN_DIMS, order, ROWS, 768)
        sums.append(jax.ShapeDtypeStruct(lead_of(rest_of(FFN_DIMS, order[0])) + (ROWS, 768), BF))
    return scratch, sums


def first_stage(links, local, used, part, sums, scratch):
    return [
        scatter_stream(
            links,
            local.at[used + i],
            part,
            FFN_DIMS,
            HALVES[i],
            FIRST_STAGE[i],
            scratch[2 * i : 2 * i + 2],
            sums[i],
            ROWS,
            16,
        )
        for i in range(2)
    ]


def rows_scatter_kernel(rows, part, out, sum_a, sum_b, send, recv, local, *scratch):
    me = here()
    links = Links(me, send, recv)
    greet(me, ("x", "y", "z", "c"))
    streams = [
        scatter_stream(links, local.at[2], rows, ROW_DIMS, (), ("c", "x"), scratch[4:], out, TOK, 16)
    ]
    weights = first_stage(links, local, 0, part, (sum_a, sum_b), scratch[:4])
    step(streams)
    step(weights)
    run_streams(streams)
    step(weights)


def scatter_rows(rows, part):
    copies = count_scatter([("c", "x")]) + count_scatter(FIRST_STAGE)
    scratch, sums = first_stage_scratch()
    return pl.pallas_call(
        rows_scatter_kernel,
        out_shape=(jax.ShapeDtypeStruct((TOK, D), F32),) + tuple(sums),
        in_specs=[ANY] * 2,
        out_specs=(VMEM,) * 3,
        scratch_shapes=[
            pltpu.SemaphoreType.DMA((copies,)),
            pltpu.SemaphoreType.DMA((copies,)),
            pltpu.SemaphoreType.DMA((3,)),
        ]
        + scratch
        + scatter_scratch(ROW_DIMS, ("c", "x"), TOK, D),
        compiler_params=pltpu.CompilerParams(
            collective_id=4, has_side_effects=True, vmem_limit_bytes=48 * 2**20
        ),
    )(rows, part)


GROUP = H // KVH
GQ = GROUP * TOK
KEYS = 512
SCALE = HD**-0.5
TO_LOG2 = SCALE * math.log2(math.e)


def head(h):
    return slice(128 * h, 128 * (h + 1))


def turned(v):
    return pltpu.roll(v, 64, 1)


def key_blocks():
    ctx = lax.axis_index("y") * 8 + lax.axis_index("x") * 2 + lax.axis_index("zh")
    return lax.div(ctx, 4) + 1, ctx * TOK


def key_block_of(ref, b, cols):
    return ref[lax.div(b, 2), pl.ds(lax.rem(b, 2) * 2, 2), :, :, cols].reshape(KEYS, HD)


def allowed_keys(b, first, row):
    key = b * KEYS + lax.broadcasted_iota(jnp.int32, (KEYS, GQ), 0)
    query = row + lax.rem(lax.broadcasted_iota(jnp.int32, (1, GQ), 1), TOK)
    return (key <= query) & (key >= first)


def mm(a, b, contract):
    return lax.dot_general(
        a, b, ((contract[:1], contract[1:]), ((), ())), preferred_element_type=F32
    )


def attend_group(g, kv, qs, first, row, blocks, acc, stats):
    acc[...] = jnp.zeros_like(acc)
    stats[0:1] = jnp.full((1, GQ), -1e30, F32)
    stats[1:2] = jnp.zeros((1, GQ), F32)

    def body(b, carry):
        keys = key_block_of(kv, b, head(g))
        values = key_block_of(kv, b, head(2 + g))
        raw = mm(keys, qs[g], (1, 1)) * TO_LOG2
        raw = jnp.where(allowed_keys(b, first, row), raw, -1e30)
        old = stats[0:1]
        top = jnp.maximum(old, jnp.max(raw, axis=0, keepdims=True))
        probs = jnp.exp2(raw - top)
        shrink = jnp.exp2(old - top)
        stats[0:1] = top
        stats[1:2] = stats[1:2] * shrink + jnp.sum(probs, axis=0, keepdims=True)
        acc[...] = acc[...] * shrink + mm(values.T, probs.astype(BF), (1, 0))
        return carry

    lax.fori_loop(0, blocks, body, 0)


QKV_ORDERS = (("x!", "y!", "z!", "c"), ("y!", "z!", "x!", "c"), ("z!", "x!", "y!", "c"))
OUT_ORDER = ("z!", "y!", "x", "c")
KEY_ORDERS = (("zh", "x!", "y"), ("zh", "y!", "x"))
ROW_ORDER = ("x", "c")


def spread_row(blocks, offset, width, count):
    f = lax.broadcasted_iota(jnp.int32, (1, count), 1).astype(F32)
    block = jnp.floor((f + 0.5) * (1.0 / width))
    lane = offset + f - block * width
    index = lax.broadcasted_iota(jnp.int32, (128, count), 0).astype(F32)
    pick = (index == lane).astype(BF)
    spread = mm(blocks, pick, (1, 0))
    return jnp.sum(jnp.where(index == block, spread, 0.0), axis=0, keepdims=True)


def front_kernel(*refs):
    tokens, cosine, sine, first_ref, spread, small, out_in, gate_in, up_in, down_in = refs[:10]
    qkv_block, cot = refs[10:12]
    normed_one, gains, queries, attended, slots, lse, middle = refs[12:19]
    kv_hbm, qkv_hbm, out_hbm, gate_all, up_all, down_all, cot_all, rows_all = refs[19:27]
    small_all, w_qkv, w_out, kv, out_block, gate, up, down = refs[27:35]
    qkv, block, qs, acc, stats, normed, send, recv, local = refs[35:]
    me = here()
    links = Links(me, send, recv)
    own = []

    def keep(src, dst):
        own.append(pltpu.make_async_copy(src, dst, local.at[len(own)]))
        own[-1].start()
        return own[-1]

    first_copies = [
        keep(qkv_block, w_qkv.at[place(AXES, me, ())]),
        keep(small, small_all.at[place(AXES, me, ())]),
        keep(cot, cot_all.at[place(ROW_DIMS, me, ())]),
    ]
    out_rows = out_in.shape[0]
    out_block[0:out_rows] = out_in[...]
    out_block[out_rows:16] = jnp.zeros((16 - out_rows, D), BF)
    first_copies.append(keep(out_block, w_out.at[place(AXES, me, ())]))
    units = gate_in.shape[0]
    ffn = ((gate_in, gate, gate_all), (up_in, up, up_all), (down_in, down, down_all))
    for a, b, c in ffn:
        b[0:units] = a[...]
        b[units:ROWS] = jnp.zeros((ROWS - units, D), BF)
        first_copies.append(keep(b, c.at[place(FFN_DIMS, me, ())]))
    greet(me, ("x", "y", "z", "c", "zh"))
    qkvs = [
        gather_stream(links, qkv_block.at[tail], w_qkv, AXES, tail, order)
        for order, tail in zip(QKV_ORDERS, THIRDS, strict=True)
    ]
    qkvs.append(gather_stream(links, small, small_all, AXES, (), QKV_ORDERS[1]))
    outs = [gather_stream(links, out_block, w_out, AXES, (), OUT_ORDER)]
    by_y, by_z = (
        [gather_stream(links, a.at[tail], b, FFN_DIMS, tail, order) for _, a, b in ffn]
        for order, tail in zip(FFN_ORDERS, HALVES, strict=True)
    )
    cots = [gather_stream(links, cot, cot_all, ROW_DIMS, (), ROW_ORDER)]
    step(qkvs)
    step(outs)
    whole = tokens[...].astype(F32)
    factor = lax.rsqrt(jnp.sum(whole * whole, axis=1, keepdims=True) / D + norm_eps)
    for c in first_copies:
        c.wait()
    step(qkvs)
    step(outs)
    step(qkvs)
    step(qkvs)
    step(by_y)
    step(by_z)
    step(outs)
    step(qkvs)
    saved = [keep(w_qkv, qkv_hbm)]
    row = lax.broadcasted_iota(jnp.int32, (128, 2048), 0)
    entry = lax.broadcasted_iota(jnp.int32, (128, 2048), 1)
    blocks = mm((entry == row * 16).astype(BF), small_all[...].reshape(2048, 128), (1, 0)).astype(BF)
    bias = spread_row(blocks, 0, 16, 2048)
    gain = spread_row(blocks, 16, 12, D)
    gains[0:8] = jnp.broadcast_to(gain, (8, D))
    gain_two = spread_row(blocks, 28, 12, D)
    gains[8:16] = jnp.broadcast_to(gain_two, (8, D))
    normed_one[...] = (tokens[...].astype(F32) * factor * gain).astype(BF)
    cos, sin = cosine[...], sine[...]

    def project(j):
        part = w_qkv[j // 4, (j // 2) % 2, 2 * (j % 2) : 2 * (j % 2) + 2].reshape(256, D)
        return mm(normed_one[...], part, (1, 1)) + bias[:, 256 * j : 256 * (j + 1)]

    part = project(6)
    for g in range(KVH):
        one = part[:, head(g)]
        block[:, head(g)] = (one * cos + turned(one) * sin).astype(BF)
    block[:, 256:512] = project(7).astype(BF)
    mine = keep(block, kv.at[place(KV_DIMS, me, ())])
    keys = []
    for half, order in enumerate(KEY_ORDERS):
        tail = (slice(None), slice(256 * half, 256 * (half + 1)))
        keys.append(gather_stream(links, block.at[tail], kv, KV_DIMS, tail, order))
    step(keys)
    step(by_y)
    step(by_z)
    mine.wait()
    for j in range(3):
        qkv[:, 256 * j : 256 * (j + 1)] = project(j)
    step(keys)
    step(by_y)
    for j in range(3, 6):
        qkv[:, 256 * j : 256 * (j + 1)] = project(j)
    step(keys)
    for h in range(H):
        one = qkv[:, head(h)]
        rotated = (one * cos + turned(one) * sin).astype(BF)
        queries[:, head(h)] = rotated
        qs[h // GROUP, (h % GROUP) * TOK : (h % GROUP + 1) * TOK, :] = rotated
    step(keys)
    step(keys)
    step(by_z)
    step(outs)
    step(cots)
    saved.append(keep(kv, kv_hbm))
    count, start = key_blocks()
    first = first_ref[0:1]
    for g in range(KVH):
        attend_group(g, kv, qs, first, start, count, acc, stats)
        total = stats[1:2]
        lse[g] = jnp.broadcast_to(stats[0:1] + jnp.log2(total), (8, GQ))
        acc[...] = acc[...] / total
        for i in range(GROUP):
            attended[:, head(GROUP * g + i)] = acc[:, head(i)].T
        if g == 0:
            step(outs)
    step(by_y)
    for i in range(4):
        part = attended[:, 384 * i : 384 * (i + 1)].astype(BF)
        slots[:, 512 * i : 512 * (i + 1)] = mm(part, spread[...], (1, 0)).astype(BF)
    step(outs)
    saved.append(keep(w_out, out_hbm))
    square = jnp.zeros((TOK, 1), F32)
    for i in range(3):
        cols = slice(512 * i, 512 * (i + 1))
        part = w_out[:, :, :, :, :, :, cols].reshape(2048, 512)
        part = tokens[:, cols].astype(F32) + mm(slots[...], part, (1, 0))
        middle[:, cols] = part
        square = square + jnp.sum(part * part, axis=1, keepdims=True)
    factor = lax.rsqrt(square / D + norm_eps)
    normed[...] = (middle[...] * factor * gains[8:9]).astype(BF)
    mine = keep(normed, rows_all.at[place(ROW_DIMS, me, ())])
    rows = [gather_stream(links, normed, rows_all, ROW_DIMS, (), ROW_ORDER)]
    step(rows)
    step(cots)
    mine.wait()
    step(rows)
    step(by_z)
    step(rows)
    step(cots)
    step(rows)
    step(cots)
    step(by_y)
    step(by_z)
    for c in saved:
        c.wait()


def front(tokens, cosine, sine, first, spread, small, out_weight, gate, up, down, qkv_weight, cot):
    every = lead_of(AXES) + (16, D)
    kv = lead_of(KV_DIMS) + (TOK, 512)
    ffn = jax.ShapeDtypeStruct(lead_of(FFN_DIMS) + (ROWS, D), BF)
    rows = jax.ShapeDtypeStruct(lead_of(ROW_DIMS) + (TOK, D), BF)
    copies = count_gather(QKV_ORDERS + QKV_ORDERS[:1] + (OUT_ORDER, ROW_ORDER, ROW_ORDER))
    copies += count_gather(KEY_ORDERS + 3 * FFN_ORDERS)
    return pl.pallas_call(
        front_kernel,
        out_shape=(
            jax.ShapeDtypeStruct((TOK, D), BF),
            jax.ShapeDtypeStruct((16, D), F32),
            jax.ShapeDtypeStruct((TOK, HQ), BF),
            jax.ShapeDtypeStruct((TOK, HQ), F32),
            jax.ShapeDtypeStruct((TOK, 2048), BF),
            jax.ShapeDtypeStruct((KVH, 8, GQ), F32),
            jax.ShapeDtypeStruct((TOK, D), F32),
            jax.ShapeDtypeStruct(kv, BF),
            jax.ShapeDtypeStruct(every, BF),
            jax.ShapeDtypeStruct(every, BF),
            ffn,
            ffn,
            ffn,
            rows,
            rows,
        ),
        in_specs=[VMEM] * 10 + [ANY] * 2,
        out_specs=(VMEM,) * 7 + (ANY,) * 8,
        scratch_shapes=[
            pltpu.VMEM(lead_of(AXES) + (16, 128), BF),
            pltpu.VMEM(every, BF),
            pltpu.VMEM(every, BF),
            pltpu.VMEM(kv, BF),
            pltpu.VMEM((16, D), BF),
            pltpu.VMEM((ROWS, D), BF),
            pltpu.VMEM((ROWS, D), BF),
            pltpu.VMEM((ROWS, D), BF),
            pltpu.VMEM((TOK, HQ), F32),
            pltpu.VMEM((TOK, 512), BF),
            pltpu.VMEM((KVH, GQ, HD), BF),
            pltpu.VMEM((HD, GQ), F32),
            pltpu.VMEM((8, GQ), F32),
            pltpu.VMEM((TOK, D), BF),
            pltpu.SemaphoreType.DMA((copies,)),
            pltpu.SemaphoreType.DMA((copies,)),
            pltpu.SemaphoreType.DMA((12,)),
        ],
        compiler_params=pltpu.CompilerParams(
            collective_id=2, has_side_effects=True, vmem_limit_bytes=56 * 2**20
        ),
    )(tokens, cosine, sine, first, spread, small, out_weight, gate, up, down, qkv_weight, cot)


def grad_group(g, kv, qs, gs, lse, delta, first, row, blocks, query_grad, kv_grad):
    query_grad[...] = jnp.zeros_like(query_grad)

    def body(b, carry):
        at = (lax.div(b, 2), pl.ds(lax.rem(b, 2) * 2, 2), slice(None), slice(None))
        keys = key_block_of(kv, b, head(g))
        values = key_block_of(kv, b, head(2 + g))
        raw = mm(keys, qs[g], (1, 1)) * TO_LOG2
        probs = jnp.where(allowed_keys(b, first, row), jnp.exp2(raw - lse), 0.0)
        prob_grad = mm(values, gs[g], (1, 1))
        score_grad = (probs * (prob_grad - delta)).astype(BF)
        key_term = mm(score_grad, qs[g], (1, 0)) * SCALE
        value_term = mm(probs.astype(BF), gs[g], (1, 0))
        kv_grad[at + (head(g),)] = key_term.astype(BF).reshape(2, 2, TOK, HD)
        kv_grad[at + (head(2 + g),)] = value_term.astype(BF).reshape(2, 2, TOK, HD)
        query_grad[...] += mm(keys.T, score_grad, (1, 0))
        return carry

    lax.fori_loop(0, blocks, body, 0)


def collect_row(row, offset, width):
    count = row.shape[1]
    f = lax.broadcasted_iota(jnp.int32, (1, count), 1).astype(F32)
    block = jnp.floor((f + 0.5) * (1.0 / width))
    lane = offset + f - block * width
    index = lax.broadcasted_iota(jnp.int32, (128, count), 0).astype(F32)
    spread = jnp.where(index == block, row, 0.0).astype(BF)
    return mm(spread, (index == lane).astype(BF), (1, 1))


def back_kernel(*refs):
    kv, queries, attended, grad_slots, lse, first_ref, cosine, sine, spread = refs[:9]
    tokens, normed_one, gains, middle, middle_grad, gain_two_grad = refs[9:15]
    gate_part, up_part, down_a, down_b, out_part, ffn_rows, w_qkv = refs[15:22]
    layer_out, input_grad, qkv_out, small_out, out_out, gate_out, up_out, down_out = refs[22:30]
    qkv_part = refs[30]
    qs, gs, delta, query_grad, kv_grad, kv_out, qkv_grad, weight, staged, total = refs[31:41]
    small, ffn_total, free, send, recv, local = refs[41:47]
    scratch = list(refs[47:])

    def take(n):
        return [scratch.pop(0) for _ in range(n)]

    me = here()
    links = Links(me, send, recv)
    used = [0]

    def slot():
        used[0] += 1
        return local.at[used[0] - 1]

    def fetch(j):
        c = pltpu.make_async_copy(w_qkv.at[pl.ds(512 * j, 512)], weight.at[j % 2], slot())
        c.start()
        return c

    fetched = [fetch(0), fetch(1)]
    greet(me, ("zh", "x", "y", "z", "c"))
    shared = [take(8) for _ in THIRDS]
    outs = [
        scatter_stream(links, slot(), out_part, AXES, tail, order, part, out_out.at[tail], 16, 16)
        for order, tail, part in zip(ALL_ORDERS, THIRDS, shared, strict=True)
    ]
    rows = [
        scatter_stream(
            links, slot(), ffn_rows, ROW_DIMS, (), ("c", "x"), take(4), ffn_total, TOK, 16
        )
    ]
    gates, ups = (
        [
            scatter_stream(
                links, slot(), source, FFN_DIMS, tail, order, take(4), target.at[tail], ROWS, 16
            )
            for order, tail in zip(FFN_ORDERS, HALVES, strict=True)
        ]
        for source, target in ((gate_part, gate_out), (up_part, up_out))
    )
    downs = [
        scatter_stream(
            links,
            slot(),
            source,
            rest_of(FFN_DIMS, order[0]),
            (),
            order[1:],
            take(2),
            down_out.at[tail],
            ROWS,
            16,
        )
        for source, order, tail in zip((down_a, down_b), FFN_ORDERS, HALVES, strict=True)
    ]
    step(outs)
    step(rows)
    step(downs)
    step(gates)
    blocks, row = key_blocks()
    first = first_ref[0:1]
    for i in range(4):
        part = mm(grad_slots[:, 512 * i : 512 * (i + 1)], spread[...], (1, 1))
        for j in range(3):
            h = 3 * i + j
            one = part[:, head(j)]
            gs[h // GROUP, (h % GROUP) * TOK : (h % GROUP + 1) * TOK, :] = one.astype(BF)
            both = (one * attended[:, head(h)]).T
            delta[h // GROUP : h // GROUP + 1, head(h % GROUP)] = jnp.sum(
                both, axis=0, keepdims=True
            )
            qs[h // GROUP, (h % GROUP) * TOK : (h % GROUP + 1) * TOK, :] = queries[:, head(h)]

    def clear(b, carry):
        at = (lax.div(b, 2), pl.ds(lax.rem(b, 2) * 2, 2))
        kv_grad[at] = jnp.zeros((2, 2, TOK, 512), BF)
        return carry

    lax.fori_loop(blocks, 8, clear, 0)
    step(outs)
    step(rows)
    cos, sin = cosine[...], sine[...]
    for g in range(KVH):
        grad_group(
            g, kv, qs, gs, lse[g, 0:1], delta[g : g + 1], first, row, blocks, query_grad, kv_grad
        )
        for i in range(GROUP):
            one = query_grad[:, head(i)].T * SCALE
            qkv_grad[:, head(GROUP * g + i)] = (one * cos - turned(one) * sin).astype(BF)
    keys = []
    for half, order in enumerate(KV_ORDERS):
        tail = (slice(None), slice(256 * half, 256 * (half + 1)))
        keys.append(
            scatter_stream(
                links, None, kv_grad, KV_DIMS, tail, order, take(6), kv_out.at[half], TOK, 32
            )
        )
    step(keys)
    step(ups[1:])
    stored = []

    def weight_terms(j):
        if j >= 2:
            fetched.append(fetch(j))
            stored[j - 2].wait()
        part = qkv_grad[:, 512 * j : 512 * (j + 1)]
        lhs = jnp.concatenate(
            [part[:, head(i)].astype(F32).T.astype(BF) for i in range(4)], axis=0
        )
        for i in range(3):
            cols = slice(512 * i, 512 * (i + 1))
            grad = mm(lhs, normed_one[:, cols], (1, 0)).astype(BF)
            staged[j % 2, :, :, :, :, cols] = grad.reshape(4, 4, 2, 16, 512)
        c = pltpu.make_async_copy(staged.at[j % 2], qkv_part.at[j // 2, j % 2], slot())
        c.start()
        stored.append(c)
        fetched[j].wait()
        for i in range(3):
            cols = slice(512 * i, 512 * (i + 1))
            term = mm(part, weight[j % 2, :, cols], (1, 0))
            if j == 0:
                total[:, cols] = term
            else:
                total[:, cols] += term

    weight_terms(0)
    weight_terms(1)
    step(outs)
    weight_terms(2)
    step(keys)
    step(outs)
    step(keys)
    step(gates)
    step(ups[:1])
    step(outs)
    for axis in ("c", "x", "y", "z"):
        for k in REACH[axis]:
            pl.semaphore_signal(
                free,
                inc=1,
                device_id=device_id(peer(me, axis, k)),
                device_id_type=pl.DeviceIdType.MESH,
            )
    step(keys)
    for g in range(KVH):
        one = kv_out[0, :, head(g)]
        qkv_grad[:, head(H + g)] = (one * cos - turned(one) * sin).astype(BF)
        qkv_grad[:, head(H + 2 + g)] = kv_out[1, :, head(g)].astype(BF)
    weight_terms(3)
    for c in stored[2:]:
        c.wait()
    pl.semaphore_wait(free, 10)
    qkvs = [
        scatter_stream(links, slot(), qkv_part, AXES, tail, order, part, qkv_out.at[tail], 16, 16)
        for order, tail, part in zip(ALL_ORDERS, THIRDS, shared, strict=True)
    ]
    step(qkvs)
    whole = tokens[...].astype(F32)
    factor = lax.rsqrt(jnp.sum(whole * whole, axis=1, keepdims=True) / D + norm_eps)
    grad = total[...]
    gain_one_grad = jnp.sum(grad * whole * factor, axis=0, keepdims=True)
    bias_grad = jnp.sum(qkv_grad[...].astype(F32), axis=0, keepdims=True)
    blocks_grad = collect_row(bias_grad, 0, 16)
    blocks_grad = blocks_grad + collect_row(gain_one_grad, 16, 12)
    blocks_grad = blocks_grad + collect_row(gain_two_grad[0:1], 28, 12)
    blocks_grad = jnp.broadcast_to(blocks_grad[:, None, :], (128, 16, 128)).astype(BF)
    small[...] = blocks_grad.reshape(lead_of(AXES) + (16, 128))
    smalls = [
        scatter_stream(links, None, small, AXES, (), ALL_ORDERS[0], take(8), small_out, 16, 16)
    ]
    step(smalls)
    step(qkvs)
    step(smalls)
    scaled = grad * gains[0:1]
    mean = jnp.sum(scaled * whole, axis=1, keepdims=True) / D
    input_grad[...] = middle_grad[...] + factor * scaled - whole * (factor * factor * factor * mean)
    step(rows)
    layer_out[...] = (middle[...] + ffn_total[...]).astype(BF)
    step(downs)
    step(gates)
    step(qkvs)
    step(smalls)
    step(ups)
    step(qkvs)
    step(smalls)
    step(qkvs)
    step(smalls)
    step(ups)


def back(inputs, parts, w_qkv):
    copies = count_scatter(KV_ORDERS) + 2 * count_scatter(ALL_ORDERS)
    copies += count_scatter(ALL_ORDERS[:1]) + count_scatter([("c", "x")])
    copies += 2 * count_scatter(FFN_ORDERS) + count_scatter(LAST_STAGE)
    every = lead_of(AXES) + (16, D)
    scratch = []
    for order in ALL_ORDERS:
        scratch += scatter_scratch(AXES, order, 16, 512)
    scratch += scatter_scratch(ROW_DIMS, ("c", "x"), TOK, D)
    for _ in range(2):
        for order in FFN_ORDERS:
            scratch += scatter_scratch(FFN_DIMS, order, ROWS, 768)
    for order in FFN_ORDERS:
        scratch += scatter_scratch(rest_of(FFN_DIMS, order[0]), order[1:], ROWS, 768)
    for order in KV_ORDERS:
        scratch += scatter_scratch(KV_DIMS, order, TOK, 256)
    scratch += scatter_scratch(AXES, ALL_ORDERS[0], 16, 128)
    attn = jax.ShapeDtypeStruct((16, D), F32)
    ffn = jax.ShapeDtypeStruct((ROWS, D), F32)
    return pl.pallas_call(
        back_kernel,
        out_shape=(
            jax.ShapeDtypeStruct((TOK, D), BF),
            jax.ShapeDtypeStruct((TOK, D), F32),
            attn,
            jax.ShapeDtypeStruct((16, 128), F32),
            attn,
            ffn,
            ffn,
            ffn,
            jax.ShapeDtypeStruct(every, BF),
        ),
        in_specs=[VMEM] * 15 + [ANY] * 7,
        out_specs=(VMEM,) * 8 + (ANY,),
        scratch_shapes=[
            pltpu.VMEM((KVH, GQ, HD), BF),
            pltpu.VMEM((KVH, GQ, HD), BF),
            pltpu.VMEM((8, GQ), F32),
            pltpu.VMEM((HD, GQ), F32),
            pltpu.VMEM(lead_of(KV_DIMS) + (TOK, 512), BF),
            pltpu.VMEM((2, TOK, 256), F32),
            pltpu.VMEM((TOK, 2048), BF),
            pltpu.VMEM((2, 512, D), BF),
            pltpu.VMEM((2, 4, 4, 2, 16, D), BF),
            pltpu.VMEM((TOK, D), F32),
            pltpu.VMEM(lead_of(AXES) + (16, 128), BF),
            pltpu.VMEM((TOK, D), F32),
            pltpu.SemaphoreType.REGULAR,
            pltpu.SemaphoreType.DMA((copies,)),
            pltpu.SemaphoreType.DMA((copies,)),
            pltpu.SemaphoreType.DMA((24,)),
        ]
        + scratch,
        compiler_params=pltpu.CompilerParams(
            collective_id=5, has_side_effects=True, vmem_limit_bytes=63 * 2**20
        ),
    )(*inputs, *parts, w_qkv)


def positions_of(documents):
    index = jnp.arange(documents.shape[0], dtype=jnp.int32)
    kinds = jnp.arange(doc_kinds, dtype=jnp.int32)
    counts = jnp.sum((documents[None, :] == kinds[:, None]).astype(jnp.int32), axis=1)
    starts = jnp.cumsum(counts) - counts
    first = jnp.sum(jnp.where(documents[:, None] == kinds[None, :], starts[None, :], 0), axis=1)
    return index - first


def rope_tables(position):
    half = HD // 2
    inverse = rope_base ** (-(jnp.arange(half, dtype=jnp.float32) * 2.0 / HD))
    angle = position.astype(jnp.float32)[:, None] * inverse[None, :]
    angle = jnp.concatenate([angle, angle], axis=1)
    return (jnp.cos(angle), jnp.sin(angle))


def dot(a, b, dims):
    return lax.dot_general(a, b, ((dims[:1], dims[1:]), ((), ())), preferred_element_type=F32)


def local(
    tokens_in,
    qkv_weight,
    qkv_bias,
    out_weight,
    norm_gains,
    gate_weight,
    up_weight,
    down_weight,
    doc_ids,
    cotangent,
):
    block_index = lax.axis_index("y") * 8 + lax.axis_index("x") * 2 + lax.axis_index("zh")
    documents = doc_ids[0]
    cot_low = cotangent[0]

    small = jnp.concatenate([qkv_bias, norm_gains.reshape(-1)])[None]
    small = jnp.pad(small, ((0, 15), (0, 128 - small.shape[1])))
    units, out_rows = gate_weight.shape[0], out_weight.shape[0]
    feature = lax.broadcasted_iota(jnp.int32, (384, 512), 0)
    slot = lax.broadcasted_iota(jnp.int32, (384, 512), 1)
    spread = (slot == feature // out_rows * 16 + feature % out_rows).astype(BF)

    first_row = block_index * TOK
    my_pos = lax.dynamic_slice_in_dim(positions_of(documents), first_row, TOK, 0)
    cosine, sine = rope_tables(my_pos)
    sine = jnp.concatenate([-sine[:, : HD // 2], sine[:, HD // 2 :]], axis=1)
    first = first_row + jnp.arange(TOK, dtype=jnp.int32) - my_pos
    first = jnp.broadcast_to(jnp.tile(first, GROUP)[None], (8, GQ))

    (
        normed_one,
        gains,
        queries,
        attended,
        slots,
        lse,
        middle,
        kv,
        w_qkv,
        w_out,
        w_gate,
        w_up,
        w_down,
        cot_rows,
        rows_two,
    ) = front(
        tokens_in[0],
        cosine,
        sine,
        first,
        spread,
        small,
        out_weight,
        gate_weight,
        up_weight,
        down_weight,
        qkv_weight,
        cot_low,
    )
    w_qkv = w_qkv.reshape(2048, D)
    w_out = w_out.reshape(2048, D)
    gain_two = gains[8]
    w_gate, w_up, w_down = (w.reshape(-1, D) for w in (w_gate, w_up, w_down))
    cot_rows, rows_two = cot_rows.reshape(-1, D), rows_two.reshape(-1, D)
    factor_two = lax.rsqrt(jnp.mean(middle * middle, axis=-1, keepdims=True) + norm_eps)

    gate = dot(rows_two, w_gate, (1, 1))
    upward = dot(rows_two, w_up, (1, 1))
    hidden_grad = dot(cot_rows, w_down, (1, 1))
    sigma = jax.nn.sigmoid(gate)
    hidden = (gate * sigma * upward).astype(BF)
    gate_grad = (hidden_grad * upward * sigma * (1.0 + gate * (1.0 - sigma))).astype(BF)
    upward_grad = (hidden_grad * gate * sigma).astype(BF)
    ffn_part = dot(hidden, w_down, (1, 0)).astype(BF)
    grad_part = (dot(gate_grad, w_gate, (1, 0)) + dot(upward_grad, w_up, (1, 0))).astype(BF)
    ffn_lead = lead_of(FFN_DIMS) + (ROWS, D)
    gate_part, up_part, down_part = (
        dot(a, b, (0, 0)).astype(BF).reshape(ffn_lead)
        for a, b in ((gate_grad, rows_two), (upward_grad, rows_two), (hidden, cot_rows))
    )
    rows_lead = lead_of(ROW_DIMS) + (TOK, D)
    normed_two_grad, *down_sums = scatter_rows(grad_part.reshape(rows_lead), down_part)

    cot_full = cot_low.astype(F32)
    scaled_two = gain_two * normed_two_grad
    gain_two_grad = jnp.sum(normed_two_grad * middle * factor_two, axis=0)
    middle_grad = (
        cot_full
        + factor_two * scaled_two
        - middle * factor_two**3 * jnp.mean(scaled_two * middle, axis=-1, keepdims=True)
    )
    branch_grad = middle_grad.astype(BF)
    grad_slots = dot(branch_grad, w_out, (1, 1)).astype(BF)
    out_part = dot(slots, branch_grad, (0, 0)).astype(BF)
    lead = lead_of(AXES)
    layer_out, input_grad, qkv_sum, small_sum, out_sum, gate_sum, up_sum, down_sum, _ = back(
        (
            kv,
            queries,
            attended,
            grad_slots,
            lse,
            first,
            cosine,
            sine,
            spread,
            tokens_in[0],
            normed_one,
            gains,
            middle,
            middle_grad,
            jnp.broadcast_to(gain_two_grad[None], (8, D)),
        ),
        (gate_part, up_part, *down_sums, out_part.reshape(lead + (16, D)), ffn_part.reshape(rows_lead)),
        w_qkv,
    )
    return (
        layer_out[None],
        input_grad[None],
        qkv_sum,
        small_sum[0, :16],
        out_sum[:out_rows],
        small_sum[0, 16:40].reshape(2, 12),
        gate_sum[:units],
        up_sum[:units],
        down_sum[:units],
    )


def solution(mesh):
    fine = Mesh(mesh.devices.reshape(tuple(SIZE[a] for a in AXES)), AXES)
    dp, ctx = ("zl", "c"), ("y", "x", "zh")
    in_specs = (
        P(dp, ctx, None),
        P(AXES, None),
        P(AXES),
        P(AXES, None),
        P(None, AXES),
        P(AXES, None),
        P(AXES, None),
        P(AXES, None),
        P(dp, None),
        P(dp, ctx, None),
    )
    out_specs = (
        P(dp, ctx, None),
        P(dp, ctx, None),
        P(AXES, None),
        P(AXES),
        P(AXES, None),
        P(None, AXES),
        P(AXES, None),
        P(AXES, None),
        P(AXES, None),
    )
    return jax.shard_map(local, mesh=fine, in_specs=in_specs, out_specs=out_specs, check_vma=False)
```

```python
import math

import jax
import jax.numpy as jnp
from jax import lax
from jax.experimental import pallas as pl
from jax.experimental.pallas import tpu as pltpu
from jax.sharding import Mesh
from jax.sharding import PartitionSpec as P

H = 12
KVH = 2
HD = 128
HQ = 1536
D = 1536
TOK = 128
ROWS = 80

norm_eps = 1e-06
rope_base = 1000000.0
doc_kinds = 3

AXES = ("zl", "c", "y", "x", "zh")
SIZE = {"zl": 2, "c": 2, "y": 4, "x": 4, "zh": 2}
PARTS_OF = {"z": ("zl", "zh"), "x": ("x",), "y": ("y",), "c": ("c",), "zh": ("zh",)}
REACH = {"z": (1, 2, 3), "x": (1, 2, 3), "y": (1, 2, 3), "c": (1,), "zh": (1,)}
BF = jnp.bfloat16
F32 = jnp.float32
ANY = pl.BlockSpec(memory_space=pl.ANY)
VMEM = pl.BlockSpec(memory_space=pltpu.VMEM)


def here():
    return {a: lax.axis_index(a) for a in AXES}


def peer(me, axis, k):
    to = dict(me)
    if axis == "z":
        z = lax.rem(me["zh"] * 2 + me["zl"] + k, 4)
        to["zl"], to["zh"] = lax.rem(z, 2), lax.div(z, 2)
    else:
        to[axis] = lax.rem(me[axis] + k, SIZE[axis])
    return to


def device_id(at):
    return tuple(at[a] for a in AXES)


def place(dims, at, whole, tail=()):
    return tuple(slice(None) if d in whole else at[d] for d in dims) + tuple(tail)


class Links:
    def __init__(self, me, send, recv):
        self.me, self.send, self.recv, self.used = me, send, recv, 0

    def copy(self, src, dst, axis, k):
        i = self.used
        self.used += 1
        c = pltpu.make_async_remote_copy(
            src_ref=src,
            dst_ref=dst,
            send_sem=self.send.at[i],
            recv_sem=self.recv.at[i],
            device_id=device_id(peer(self.me, axis, k)),
            device_id_type=pl.DeviceIdType.MESH,
        )
        c.start()
        return c


def greet(me, axes):
    barrier = pltpu.get_barrier_semaphore()
    count = 0
    for axis in axes:
        for k in REACH[axis]:
            pl.semaphore_signal(
                barrier,
                inc=1,
                device_id=device_id(peer(me, axis, k)),
                device_id_type=pl.DeviceIdType.MESH,
            )
            count += 1
    pl.semaphore_wait(barrier, count)


def halves_of(tail, cols):
    rows = tail[:-1] if tail else (slice(None),)
    start = tail[-1].start if tail else 0
    cut = cols // 2
    return tuple(rows + (slice(start + cut * i, start + cut * (i + 1)),) for i in range(2))


def gather_stream(links, block, buf, dims, tail, order):
    me = links.me
    whole = ()
    cols = block.shape[-1]
    for n, axis in enumerate(order):
        direct = axis.endswith("!")
        axis = axis.rstrip("!")
        mine = place(dims, me, whole, tail)
        src = block if n == 0 else buf.at[mine]
        ring = len(REACH[axis]) == 3 and not direct
        near = (1, 3) if ring else REACH[axis]
        copies = [links.copy(src, buf.at[mine], axis, k) for k in near]
        yield
        for c in copies:
            c.wait()
        if ring:
            copies = []
            for k, half in zip(near, halves_of(tail, cols), strict=True):
                theirs = buf.at[place(dims, peer(me, axis, 4 - k), whole, half)]
                copies.append(links.copy(theirs, theirs, axis, k))
            yield
            for c in copies:
                c.wait()
        whole = whole + PARTS_OF[axis]


def run_streams(streams):
    live = list(streams)
    while live:
        live = [s for s in live if next(s, live) is not live]


def step(streams):
    for s in streams:
        next(s, None)


def count_gather(orders):
    return sum({"c": 1, "zh": 1}.get(a, 3 if "!" in a else 4) for order in orders for a in order)


def count_scatter(orders):
    return sum(4 if "~" in a else len(REACH[a]) for order in orders for a in order)


THIRDS = tuple((slice(None), slice(512 * i, 512 * (i + 1))) for i in range(3))
ORDERS = (("x", "y", "z"), ("y", "z", "x"), ("z", "x", "y"))


def cut_at(column):
    return ((slice(None), slice(0, column)), (slice(None), slice(column, D)))


HALVES = cut_at(768)
GATHER_CUTS = (1024, 768, 1024)
THIRD_ORDERS = (("y", "z"), ("z", "y"), ("z", "y"))
FFN_ORDERS = (("y", "z"), ("z", "y"))
FFN_DIMS = ("zl", "y", "zh")
ROW_DIMS = ("x", "c")
KV_DIMS = ("y", "x", "zh")


def lead_of(dims):
    return tuple(SIZE[d] for d in dims)


def rest_of(dims, axis):
    return tuple(d for d in dims if d not in PARTS_OF[axis])


def scatter_scratch(dims, order, rows, cols):
    shapes = []
    for axis in order:
        ring = axis.endswith("~")
        axis = axis.rstrip("~")
        dims = rest_of(dims, axis)
        block = lead_of(dims) + (rows, cols)
        shapes.append(pltpu.VMEM((2 if ring else len(REACH[axis]),) + block, BF))
        shapes.append(pltpu.VMEM(block, BF))
        if ring:
            shapes.append(pltpu.VMEM((2,) + lead_of(dims) + (rows, cols // 2), BF))
            shapes.append(pltpu.VMEM((2,) + block, BF))
    return shapes


def sum_blocks(own, arrived, out, lead, rows, step):
    count = 1
    for n in lead:
        count *= n
    per = rows // step
    parts = arrived.shape[0]

    def body(i, carry):
        block, row = lax.div(i, per), lax.rem(i, per)
        index = []
        for n in reversed(lead):
            index.append(lax.rem(block, n))
            block = lax.div(block, n)
        at = tuple(reversed(index)) + (pl.ds(pl.multiple_of(row * step, step), step),)
        total = own[at].astype(F32)
        for p in range(parts):
            total = total + arrived[(p,) + at].astype(F32)
        out[at] = total.astype(out.dtype)
        return carry

    lax.fori_loop(0, count * per, body, 0)


def add_blocks(total, part, lead, rows, step, cols):
    count = 1
    for n in lead:
        count *= n
    per = rows // step

    def body(i, carry):
        block, row = lax.div(i, per), lax.rem(i, per)
        index = []
        for n in reversed(lead):
            index.append(lax.rem(block, n))
            block = lax.div(block, n)
        at = tuple(reversed(index)) + (pl.ds(pl.multiple_of(row * step, step), step),)
        whole = total[at + (cols,)].astype(F32) + part[at + (slice(None),)].astype(F32)
        total[at + (cols,)] = whole.astype(BF)
        return carry

    lax.fori_loop(0, count * per, body, 0)


def scatter_stream(links, local, source, dims, tail, order, scratch, out, rows, step):
    me = links.me
    now = None
    scratch = list(scratch)
    for n, axis in enumerate(order):
        ring = axis.endswith("~")
        axis = axis.rstrip("~")
        arrived, own = scratch.pop(0), scratch.pop(0)
        gone = PARTS_OF[axis]
        keep = tuple(d for d in dims if d not in gone)
        lead = lead_of(keep)
        end = tail if n == 0 else ()
        base = source if n == 0 else now
        staged = n == 0 and local is not None
        held = base.at[place(dims, me, keep, end)]
        fetched = []

        def stage(src, dst, sem):
            fetched.append(pltpu.make_async_copy(src, dst, sem))
            fetched[-1].start()

        if ring:
            passed, onward = scratch.pop(0), scratch.pop(0)
            cut = passed.shape[-1]
            copies = []
            for i, k in enumerate((1, 3)):
                half = halves_of(end, 2 * cut)[i]
                src = base.at[place(dims, peer(me, axis, 2), keep, half)]
                copies.append(links.copy(src, passed.at[i], axis, k))
                src = base.at[place(dims, peer(me, axis, k), keep, end)]
                if staged:
                    stage(src, onward.at[i], local.at[i])
            if staged:
                stage(held, own, local.at[2])
                held = own
            yield
            for c in fetched + copies:
                c.wait()
            copies = []
            for i, k in enumerate((1, 3)):
                cols = pl.ds(cut * i, cut)
                to = onward.at[i]
                add_blocks(to, passed.at[i], lead, rows, step, cols)
                copies.append(links.copy(to, arrived.at[i], axis, k))
        else:
            copies = []
            for k in REACH[axis]:
                src = base.at[place(dims, peer(me, axis, k), keep, end)]
                copies.append(links.copy(src, arrived.at[k - 1], axis, k))
            if staged:
                stage(held, own, local)
                held = own
        yield
        for c in ([] if ring else fetched) + copies:
            c.wait()
        target = out if n == len(order) - 1 else own
        sum_blocks(held, arrived, target, lead, rows, step)
        now, dims = own, keep


FIRST_STAGE = (("y~",), ("z~",))
LAST_STAGE = (("z",), ("y",))
KV_ORDERS = (("y", "x", "zh"), ("x", "y", "zh"))
ALL_ORDERS = tuple(("c",) + o for o in ORDERS)


def rows_scatter_kernel(*refs):
    rows, tokens, cots, hidden, gate, up = refs[:6]
    out, sum_a, sum_b, gate_part, up_part = refs[6:11]
    tokens_v, cots_v, lhs, part, down, send, recv, local = refs[11:19]
    scratch = refs[19:]
    me = here()
    links = Links(me, send, recv)
    used = [0]

    def move(src, dst):
        used[0] += 1
        c = pltpu.make_async_copy(src, dst, local.at[used[0] - 1])
        c.start()
        return c

    first = [move(hidden, lhs.at[0]), move(cots, cots_v)]
    second = [move(gate, lhs.at[1]), move(tokens, tokens_v)]
    greet(me, ("x", "y", "z", "c"))
    streams = [
        scatter_stream(links, local.at[7], rows, ROW_DIMS, (), ("c", "x"), scratch[8:], out, TOK, 16)
    ]
    step(streams)

    def product(left, right, result):
        def body(i, carry):
            at = pl.ds(pl.multiple_of(i * 4 * ROWS, 4 * ROWS), 4 * ROWS)
            for j in range(3):
                cols = slice(512 * j, 512 * (j + 1))
                block = mm(left[at], right[:, cols], (1, 0)).astype(BF)
                result[lax.div(i, 2), pl.ds(lax.rem(i, 2) * 2, 2), :, :, cols] = block.reshape(
                    2, 2, ROWS, 512
                )
            return carry

        lax.fori_loop(0, 4, body, 0)

    for c in first:
        c.wait()
    product(lhs.at[0], cots_v, down)
    step(streams)
    weights = [
        scatter_stream(
            links,
            local.at[pl.ds(8 + 3 * i, 3)],
            down,
            FFN_DIMS,
            HALVES[i],
            FIRST_STAGE[i],
            scratch[4 * i : 4 * i + 4],
            (sum_a, sum_b)[i],
            ROWS,
            16,
        )
        for i in range(2)
    ]
    step(weights)
    third = move(up, lhs.at[0])
    for c in second:
        c.wait()
    product(lhs.at[1], tokens_v, part.at[0])
    stored = [move(part.at[0], gate_part)]
    step(weights)
    third.wait()
    product(lhs.at[0], tokens_v, part.at[1])
    stored.append(move(part.at[1], up_part))
    step(streams)
    step(weights)
    for c in stored:
        c.wait()


def scatter_rows(rows, tokens, cots, hidden, gate, up):
    copies = count_scatter([("c", "x")]) + count_scatter(FIRST_STAGE)
    lead = lead_of(FFN_DIMS) + (ROWS, D)
    scratch, sums = [], []
    for order in FIRST_STAGE:
        scratch += scatter_scratch(FFN_DIMS, order, ROWS, 768)
        rest = rest_of(FFN_DIMS, order[0].rstrip("~"))
        sums.append(jax.ShapeDtypeStruct(lead_of(rest) + (ROWS, 768), BF))
    part = jax.ShapeDtypeStruct(lead, BF)
    return pl.pallas_call(
        rows_scatter_kernel,
        out_shape=(jax.ShapeDtypeStruct((TOK, D), F32), *sums, part, part),
        in_specs=[ANY] * 6,
        out_specs=(VMEM,) * 3 + (ANY,) * 2,
        scratch_shapes=[
            pltpu.VMEM(tokens.shape, BF),
            pltpu.VMEM(cots.shape, BF),
            pltpu.VMEM((2,) + hidden.shape, BF),
            pltpu.VMEM((2,) + lead, BF),
            pltpu.VMEM(lead, BF),
            pltpu.SemaphoreType.DMA((copies,)),
            pltpu.SemaphoreType.DMA((copies,)),
            pltpu.SemaphoreType.DMA((14,)),
        ]
        + scratch
        + scatter_scratch(ROW_DIMS, ("c", "x"), TOK, D),
        compiler_params=pltpu.CompilerParams(
            collective_id=4, has_side_effects=True, vmem_limit_bytes=60 * 2**20
        ),
    )(rows, tokens, cots, hidden, gate, up)


GROUP = H // KVH
GQ = GROUP * TOK
KEYS = 512
SCALE = HD**-0.5
TO_LOG2 = SCALE * math.log2(math.e)


def head(h):
    return slice(128 * h, 128 * (h + 1))


def turned(v):
    return pltpu.roll(v, 64, 1)


def key_blocks():
    ctx = lax.axis_index("y") * 8 + lax.axis_index("x") * 2 + lax.axis_index("zh")
    return lax.div(ctx, 4) + 1, ctx * TOK


def key_block_of(ref, b, cols):
    return ref[lax.div(b, 2), pl.ds(lax.rem(b, 2) * 2, 2), :, :, cols].reshape(KEYS, HD)


def allowed_keys(b, first, row):
    key = b * KEYS + lax.broadcasted_iota(jnp.int32, (KEYS, GQ), 0)
    query = row + lax.rem(lax.broadcasted_iota(jnp.int32, (1, GQ), 1), TOK)
    return (key <= query) & (key >= first)


def mm(a, b, contract):
    return lax.dot_general(
        a, b, ((contract[:1], contract[1:]), ((), ())), preferred_element_type=F32
    )


def attend_all(kv, qs, first, row, blocks, acc, stats):
    acc[...] = jnp.zeros_like(acc)
    stats[:, 0:1] = jnp.full((KVH, 1, GQ), -1e30, F32)
    stats[:, 1:2] = jnp.zeros((KVH, 1, GQ), F32)

    def body(b, carry):
        allowed = allowed_keys(b, first, row)
        for g in range(KVH):
            keys = key_block_of(kv, b, head(g))
            values = key_block_of(kv, b, head(2 + g))
            raw = mm(keys, qs[g], (1, 1)) * TO_LOG2
            raw = jnp.where(allowed, raw, -1e30)
            old = stats[g, 0:1]
            top = jnp.maximum(old, jnp.max(raw, axis=0, keepdims=True))
            probs = jnp.exp2(raw - top)
            shrink = jnp.exp2(old - top)
            stats[g, 0:1] = top
            stats[g, 1:2] = stats[g, 1:2] * shrink + jnp.sum(probs, axis=0, keepdims=True)
            acc[g] = acc[g] * shrink + mm(values.T, probs.astype(BF), (1, 0))
        return carry

    lax.fori_loop(0, blocks, body, 0)


QKV_ORDERS = (("x!", "y!", "z!", "c"), ("y!", "z!", "x!", "c"), ("z!", "x!", "y!", "c"))
OUT_ORDERS = (("y!", "z!", "x", "c"), ("x!", "y!", "z", "c"))
KEY_ORDERS = (("zh", "x!", "y"), ("zh", "y!", "x"))
ROW_ORDER = ("x", "c")


def spread_row(blocks, offset, width, count):
    f = lax.broadcasted_iota(jnp.int32, (1, count), 1).astype(F32)
    block = jnp.floor((f + 0.5) * (1.0 / width))
    lane = offset + f - block * width
    index = lax.broadcasted_iota(jnp.int32, (128, count), 0).astype(F32)
    pick = (index == lane).astype(BF)
    spread = mm(blocks, pick, (1, 0))
    return jnp.sum(jnp.where(index == block, spread, 0.0), axis=0, keepdims=True)


def front_kernel(*refs):
    tokens, cosine, sine, first_ref, spread, small, out_in, gate_in, up_in, down_in = refs[:10]
    qkv_block, cot = refs[10:12]
    normed_one, gains, queries, attended, slots, lse, middle = refs[12:19]
    kv_hbm, qkv_hbm, out_hbm, gate_all, up_all, down_all, cot_all, rows_all = refs[19:27]
    small_all, w_qkv, w_out, kv, out_block, gate, up, down = refs[27:35]
    qkv, block, qs, acc, stats, normed, send, recv, local = refs[35:]
    me = here()
    links = Links(me, send, recv)
    own = []

    def keep(src, dst):
        own.append(pltpu.make_async_copy(src, dst, local.at[len(own)]))
        own[-1].start()
        return own[-1]

    first_copies = [
        keep(qkv_block, w_qkv.at[place(AXES, me, ())]),
        keep(small, small_all.at[place(AXES, me, ())]),
        keep(cot, cot_all.at[place(ROW_DIMS, me, ())]),
    ]
    out_rows = out_in.shape[0]
    out_block[0:out_rows] = out_in[...]
    out_block[out_rows:16] = jnp.zeros((16 - out_rows, D), BF)
    first_copies.append(keep(out_block, w_out.at[place(AXES, me, ())]))
    units = gate_in.shape[0]
    ffn = ((gate_in, gate, gate_all), (up_in, up, up_all), (down_in, down, down_all))
    for a, b, c in ffn:
        b[0:units] = a[...]
        b[units:ROWS] = jnp.zeros((ROWS - units, D), BF)
        first_copies.append(keep(b, c.at[place(FFN_DIMS, me, ())]))
    greet(me, ("x", "y", "z", "c", "zh"))
    qkvs = [
        gather_stream(links, qkv_block.at[tail], w_qkv, AXES, tail, order)
        for order, tail in zip(QKV_ORDERS, THIRDS, strict=True)
    ]
    qkvs.append(gather_stream(links, small, small_all, AXES, (), QKV_ORDERS[1]))
    outs = [
        gather_stream(links, out_block.at[tail], w_out, AXES, tail, order)
        for order, tail in zip(OUT_ORDERS, HALVES, strict=True)
    ]
    by_y, by_z = (
        [
            gather_stream(links, a.at[cut_at(column)[i]], b, FFN_DIMS, cut_at(column)[i], order)
            for (_, a, b), column in zip(ffn, GATHER_CUTS, strict=True)
        ]
        for i, order in enumerate(FFN_ORDERS)
    )
    cots = [gather_stream(links, cot, cot_all, ROW_DIMS, (), ROW_ORDER)]
    step(qkvs)
    step(outs)
    whole = tokens[...].astype(F32)
    factor = lax.rsqrt(jnp.sum(whole * whole, axis=1, keepdims=True) / D + norm_eps)
    for c in first_copies:
        c.wait()
    step(qkvs)
    step(outs)
    step(qkvs)
    step(qkvs)
    step(by_y)
    step(outs)
    step(qkvs)
    saved = [keep(w_qkv, qkv_hbm)]
    row = lax.broadcasted_iota(jnp.int32, (128, 2048), 0)
    entry = lax.broadcasted_iota(jnp.int32, (128, 2048), 1)
    blocks = mm((entry == row * 16).astype(BF), small_all[...].reshape(2048, 128), (1, 0)).astype(BF)
    bias = spread_row(blocks, 0, 16, 2048)
    gain = spread_row(blocks, 16, 12, D)
    gains[0:8] = jnp.broadcast_to(gain, (8, D))
    gain_two = spread_row(blocks, 28, 12, D)
    gains[8:16] = jnp.broadcast_to(gain_two, (8, D))
    normed_one[...] = (tokens[...].astype(F32) * factor * gain).astype(BF)
    cos, sin = cosine[...], sine[...]

    def project(j):
        part = w_qkv[j // 4, (j // 2) % 2, 2 * (j % 2) : 2 * (j % 2) + 2].reshape(256, D)
        return mm(normed_one[...], part, (1, 1)) + bias[:, 256 * j : 256 * (j + 1)]

    part = project(6)
    for g in range(KVH):
        one = part[:, head(g)]
        block[:, head(g)] = (one * cos + turned(one) * sin).astype(BF)
    block[:, 256:512] = project(7).astype(BF)
    mine = keep(block, kv.at[place(KV_DIMS, me, ())])
    keys = []
    for half, order in enumerate(KEY_ORDERS):
        tail = (slice(None), slice(256 * half, 256 * (half + 1)))
        keys.append(gather_stream(links, block.at[tail], kv, KV_DIMS, tail, order))
    step(keys)
    step(by_y)
    step(outs)
    step(by_z)
    mine.wait()
    for j in range(3):
        qkv[:, 256 * j : 256 * (j + 1)] = project(j)
    step(keys)
    for j in range(3, 6):
        qkv[:, 256 * j : 256 * (j + 1)] = project(j)
    step(by_z)
    step(by_y)
    step(keys)
    step(outs)
    for h in range(H):
        one = qkv[:, head(h)]
        rotated = (one * cos + turned(one) * sin).astype(BF)
        queries[:, head(h)] = rotated
        qs[h // GROUP, (h % GROUP) * TOK : (h % GROUP + 1) * TOK, :] = rotated
    step(keys)
    step(keys)
    step(by_z)
    step(cots)
    saved.append(keep(kv, kv_hbm))
    count, start = key_blocks()
    first = first_ref[0:1]
    attend_all(kv, qs, first, start, count, acc, stats)
    for g in range(KVH):
        total = stats[g, 1:2]
        lse[g] = jnp.broadcast_to(stats[g, 0:1] + jnp.log2(total), (8, GQ))
        for i in range(GROUP):
            attended[:, head(GROUP * g + i)] = (acc[g, :, head(i)] / total[:, head(i)]).T
    step(cots)
    for i in range(4):
        part = attended[:, 384 * i : 384 * (i + 1)].astype(BF)
        slots[:, 512 * i : 512 * (i + 1)] = mm(part, spread[...], (1, 0)).astype(BF)
    step(outs)
    saved.append(keep(w_out, out_hbm))
    square = jnp.zeros((TOK, 1), F32)
    for i in range(3):
        cols = slice(512 * i, 512 * (i + 1))
        part = w_out[:, :, :, :, :, :, cols].reshape(2048, 512)
        part = tokens[:, cols].astype(F32) + mm(slots[...], part, (1, 0))
        middle[:, cols] = part
        square = square + jnp.sum(part * part, axis=1, keepdims=True)
    factor = lax.rsqrt(square / D + norm_eps)
    normed[...] = (middle[...] * factor * gains[8:9]).astype(BF)
    mine = keep(normed, rows_all.at[place(ROW_DIMS, me, ())])
    rows = [gather_stream(links, normed, rows_all, ROW_DIMS, (), ROW_ORDER)]
    step(rows)
    step(by_y)
    step(by_z)
    step(cots)
    mine.wait()
    step(rows)
    step(rows)
    step(cots)
    step(rows)
    step(by_y)
    step(by_z)
    for c in saved:
        c.wait()


def front(tokens, cosine, sine, first, spread, small, out_weight, gate, up, down, qkv_weight, cot):
    every = lead_of(AXES) + (16, D)
    kv = lead_of(KV_DIMS) + (TOK, 512)
    ffn = jax.ShapeDtypeStruct(lead_of(FFN_DIMS) + (ROWS, D), BF)
    rows = jax.ShapeDtypeStruct(lead_of(ROW_DIMS) + (TOK, D), BF)
    copies = count_gather(QKV_ORDERS + QKV_ORDERS[:1] + OUT_ORDERS + (ROW_ORDER, ROW_ORDER))
    copies += count_gather(KEY_ORDERS + 3 * FFN_ORDERS)
    return pl.pallas_call(
        front_kernel,
        out_shape=(
            jax.ShapeDtypeStruct((TOK, D), BF),
            jax.ShapeDtypeStruct((16, D), F32),
            jax.ShapeDtypeStruct((TOK, HQ), BF),
            jax.ShapeDtypeStruct((TOK, HQ), F32),
            jax.ShapeDtypeStruct((TOK, 2048), BF),
            jax.ShapeDtypeStruct((KVH, 8, GQ), F32),
            jax.ShapeDtypeStruct((TOK, D), F32),
            jax.ShapeDtypeStruct(kv, BF),
            jax.ShapeDtypeStruct(every, BF),
            jax.ShapeDtypeStruct(every, BF),
            ffn,
            ffn,
            ffn,
            rows,
            rows,
        ),
        in_specs=[VMEM] * 10 + [ANY] * 2,
        out_specs=(VMEM,) * 7 + (ANY,) * 8,
        scratch_shapes=[
            pltpu.VMEM(lead_of(AXES) + (16, 128), BF),
            pltpu.VMEM(every, BF),
            pltpu.VMEM(every, BF),
            pltpu.VMEM(kv, BF),
            pltpu.VMEM((16, D), BF),
            pltpu.VMEM((ROWS, D), BF),
            pltpu.VMEM((ROWS, D), BF),
            pltpu.VMEM((ROWS, D), BF),
            pltpu.VMEM((TOK, HQ), F32),
            pltpu.VMEM((TOK, 512), BF),
            pltpu.VMEM((KVH, GQ, HD), BF),
            pltpu.VMEM((KVH, HD, GQ), F32),
            pltpu.VMEM((KVH, 8, GQ), F32),
            pltpu.VMEM((TOK, D), BF),
            pltpu.SemaphoreType.DMA((copies,)),
            pltpu.SemaphoreType.DMA((copies,)),
            pltpu.SemaphoreType.DMA((12,)),
        ],
        compiler_params=pltpu.CompilerParams(
            collective_id=2, has_side_effects=True, vmem_limit_bytes=56 * 2**20
        ),
    )(tokens, cosine, sine, first, spread, small, out_weight, gate, up, down, qkv_weight, cot)


def grad_all(kv, qs, gs, lse, delta, first, row, blocks, query_grad, kv_grad):
    query_grad[...] = jnp.zeros_like(query_grad)

    def body(b, carry):
        at = (lax.div(b, 2), pl.ds(lax.rem(b, 2) * 2, 2), slice(None), slice(None))
        allowed = allowed_keys(b, first, row)
        for g in range(KVH):
            keys = key_block_of(kv, b, head(g))
            values = key_block_of(kv, b, head(2 + g))
            raw = mm(keys, qs[g], (1, 1)) * TO_LOG2
            probs = jnp.where(allowed, jnp.exp2(raw - lse[g, 0:1]), 0.0)
            prob_grad = mm(values, gs[g], (1, 1))
            score_grad = (probs * (prob_grad - delta[g : g + 1])).astype(BF)
            key_term = mm(score_grad, qs[g], (1, 0)) * SCALE
            value_term = mm(probs.astype(BF), gs[g], (1, 0))
            kv_grad[at + (head(g),)] = key_term.astype(BF).reshape(2, 2, TOK, HD)
            kv_grad[at + (head(2 + g),)] = value_term.astype(BF).reshape(2, 2, TOK, HD)
            query_grad[g] += mm(keys.T, score_grad, (1, 0))
        return carry

    lax.fori_loop(0, blocks, body, 0)


def collect_row(row, offset, width):
    count = row.shape[1]
    f = lax.broadcasted_iota(jnp.int32, (1, count), 1).astype(F32)
    block = jnp.floor((f + 0.5) * (1.0 / width))
    lane = offset + f - block * width
    index = lax.broadcasted_iota(jnp.int32, (128, count), 0).astype(F32)
    spread = jnp.where(index == block, row, 0.0).astype(BF)
    return mm(spread, (index == lane).astype(BF), (1, 1))


def back_kernel(*refs):
    kv, queries, attended, grad_slots, lse, first_ref, cosine, sine, spread = refs[:9]
    tokens, normed_one, gains, middle, middle_grad, gain_two_grad = refs[9:15]
    gate_part, up_part, down_a, down_b, out_part, ffn_rows, w_qkv = refs[15:22]
    layer_out, input_grad, qkv_out, small_out, out_out, gate_out, up_out, down_out = refs[22:30]
    qkv_part = refs[30]
    qs, gs, delta, query_grad, kv_grad, kv_out, qkv_grad, weight, staged = refs[31:40]
    small, ffn_total, free, send, recv, local = refs[40:46]
    scratch = list(refs[46:])
    total = input_grad

    def take(n):
        return [scratch.pop(0) for _ in range(n)]

    me = here()
    links = Links(me, send, recv)
    used = [0]

    def slot():
        used[0] += 1
        return local.at[used[0] - 1]

    def fetch(j):
        c = pltpu.make_async_copy(w_qkv.at[pl.ds(512 * j, 512)], weight.at[j % 2], slot())
        c.start()
        return c

    fetched = [fetch(0), fetch(1)]
    greet(me, ("zh", "x", "y", "z", "c"))
    shared = [take(8) for _ in THIRDS]
    outs = [
        scatter_stream(links, slot(), out_part, AXES, tail, order, part, out_out.at[tail], 16, 16)
        for order, tail, part in zip(ALL_ORDERS, THIRDS, shared, strict=True)
    ]
    rows = [
        scatter_stream(
            links, slot(), ffn_rows, ROW_DIMS, (), ("c", "x"), take(4), ffn_total, TOK, 16
        )
    ]
    gates, ups = (
        [
            scatter_stream(
                links, slot(), source, FFN_DIMS, tail, order, take(4), target.at[tail], ROWS, 16
            )
            for order, tail in zip(THIRD_ORDERS, THIRDS, strict=True)
        ]
        for source, target in ((gate_part, gate_out), (up_part, up_out))
    )
    downs = [
        scatter_stream(
            links,
            slot(),
            source,
            rest_of(FFN_DIMS, order[0]),
            (),
            order[1:],
            take(2),
            down_out.at[tail],
            ROWS,
            16,
        )
        for source, order, tail in zip((down_a, down_b), FFN_ORDERS, HALVES, strict=True)
    ]
    step(outs)
    step(rows)
    step(downs)
    step(gates)
    blocks, row = key_blocks()
    first = first_ref[0:1]
    for i in range(4):
        part = mm(grad_slots[:, 512 * i : 512 * (i + 1)], spread[...], (1, 1))
        for j in range(3):
            h = 3 * i + j
            one = part[:, head(j)]
            gs[h // GROUP, (h % GROUP) * TOK : (h % GROUP + 1) * TOK, :] = one.astype(BF)
            both = (one * attended[:, head(h)]).T
            delta[h // GROUP : h // GROUP + 1, head(h % GROUP)] = jnp.sum(
                both, axis=0, keepdims=True
            )
            qs[h // GROUP, (h % GROUP) * TOK : (h % GROUP + 1) * TOK, :] = queries[:, head(h)]

    def clear(b, carry):
        at = (lax.div(b, 2), pl.ds(lax.rem(b, 2) * 2, 2))
        kv_grad[at] = jnp.zeros((2, 2, TOK, 512), BF)
        return carry

    lax.fori_loop(blocks, 8, clear, 0)
    step(outs)
    step(rows)
    cos, sin = cosine[...], sine[...]
    grad_all(kv, qs, gs, lse, delta, first, row, blocks, query_grad, kv_grad)
    keys = []
    for half, order in enumerate(KV_ORDERS):
        tail = (slice(None), slice(256 * half, 256 * (half + 1)))
        keys.append(
            scatter_stream(
                links, None, kv_grad, KV_DIMS, tail, order, take(6), kv_out.at[half], TOK, 32
            )
        )
    step(keys)
    for g in range(KVH):
        for i in range(GROUP):
            one = query_grad[g, :, head(i)].T * SCALE
            qkv_grad[:, head(GROUP * g + i)] = (one * cos - turned(one) * sin).astype(BF)
    step(outs)
    step(ups[1:2])
    stored = []

    def weight_terms(j):
        if j >= 2:
            fetched.append(fetch(j))
            stored[j - 2].wait()
        part = qkv_grad[:, 512 * j : 512 * (j + 1)]
        lhs = jnp.concatenate(
            [part[:, head(i)].astype(F32).T.astype(BF) for i in range(4)], axis=0
        )
        for i in range(3):
            cols = slice(512 * i, 512 * (i + 1))
            grad = mm(lhs, normed_one[:, cols], (1, 0)).astype(BF)
            staged[j % 2, :, :, :, :, cols] = grad.reshape(4, 4, 2, 16, 512)
        c = pltpu.make_async_copy(staged.at[j % 2], qkv_part.at[j // 2, j % 2], slot())
        c.start()
        stored.append(c)
        fetched[j].wait()
        for i in range(3):
            cols = slice(512 * i, 512 * (i + 1))
            term = mm(part, weight[j % 2, :, cols], (1, 0))
            if j == 0:
                total[:, cols] = term
            else:
                total[:, cols] += term

    weight_terms(0)
    weight_terms(1)
    weight_terms(2)
    step(keys)
    step(outs)
    step(keys)
    step(gates)
    step(ups[:1])
    step(ups[2:])
    step(outs)
    for axis in ("c", "x", "y", "z"):
        for k in REACH[axis]:
            pl.semaphore_signal(
                free,
                inc=1,
                device_id=device_id(peer(me, axis, k)),
                device_id_type=pl.DeviceIdType.MESH,
            )
    step(keys)
    for g in range(KVH):
        one = kv_out[0, :, head(g)]
        qkv_grad[:, head(H + g)] = (one * cos - turned(one) * sin).astype(BF)
        qkv_grad[:, head(H + 2 + g)] = kv_out[1, :, head(g)].astype(BF)
    weight_terms(3)
    for c in stored[2:]:
        c.wait()
    pl.semaphore_wait(free, 10)
    qkvs = [
        scatter_stream(links, slot(), qkv_part, AXES, tail, order, part, qkv_out.at[tail], 16, 16)
        for order, tail, part in zip(ALL_ORDERS, THIRDS, shared, strict=True)
    ]
    step(qkvs)
    whole = tokens[...].astype(F32)
    factor = lax.rsqrt(jnp.sum(whole * whole, axis=1, keepdims=True) / D + norm_eps)
    grad = total[...]
    gain_one_grad = jnp.sum(grad * whole * factor, axis=0, keepdims=True)
    bias_grad = jnp.sum(qkv_grad[...].astype(F32), axis=0, keepdims=True)
    blocks_grad = collect_row(bias_grad, 0, 16)
    blocks_grad = blocks_grad + collect_row(gain_one_grad, 16, 12)
    blocks_grad = blocks_grad + collect_row(gain_two_grad[0:1], 28, 12)
    blocks_grad = jnp.broadcast_to(blocks_grad[:, None, :], (128, 16, 128)).astype(BF)
    small[...] = blocks_grad.reshape(lead_of(AXES) + (16, 128))
    smalls = [
        scatter_stream(links, None, small, AXES, (), ALL_ORDERS[0], take(8), small_out, 16, 16)
    ]
    step(smalls)
    step(qkvs)
    step(smalls)
    scaled = grad * gains[0:1]
    mean = jnp.sum(scaled * whole, axis=1, keepdims=True) / D
    input_grad[...] = middle_grad[...] + factor * scaled - whole * (factor * factor * factor * mean)
    step(rows)
    layer_out[...] = (middle[...] + ffn_total[...]).astype(BF)
    step(downs)
    step(gates)
    step(qkvs)
    step(smalls)
    step(ups)
    step(qkvs)
    step(smalls)
    step(qkvs)
    step(smalls)
    step(ups)


def back(inputs, parts, w_qkv):
    copies = count_scatter(KV_ORDERS) + 2 * count_scatter(ALL_ORDERS)
    copies += count_scatter(ALL_ORDERS[:1]) + count_scatter([("c", "x")])
    copies += 2 * count_scatter(THIRD_ORDERS) + count_scatter(LAST_STAGE)
    every = lead_of(AXES) + (16, D)
    scratch = []
    for order in ALL_ORDERS:
        scratch += scatter_scratch(AXES, order, 16, 512)
    scratch += scatter_scratch(ROW_DIMS, ("c", "x"), TOK, D)
    for _ in range(2):
        for order in THIRD_ORDERS:
            scratch += scatter_scratch(FFN_DIMS, order, ROWS, 512)
    for order in FFN_ORDERS:
        scratch += scatter_scratch(rest_of(FFN_DIMS, order[0]), order[1:], ROWS, 768)
    for order in KV_ORDERS:
        scratch += scatter_scratch(KV_DIMS, order, TOK, 256)
    scratch += scatter_scratch(AXES, ALL_ORDERS[0], 16, 128)
    attn = jax.ShapeDtypeStruct((16, D), F32)
    ffn = jax.ShapeDtypeStruct((ROWS, D), F32)
    return pl.pallas_call(
        back_kernel,
        out_shape=(
            jax.ShapeDtypeStruct((TOK, D), BF),
            jax.ShapeDtypeStruct((TOK, D), F32),
            attn,
            jax.ShapeDtypeStruct((16, 128), F32),
            attn,
            ffn,
            ffn,
            ffn,
            jax.ShapeDtypeStruct(every, BF),
        ),
        in_specs=[VMEM] * 15 + [ANY] * 7,
        out_specs=(VMEM,) * 8 + (ANY,),
        scratch_shapes=[
            pltpu.VMEM((KVH, GQ, HD), BF),
            pltpu.VMEM((KVH, GQ, HD), BF),
            pltpu.VMEM((8, GQ), F32),
            pltpu.VMEM((KVH, HD, GQ), F32),
            pltpu.VMEM(lead_of(KV_DIMS) + (TOK, 512), BF),
            pltpu.VMEM((2, TOK, 256), F32),
            pltpu.VMEM((TOK, 2048), BF),
            pltpu.VMEM((2, 512, D), BF),
            pltpu.VMEM((2, 4, 4, 2, 16, D), BF),
            pltpu.VMEM(lead_of(AXES) + (16, 128), BF),
            pltpu.VMEM((TOK, D), F32),
            pltpu.SemaphoreType.REGULAR,
            pltpu.SemaphoreType.DMA((copies,)),
            pltpu.SemaphoreType.DMA((copies,)),
            pltpu.SemaphoreType.DMA((38,)),
        ]
        + scratch,
        compiler_params=pltpu.CompilerParams(
            collective_id=5, has_side_effects=True, vmem_limit_bytes=63 * 2**20
        ),
    )(*inputs, *parts, w_qkv)


def positions_of(documents):
    index = jnp.arange(documents.shape[0], dtype=jnp.int32)
    kinds = jnp.arange(doc_kinds, dtype=jnp.int32)
    counts = jnp.sum((documents[None, :] == kinds[:, None]).astype(jnp.int32), axis=1)
    starts = jnp.cumsum(counts) - counts
    first = jnp.sum(jnp.where(documents[:, None] == kinds[None, :], starts[None, :], 0), axis=1)
    return index - first


def rope_tables(position):
    half = HD // 2
    inverse = rope_base ** (-(jnp.arange(half, dtype=jnp.float32) * 2.0 / HD))
    angle = position.astype(jnp.float32)[:, None] * inverse[None, :]
    angle = jnp.concatenate([angle, angle], axis=1)
    return (jnp.cos(angle), jnp.sin(angle))


def dot(a, b, dims):
    return lax.dot_general(a, b, ((dims[:1], dims[1:]), ((), ())), preferred_element_type=F32)


def local(
    tokens_in,
    qkv_weight,
    qkv_bias,
    out_weight,
    norm_gains,
    gate_weight,
    up_weight,
    down_weight,
    doc_ids,
    cotangent,
):
    block_index = lax.axis_index("y") * 8 + lax.axis_index("x") * 2 + lax.axis_index("zh")
    documents = doc_ids[0]
    cot_low = cotangent[0]

    small = jnp.concatenate([qkv_bias, norm_gains.reshape(-1)])[None]
    small = jnp.pad(small, ((0, 15), (0, 128 - small.shape[1])))
    units, out_rows = gate_weight.shape[0], out_weight.shape[0]
    feature = lax.broadcasted_iota(jnp.int32, (384, 512), 0)
    slot = lax.broadcasted_iota(jnp.int32, (384, 512), 1)
    spread = (slot == feature // out_rows * 16 + feature % out_rows).astype(BF)

    first_row = block_index * TOK
    my_pos = lax.dynamic_slice_in_dim(positions_of(documents), first_row, TOK, 0)
    cosine, sine = rope_tables(my_pos)
    sine = jnp.concatenate([-sine[:, : HD // 2], sine[:, HD // 2 :]], axis=1)
    first = first_row + jnp.arange(TOK, dtype=jnp.int32) - my_pos
    first = jnp.broadcast_to(jnp.tile(first, GROUP)[None], (8, GQ))

    (
        normed_one,
        gains,
        queries,
        attended,
        slots,
        lse,
        middle,
        kv,
        w_qkv,
        w_out,
        w_gate,
        w_up,
        w_down,
        cot_rows,
        rows_two,
    ) = front(
        tokens_in[0],
        cosine,
        sine,
        first,
        spread,
        small,
        out_weight,
        gate_weight,
        up_weight,
        down_weight,
        qkv_weight,
        cot_low,
    )
    w_qkv = w_qkv.reshape(2048, D)
    w_out = w_out.reshape(2048, D)
    gain_two = gains[8]
    w_gate, w_up, w_down = (w.reshape(-1, D) for w in (w_gate, w_up, w_down))
    cot_rows, rows_two = cot_rows.reshape(-1, D), rows_two.reshape(-1, D)
    factor_two = lax.rsqrt(jnp.mean(middle * middle, axis=-1, keepdims=True) + norm_eps)

    gate = dot(w_gate, rows_two, (1, 1))
    upward = dot(w_up, rows_two, (1, 1))
    hidden_grad = dot(w_down, cot_rows, (1, 1))
    sigma = jax.nn.sigmoid(gate)
    hidden = (gate * sigma * upward).astype(BF)
    gate_grad = (hidden_grad * upward * sigma * (1.0 + gate * (1.0 - sigma))).astype(BF)
    upward_grad = (hidden_grad * gate * sigma).astype(BF)
    ffn_part = dot(hidden, w_down, (0, 0)).astype(BF)
    grad_part = (dot(gate_grad, w_gate, (0, 0)) + dot(upward_grad, w_up, (0, 0))).astype(BF)
    rows_lead = lead_of(ROW_DIMS) + (TOK, D)
    normed_two_grad, *down_sums, gate_part, up_part = scatter_rows(
        grad_part.reshape(rows_lead), rows_two, cot_rows, hidden, gate_grad, upward_grad
    )

    cot_full = cot_low.astype(F32)
    scaled_two = gain_two * normed_two_grad
    gain_two_grad = jnp.sum(normed_two_grad * middle * factor_two, axis=0)
    middle_grad = (
        cot_full
        + factor_two * scaled_two
        - middle * factor_two**3 * jnp.mean(scaled_two * middle, axis=-1, keepdims=True)
    )
    branch_grad = middle_grad.astype(BF)
    grad_slots = dot(branch_grad, w_out, (1, 1)).astype(BF)
    out_part = dot(slots, branch_grad, (0, 0)).astype(BF)
    lead = lead_of(AXES)
    layer_out, input_grad, qkv_sum, small_sum, out_sum, gate_sum, up_sum, down_sum, _ = back(
        (
            kv,
            queries,
            attended,
            grad_slots,
            lse,
            first,
            cosine,
            sine,
            spread,
            tokens_in[0],
            normed_one,
            gains,
            middle,
            middle_grad,
            jnp.broadcast_to(gain_two_grad[None], (8, D)),
        ),
        (gate_part, up_part, *down_sums, out_part.reshape(lead + (16, D)), ffn_part.reshape(rows_lead)),
        w_qkv,
    )
    return (
        layer_out[None],
        input_grad[None],
        qkv_sum,
        small_sum[0, :16],
        out_sum[:out_rows],
        small_sum[0, 16:40].reshape(2, 12),
        gate_sum[:units],
        up_sum[:units],
        down_sum[:units],
    )


def solution(mesh):
    fine = Mesh(mesh.devices.reshape(tuple(SIZE[a] for a in AXES)), AXES)
    dp, ctx = ("zl", "c"), ("y", "x", "zh")
    in_specs = (
        P(dp, ctx, None),
        P(AXES, None),
        P(AXES),
        P(AXES, None),
        P(None, AXES),
        P(AXES, None),
        P(AXES, None),
        P(AXES, None),
        P(dp, None),
        P(dp, ctx, None),
    )
    out_specs = (
        P(dp, ctx, None),
        P(dp, ctx, None),
        P(AXES, None),
        P(AXES),
        P(AXES, None),
        P(None, AXES),
        P(AXES, None),
        P(AXES, None),
        P(AXES, None),
    )
    return jax.shard_map(local, mesh=fine, in_specs=in_specs, out_specs=out_specs, check_vma=False)
```

```python
import math

import jax
import jax.numpy as jnp
from jax import lax
from jax.experimental import pallas as pl
from jax.experimental.pallas import tpu as pltpu
from jax.sharding import Mesh
from jax.sharding import PartitionSpec as P

H = 12
KVH = 2
HD = 128
HQ = 1536
D = 1536
TOK = 128
ROWS = 80

norm_eps = 1e-06
rope_base = 1000000.0
doc_kinds = 3

AXES = ("zl", "c", "y", "x", "zh")
SIZE = {"zl": 2, "c": 2, "y": 4, "x": 4, "zh": 2}
PARTS_OF = {"z": ("zl", "zh"), "x": ("x",), "y": ("y",), "c": ("c",), "zh": ("zh",)}
REACH = {"z": (1, 2, 3), "x": (1, 2, 3), "y": (1, 2, 3), "c": (1,), "zh": (1,)}
BF = jnp.bfloat16
F32 = jnp.float32
ANY = pl.BlockSpec(memory_space=pl.ANY)
VMEM = pl.BlockSpec(memory_space=pltpu.VMEM)


def here():
    return {a: lax.axis_index(a) for a in AXES}


def peer(me, axis, k):
    to = dict(me)
    if axis == "z":
        z = lax.rem(me["zh"] * 2 + me["zl"] + k, 4)
        to["zl"], to["zh"] = lax.rem(z, 2), lax.div(z, 2)
    else:
        to[axis] = lax.rem(me[axis] + k, SIZE[axis])
    return to


def device_id(at):
    return tuple(at[a] for a in AXES)


def place(dims, at, whole, tail=()):
    return tuple(slice(None) if d in whole else at[d] for d in dims) + tuple(tail)


class Links:
    def __init__(self, me, send, recv):
        self.me, self.send, self.recv, self.used = me, send, recv, 0

    def copy(self, src, dst, axis, k):
        i = self.used
        self.used += 1
        c = pltpu.make_async_remote_copy(
            src_ref=src,
            dst_ref=dst,
            send_sem=self.send.at[i],
            recv_sem=self.recv.at[i],
            device_id=device_id(peer(self.me, axis, k)),
            device_id_type=pl.DeviceIdType.MESH,
        )
        c.start()
        return c


def greet(me, axes):
    barrier = pltpu.get_barrier_semaphore()
    count = 0
    for axis in axes:
        for k in REACH[axis]:
            pl.semaphore_signal(
                barrier,
                inc=1,
                device_id=device_id(peer(me, axis, k)),
                device_id_type=pl.DeviceIdType.MESH,
            )
            count += 1
    pl.semaphore_wait(barrier, count)


def halves_of(tail, cols):
    rows = tail[:-1] if tail else (slice(None),)
    start = tail[-1].start if tail else 0
    cut = cols // 2
    return tuple(rows + (slice(start + cut * i, start + cut * (i + 1)),) for i in range(2))


def gather_stream(links, block, buf, dims, tail, order):
    me = links.me
    whole = ()
    cols = block.shape[-1]
    for n, axis in enumerate(order):
        direct = axis.endswith("!")
        axis = axis.rstrip("!")
        mine = place(dims, me, whole, tail)
        src = block if n == 0 else buf.at[mine]
        ring = len(REACH[axis]) == 3 and not direct
        near = (1, 3) if ring else REACH[axis]
        copies = [links.copy(src, buf.at[mine], axis, k) for k in near]
        yield
        for c in copies:
            c.wait()
        if ring:
            copies = []
            for k, half in zip(near, halves_of(tail, cols), strict=True):
                theirs = buf.at[place(dims, peer(me, axis, 4 - k), whole, half)]
                copies.append(links.copy(theirs, theirs, axis, k))
            yield
            for c in copies:
                c.wait()
        whole = whole + PARTS_OF[axis]


def run_streams(streams):
    live = list(streams)
    while live:
        live = [s for s in live if next(s, live) is not live]


def step(streams):
    for s in streams:
        next(s, None)


def count_gather(orders):
    return sum({"c": 1, "zh": 1}.get(a, 3 if "!" in a else 4) for order in orders for a in order)


def count_scatter(orders):
    return sum(4 if "~" in a else len(REACH[a]) for order in orders for a in order)


THIRDS = tuple((slice(None), slice(512 * i, 512 * (i + 1))) for i in range(3))
ORDERS = (("x", "y", "z"), ("y", "z", "x"), ("z", "x", "y"))


def cut_at(column):
    return ((slice(None), slice(0, column)), (slice(None), slice(column, D)))


HALVES = cut_at(768)
GATHER_CUTS = (1024, 768, 1024)
THIRD_ORDERS = (("y", "z"), ("z", "y"), ("z", "y"))
FFN_ORDERS = (("y", "z"), ("z", "y"))
FFN_DIMS = ("zl", "y", "zh")
ROW_DIMS = ("x", "c")
KV_DIMS = ("y", "x", "zh")


def lead_of(dims):
    return tuple(SIZE[d] for d in dims)


def rest_of(dims, axis):
    return tuple(d for d in dims if d not in PARTS_OF[axis])


def scatter_scratch(dims, order, rows, cols):
    shapes = []
    for axis in order:
        ring = axis.endswith("~")
        axis = axis.rstrip("~")
        dims = rest_of(dims, axis)
        block = lead_of(dims) + (rows, cols)
        shapes.append(pltpu.VMEM((2 if ring else len(REACH[axis]),) + block, BF))
        shapes.append(pltpu.VMEM(block, BF))
        if ring:
            shapes.append(pltpu.VMEM((2,) + lead_of(dims) + (rows, cols // 2), BF))
            shapes.append(pltpu.VMEM((2,) + block, BF))
    return shapes


def block_index(i, lead, rows, step):
    per = rows // step
    block, row = lax.div(i, per), lax.rem(i, per)
    fine = lead[-1:] == (2,)
    index = []
    for n in reversed(lead[:-1] if fine else lead):
        index.append(lax.rem(block, n))
        block = lax.div(block, n)
    at = tuple(reversed(index)) + ((slice(None),) if fine else ())
    return at + (pl.ds(pl.multiple_of(row * step, step), step),)


def step_count(lead, rows, step):
    count = rows // step
    for n in lead[:-1] if lead[-1:] == (2,) else lead:
        count *= n
    return count


def sum_blocks(own, arrived, out, lead, rows, step):
    parts = arrived.shape[0]

    def body(i, carry):
        at = block_index(i, lead, rows, step)
        total = own[at].astype(F32)
        for p in range(parts):
            total = total + arrived[(p,) + at].astype(F32)
        out[at] = total.astype(out.dtype)
        return carry

    lax.fori_loop(0, step_count(lead, rows, step), body, 0)


def add_blocks(total, part, lead, rows, step, cols):
    def body(i, carry):
        at = block_index(i, lead, rows, step)
        whole = total[at + (cols,)].astype(F32) + part[at + (slice(None),)].astype(F32)
        total[at + (cols,)] = whole.astype(BF)
        return carry

    lax.fori_loop(0, step_count(lead, rows, step), body, 0)


def scatter_stream(links, local, source, dims, tail, order, scratch, out, rows, step):
    me = links.me
    now = None
    scratch = list(scratch)
    for n, axis in enumerate(order):
        ring = axis.endswith("~")
        axis = axis.rstrip("~")
        arrived, own = scratch.pop(0), scratch.pop(0)
        gone = PARTS_OF[axis]
        keep = tuple(d for d in dims if d not in gone)
        lead = lead_of(keep)
        end = tail if n == 0 else ()
        base = source if n == 0 else now
        staged = n == 0 and local is not None
        held = base.at[place(dims, me, keep, end)]
        fetched = []

        def stage(src, dst, sem):
            fetched.append(pltpu.make_async_copy(src, dst, sem))
            fetched[-1].start()

        if ring:
            passed, onward = scratch.pop(0), scratch.pop(0)
            cut = passed.shape[-1]
            copies = []
            for i, k in enumerate((1, 3)):
                half = halves_of(end, 2 * cut)[i]
                src = base.at[place(dims, peer(me, axis, 2), keep, half)]
                copies.append(links.copy(src, passed.at[i], axis, k))
                src = base.at[place(dims, peer(me, axis, k), keep, end)]
                if staged:
                    stage(src, onward.at[i], local.at[i])
            if staged:
                stage(held, own, local.at[2])
                held = own
            yield
            for c in fetched + copies:
                c.wait()
            copies = []
            for i, k in enumerate((1, 3)):
                cols = pl.ds(cut * i, cut)
                to = onward.at[i]
                add_blocks(to, passed.at[i], lead, rows, step, cols)
                copies.append(links.copy(to, arrived.at[i], axis, k))
        else:
            copies = []
            for k in REACH[axis]:
                src = base.at[place(dims, peer(me, axis, k), keep, end)]
                copies.append(links.copy(src, arrived.at[k - 1], axis, k))
            if staged:
                stage(held, own, local)
                held = own
        yield
        for c in ([] if ring else fetched) + copies:
            c.wait()
        target = out if n == len(order) - 1 else own
        sum_blocks(held, arrived, target, lead, rows, step)
        now, dims = own, keep


FIRST_STAGE = (("y~",), ("z~",))
LAST_STAGE = (("z",), ("y",))
KV_ORDERS = (("y", "x", "zh"), ("x", "y", "zh"))
ALL_ORDERS = tuple(("c",) + o for o in ORDERS)


def rows_scatter_kernel(*refs):
    middle, cot, gains, slots = refs[:4]
    rows, tokens, cots, hidden, gate, up, w_out = refs[4:11]
    middle_grad, gain_two_grad, grad_slots, sum_a, sum_b = refs[11:16]
    gate_part, up_part, out_part = refs[16:19]
    out, weight, tokens_v, cots_v, lhs, part, down, out_v, send, recv, local = refs[19:30]
    scratch = refs[30:]
    me = here()
    links = Links(me, send, recv)
    used = [0]

    def move(src, dst):
        used[0] += 1
        c = pltpu.make_async_copy(src, dst, local.at[used[0] - 1])
        c.start()
        return c

    first = [move(hidden, lhs.at[0]), move(cots, cots_v)]
    second = [move(gate, lhs.at[1]), move(tokens, tokens_v)]
    fetched = move(w_out, weight)
    greet(me, ("x", "y", "z", "c"))
    streams = [
        scatter_stream(links, local.at[20], rows, ROW_DIMS, (), ("c", "x"), scratch[8:], out, TOK, 16)
    ]
    step(streams)

    def product(left, right, result):
        def body(i, carry):
            at = pl.ds(pl.multiple_of(i * 4 * ROWS, 4 * ROWS), 4 * ROWS)
            for j in range(3):
                cols = slice(512 * j, 512 * (j + 1))
                block = mm(left[at], right[:, cols], (1, 0)).astype(BF)
                result[lax.div(i, 2), pl.ds(lax.rem(i, 2) * 2, 2), :, :, cols] = block.reshape(
                    2, 2, ROWS, 512
                )
            return carry

        lax.fori_loop(0, 4, body, 0)

    for c in first:
        c.wait()
    product(lhs.at[0], cots_v, down)
    step(streams)
    weights = [
        scatter_stream(
            links,
            local.at[pl.ds(21 + 3 * i, 3)],
            down,
            FFN_DIMS,
            HALVES[i],
            FIRST_STAGE[i],
            scratch[4 * i : 4 * i + 4],
            (sum_a, sum_b)[i],
            ROWS,
            16,
        )
        for i in range(2)
    ]
    step(weights)
    third = move(up, lhs.at[0])
    for c in second:
        c.wait()
    product(lhs.at[1], tokens_v, part.at[0])
    stored = [move(part.at[0], gate_part)]
    step(weights)
    third.wait()
    product(lhs.at[0], tokens_v, part.at[1])
    stored.append(move(part.at[1], up_part))
    turned_slots = jnp.concatenate(
        [slots[:, head(i)].astype(F32).T.astype(BF) for i in range(16)], axis=0
    )
    step(streams)
    grad = out[...]
    mid = middle[...]
    factor = lax.rsqrt(jnp.sum(mid * mid, axis=1, keepdims=True) / D + norm_eps)
    gain_two_grad[...] = jnp.sum(grad * mid * factor, axis=0, keepdims=True)
    scaled = grad * gains[8:9]
    mean = jnp.sum(scaled * mid, axis=1, keepdims=True) / D
    total = cot[...].astype(F32) + factor * scaled - mid * (factor * factor * factor * mean)
    middle_grad[...] = total
    branch = total.astype(BF)
    fetched.wait()
    for i in range(4):
        grad_slots[:, 512 * i : 512 * (i + 1)] = mm(
            branch, weight[512 * i : 512 * (i + 1)], (1, 1)
        ).astype(BF)
    for i in range(4):
        for j in range(3):
            cols = slice(512 * j, 512 * (j + 1))
            block = mm(turned_slots[512 * i : 512 * (i + 1)], branch[:, cols], (1, 0))
            out_v[i // 2, i % 2, :, :, :, :, cols] = block.astype(BF).reshape(4, 4, 2, 16, 512)
        stored.append(move(out_v.at[i // 2, i % 2], out_part.at[i // 2, i % 2]))
    step(weights)
    for c in stored:
        c.wait()


def scatter_rows(own, rows, tokens, cots, hidden, gate, up, w_out):
    copies = count_scatter([("c", "x")]) + count_scatter(FIRST_STAGE)
    lead = lead_of(FFN_DIMS) + (ROWS, D)
    every = lead_of(AXES) + (16, D)
    scratch, sums = [], []
    for order in FIRST_STAGE:
        scratch += scatter_scratch(FFN_DIMS, order, ROWS, 768)
        rest = rest_of(FFN_DIMS, order[0].rstrip("~"))
        sums.append(jax.ShapeDtypeStruct(lead_of(rest) + (ROWS, 768), BF))
    part = jax.ShapeDtypeStruct(lead, BF)
    return pl.pallas_call(
        rows_scatter_kernel,
        out_shape=(
            jax.ShapeDtypeStruct((TOK, D), F32),
            jax.ShapeDtypeStruct((1, D), F32),
            jax.ShapeDtypeStruct((TOK, 2048), BF),
            *sums,
            part,
            part,
            jax.ShapeDtypeStruct(every, BF),
        ),
        in_specs=[VMEM] * 4 + [ANY] * 7,
        out_specs=(VMEM,) * 5 + (ANY,) * 3,
        scratch_shapes=[
            pltpu.VMEM((TOK, D), F32),
            pltpu.VMEM((2048, D), BF),
            pltpu.VMEM(tokens.shape, BF),
            pltpu.VMEM(cots.shape, BF),
            pltpu.VMEM((2,) + hidden.shape, BF),
            pltpu.VMEM((2,) + lead, BF),
            pltpu.VMEM(lead, BF),
            pltpu.VMEM(every, BF),
            pltpu.SemaphoreType.DMA((copies,)),
            pltpu.SemaphoreType.DMA((copies,)),
            pltpu.SemaphoreType.DMA((27,)),
        ]
        + scratch
        + scatter_scratch(ROW_DIMS, ("c", "x"), TOK, D),
        compiler_params=pltpu.CompilerParams(
            collective_id=4, has_side_effects=True, vmem_limit_bytes=63 * 2**20
        ),
    )(*own, rows, tokens, cots, hidden, gate, up, w_out)


GROUP = H // KVH
GQ = GROUP * TOK
KEYS = 512
SCALE = HD**-0.5
TO_LOG2 = SCALE * math.log2(math.e)


def head(h):
    return slice(128 * h, 128 * (h + 1))


def turned(v):
    return pltpu.roll(v, 64, 1)


def key_blocks():
    ctx = lax.axis_index("y") * 8 + lax.axis_index("x") * 2 + lax.axis_index("zh")
    return lax.div(ctx, 4) + 1, ctx * TOK


def key_block_of(ref, b, cols):
    return ref[lax.div(b, 2), pl.ds(lax.rem(b, 2) * 2, 2), :, :, cols].reshape(KEYS, HD)


def allowed_keys(b, first, row):
    key = b * KEYS + lax.broadcasted_iota(jnp.int32, (KEYS, GQ), 0)
    query = row + lax.rem(lax.broadcasted_iota(jnp.int32, (1, GQ), 1), TOK)
    return (key <= query) & (key >= first)


def mm(a, b, contract):
    return lax.dot_general(
        a, b, ((contract[:1], contract[1:]), ((), ())), preferred_element_type=F32
    )


def attend_all(kv, qs, first, row, blocks, acc, stats):
    acc[...] = jnp.zeros_like(acc)
    stats[:, 0:1] = jnp.full((KVH, 1, GQ), -1e30, F32)
    stats[:, 1:2] = jnp.zeros((KVH, 1, GQ), F32)

    def body(b, carry):
        allowed = allowed_keys(b, first, row)
        for g in range(KVH):
            keys = key_block_of(kv, b, head(g))
            values = key_block_of(kv, b, head(2 + g))
            raw = mm(keys, qs[g], (1, 1)) * TO_LOG2
            raw = jnp.where(allowed, raw, -1e30)
            old = stats[g, 0:1]
            top = jnp.maximum(old, jnp.max(raw, axis=0, keepdims=True))
            probs = jnp.exp2(raw - top)
            shrink = jnp.exp2(old - top)
            stats[g, 0:1] = top
            stats[g, 1:2] = stats[g, 1:2] * shrink + jnp.sum(probs, axis=0, keepdims=True)
            acc[g] = acc[g] * shrink + mm(values.T, probs.astype(BF), (1, 0))
        return carry

    lax.fori_loop(0, blocks, body, 0)


QKV_ORDERS = (("x!", "y!", "z!", "c"), ("y!", "z!", "x!", "c"), ("z!", "x!", "y!", "c"))
OUT_ORDERS = (("y!", "z!", "x", "c"), ("x!", "y!", "z", "c"))
KEY_ORDERS = (("zh", "x!", "y"), ("zh", "y!", "x"))
ROW_ORDER = ("x", "c")


def spread_row(blocks, offset, width, count):
    f = lax.broadcasted_iota(jnp.int32, (1, count), 1).astype(F32)
    block = jnp.floor((f + 0.5) * (1.0 / width))
    lane = offset + f - block * width
    index = lax.broadcasted_iota(jnp.int32, (128, count), 0).astype(F32)
    pick = (index == lane).astype(BF)
    spread = mm(blocks, pick, (1, 0))
    return jnp.sum(jnp.where(index == block, spread, 0.0), axis=0, keepdims=True)


def slot_matrix(out_rows):
    feature = lax.broadcasted_iota(jnp.int32, (384, 512), 0).astype(F32)
    slot = lax.broadcasted_iota(jnp.int32, (384, 512), 1).astype(F32)
    block = jnp.floor((feature + 0.5) * (1.0 / out_rows))
    return (slot == feature + block * (16 - out_rows)).astype(BF)


def front_kernel(*refs):
    tokens, cosine, sine, first_ref, small, out_in, gate_in, up_in, down_in, cot = refs[:10]
    qkv_block = refs[10]
    normed_one, gains, queries, attended, slots, lse, middle = refs[11:18]
    kv_hbm, qkv_hbm, out_hbm, gate_all, up_all, down_all, cot_all, rows_all = refs[18:26]
    small_all, w_qkv, w_out, kv, out_block, gate, up, down = refs[26:34]
    qkv, block, qs, acc, stats, normed, send, recv, local = refs[34:]
    me = here()
    links = Links(me, send, recv)
    own = []

    def keep(src, dst):
        own.append(pltpu.make_async_copy(src, dst, local.at[len(own)]))
        own[-1].start()
        return own[-1]

    first_copies = [
        keep(qkv_block, w_qkv.at[place(AXES, me, ())]),
        keep(small, small_all.at[place(AXES, me, ())]),
        keep(cot, cot_all.at[place(ROW_DIMS, me, ())]),
    ]
    out_rows = out_in.shape[0]
    out_block[0:out_rows] = out_in[...]
    out_block[out_rows:16] = jnp.zeros((16 - out_rows, D), BF)
    first_copies.append(keep(out_block, w_out.at[place(AXES, me, ())]))
    units = gate_in.shape[0]
    ffn = ((gate_in, gate, gate_all), (up_in, up, up_all), (down_in, down, down_all))
    for a, b, c in ffn:
        b[0:units] = a[...]
        b[units:ROWS] = jnp.zeros((ROWS - units, D), BF)
        first_copies.append(keep(b, c.at[place(FFN_DIMS, me, ())]))
    greet(me, ("x", "y", "z", "c", "zh"))
    qkvs = [
        gather_stream(links, qkv_block.at[tail], w_qkv, AXES, tail, order)
        for order, tail in zip(QKV_ORDERS, THIRDS, strict=True)
    ]
    qkvs.append(gather_stream(links, small, small_all, AXES, (), QKV_ORDERS[1]))
    outs = [
        gather_stream(links, out_block.at[tail], w_out, AXES, tail, order)
        for order, tail in zip(OUT_ORDERS, HALVES, strict=True)
    ]
    by_y, by_z = (
        [
            gather_stream(links, a.at[cut_at(column)[i]], b, FFN_DIMS, cut_at(column)[i], order)
            for (_, a, b), column in zip(ffn, GATHER_CUTS, strict=True)
        ]
        for i, order in enumerate(FFN_ORDERS)
    )
    cots = [gather_stream(links, cot, cot_all, ROW_DIMS, (), ROW_ORDER)]
    step(qkvs)
    step(outs)
    whole = tokens[...].astype(F32)
    factor = lax.rsqrt(jnp.sum(whole * whole, axis=1, keepdims=True) / D + norm_eps)
    first_copies[0].wait()
    first_copies[1].wait()
    step(qkvs)
    for c in first_copies[2:]:
        c.wait()
    step(outs)
    step(qkvs)
    step(qkvs)
    step(by_y)
    step(outs)
    step(qkvs)
    saved = [keep(w_qkv, qkv_hbm)]
    row = lax.broadcasted_iota(jnp.int32, (128, 2048), 0)
    entry = lax.broadcasted_iota(jnp.int32, (128, 2048), 1)
    blocks = mm((entry == row * 16).astype(BF), small_all[...].reshape(2048, 128), (1, 0)).astype(BF)
    bias = spread_row(blocks, 0, 16, 2048)
    gain = spread_row(blocks, 16, 12, D)
    gains[0:8] = jnp.broadcast_to(gain, (8, D))
    gain_two = spread_row(blocks, 28, 12, D)
    gains[8:16] = jnp.broadcast_to(gain_two, (8, D))
    normed_one[...] = (tokens[...].astype(F32) * factor * gain).astype(BF)
    cos, sin = cosine[...], sine[...]

    def project(j):
        part = w_qkv[j // 4, (j // 2) % 2, 2 * (j % 2) : 2 * (j % 2) + 2].reshape(256, D)
        return mm(normed_one[...], part, (1, 1)) + bias[:, 256 * j : 256 * (j + 1)]

    part = project(6)
    for g in range(KVH):
        one = part[:, head(g)]
        block[:, head(g)] = (one * cos + turned(one) * sin).astype(BF)
    block[:, 256:512] = project(7).astype(BF)
    mine = keep(block, kv.at[place(KV_DIMS, me, ())])
    keys = []
    for half, order in enumerate(KEY_ORDERS):
        tail = (slice(None), slice(256 * half, 256 * (half + 1)))
        keys.append(gather_stream(links, block.at[tail], kv, KV_DIMS, tail, order))
    step(keys)
    step(by_y)
    step(outs)
    step(by_z)
    mine.wait()
    for j in range(3):
        qkv[:, 256 * j : 256 * (j + 1)] = project(j)
    step(keys)
    for j in range(3, 6):
        qkv[:, 256 * j : 256 * (j + 1)] = project(j)
    step(by_z)
    step(by_y)
    step(keys)
    step(outs)
    for h in range(H):
        one = qkv[:, head(h)]
        rotated = (one * cos + turned(one) * sin).astype(BF)
        queries[:, head(h)] = rotated
        qs[h // GROUP, (h % GROUP) * TOK : (h % GROUP + 1) * TOK, :] = rotated
    step(keys)
    step(by_z)
    step(cots)
    step(keys)
    saved.append(keep(kv, kv_hbm))
    count, start = key_blocks()
    first = jnp.concatenate([first_ref[...]] * GROUP, axis=1)
    attend_all(kv, qs, first, start, count, acc, stats)
    for g in range(KVH):
        total = stats[g, 1:2]
        lse[g] = jnp.broadcast_to(stats[g, 0:1] + jnp.log2(total), (8, GQ))
        for i in range(GROUP):
            attended[:, head(GROUP * g + i)] = (acc[g, :, head(i)] / total[:, head(i)]).T
    step(cots)
    spread = slot_matrix(out_rows)
    for i in range(4):
        part = attended[:, 384 * i : 384 * (i + 1)].astype(BF)
        slots[:, 512 * i : 512 * (i + 1)] = mm(part, spread, (1, 0)).astype(BF)
    step(outs)
    saved.append(keep(w_out, out_hbm))
    square = jnp.zeros((TOK, 1), F32)
    for i in range(3):
        cols = slice(512 * i, 512 * (i + 1))
        part = w_out[:, :, :, :, :, :, cols].reshape(2048, 512)
        part = tokens[:, cols].astype(F32) + mm(slots[...], part, (1, 0))
        middle[:, cols] = part
        square = square + jnp.sum(part * part, axis=1, keepdims=True)
    factor = lax.rsqrt(square / D + norm_eps)
    normed[...] = (middle[...] * factor * gains[8:9]).astype(BF)
    mine = keep(normed, rows_all.at[place(ROW_DIMS, me, ())])
    rows = [gather_stream(links, normed, rows_all, ROW_DIMS, (), ROW_ORDER)]
    step(rows)
    step(by_y)
    step(by_z)
    step(cots)
    mine.wait()
    step(rows)
    step(rows)
    step(cots)
    step(rows)
    step(by_y)
    step(by_z)
    for c in saved:
        c.wait()


def front(tokens, cosine, sine, first, small, out_weight, gate, up, down, cot, qkv_weight):
    every = lead_of(AXES) + (16, D)
    kv = lead_of(KV_DIMS) + (TOK, 512)
    ffn = jax.ShapeDtypeStruct(lead_of(FFN_DIMS) + (ROWS, D), BF)
    rows = jax.ShapeDtypeStruct(lead_of(ROW_DIMS) + (TOK, D), BF)
    copies = count_gather(QKV_ORDERS + QKV_ORDERS[:1] + OUT_ORDERS + (ROW_ORDER, ROW_ORDER))
    copies += count_gather(KEY_ORDERS + 3 * FFN_ORDERS)
    return pl.pallas_call(
        front_kernel,
        out_shape=(
            jax.ShapeDtypeStruct((TOK, D), BF),
            jax.ShapeDtypeStruct((16, D), F32),
            jax.ShapeDtypeStruct((TOK, HQ), BF),
            jax.ShapeDtypeStruct((TOK, HQ), F32),
            jax.ShapeDtypeStruct((TOK, 2048), BF),
            jax.ShapeDtypeStruct((KVH, 8, GQ), F32),
            jax.ShapeDtypeStruct((TOK, D), F32),
            jax.ShapeDtypeStruct(kv, BF),
            jax.ShapeDtypeStruct(every, BF),
            jax.ShapeDtypeStruct(every, BF),
            ffn,
            ffn,
            ffn,
            rows,
            rows,
        ),
        in_specs=[VMEM] * 10 + [ANY],
        out_specs=(VMEM,) * 7 + (ANY,) * 8,
        scratch_shapes=[
            pltpu.VMEM(lead_of(AXES) + (16, 128), BF),
            pltpu.VMEM(every, BF),
            pltpu.VMEM(every, BF),
            pltpu.VMEM(kv, BF),
            pltpu.VMEM((16, D), BF),
            pltpu.VMEM((ROWS, D), BF),
            pltpu.VMEM((ROWS, D), BF),
            pltpu.VMEM((ROWS, D), BF),
            pltpu.VMEM((TOK, HQ), F32),
            pltpu.VMEM((TOK, 512), BF),
            pltpu.VMEM((KVH, GQ, HD), BF),
            pltpu.VMEM((KVH, HD, GQ), F32),
            pltpu.VMEM((KVH, 8, GQ), F32),
            pltpu.VMEM((TOK, D), BF),
            pltpu.SemaphoreType.DMA((copies,)),
            pltpu.SemaphoreType.DMA((copies,)),
            pltpu.SemaphoreType.DMA((12,)),
        ],
        compiler_params=pltpu.CompilerParams(
            collective_id=2, has_side_effects=True, vmem_limit_bytes=56 * 2**20
        ),
    )(tokens, cosine, sine, first, small, out_weight, gate, up, down, cot, qkv_weight)


def grad_all(kv, qs, gs, lse, delta, first, row, blocks, query_grad, kv_grad):
    query_grad[...] = jnp.zeros_like(query_grad)

    def body(b, carry):
        at = (lax.div(b, 2), pl.ds(lax.rem(b, 2) * 2, 2), slice(None), slice(None))
        allowed = allowed_keys(b, first, row)
        for g in range(KVH):
            keys = key_block_of(kv, b, head(g))
            values = key_block_of(kv, b, head(2 + g))
            raw = mm(keys, qs[g], (1, 1)) * TO_LOG2
            probs = jnp.where(allowed, jnp.exp2(raw - lse[g, 0:1]), 0.0)
            prob_grad = mm(values, gs[g], (1, 1))
            score_grad = (probs * (prob_grad - delta[g : g + 1])).astype(BF)
            key_term = mm(score_grad, qs[g], (1, 0)) * SCALE
            value_term = mm(probs.astype(BF), gs[g], (1, 0))
            kv_grad[at + (head(g),)] = key_term.astype(BF).reshape(2, 2, TOK, HD)
            kv_grad[at + (head(2 + g),)] = value_term.astype(BF).reshape(2, 2, TOK, HD)
            query_grad[g] += mm(keys.T, score_grad, (1, 0))
        return carry

    lax.fori_loop(0, blocks, body, 0)


def collect_row(row, offset, width):
    count = row.shape[1]
    f = lax.broadcasted_iota(jnp.int32, (1, count), 1).astype(F32)
    block = jnp.floor((f + 0.5) * (1.0 / width))
    lane = offset + f - block * width
    index = lax.broadcasted_iota(jnp.int32, (128, count), 0).astype(F32)
    spread = jnp.where(index == block, row, 0.0).astype(BF)
    return mm(spread, (index == lane).astype(BF), (1, 1))


def back_kernel(*refs):
    kv, queries, attended, grad_slots, lse, first_ref, cosine, sine = refs[:8]
    tokens, normed_one, gains, middle, middle_grad, gain_two_grad = refs[8:14]
    gate_part, up_part, down_a, down_b, out_part, ffn_rows, w_qkv = refs[14:21]
    layer_out, input_grad, qkv_out, small_out, out_last, gate_last, up_last, down_last = refs[21:29]
    qkv_part = refs[29]
    qs, gs, delta, query_grad, kv_grad, kv_out, qkv_grad, weight, staged = refs[30:39]
    small, ffn_total, out_out, gate_out, up_out, down_out, free, send, recv, local = refs[39:49]
    scratch = list(refs[49:])
    total = input_grad

    def take(n):
        return [scratch.pop(0) for _ in range(n)]

    me = here()
    links = Links(me, send, recv)
    used = [0]

    def slot():
        used[0] += 1
        return local.at[used[0] - 1]

    def fetch(j):
        c = pltpu.make_async_copy(w_qkv.at[pl.ds(512 * j, 512)], weight.at[j % 2], slot())
        c.start()
        return c

    fetched = [fetch(0), fetch(1)]
    greet(me, ("zh", "x", "y", "z", "c"))
    shared = [take(8) for _ in THIRDS]
    outs = [
        scatter_stream(links, slot(), out_part, AXES, tail, order, part, out_out.at[tail], 16, 16)
        for order, tail, part in zip(ALL_ORDERS, THIRDS, shared, strict=True)
    ]
    rows = [
        scatter_stream(
            links, slot(), ffn_rows, ROW_DIMS, (), ("c", "x"), take(4), ffn_total, TOK, 16
        )
    ]
    gates, ups = (
        [
            scatter_stream(
                links, slot(), source, FFN_DIMS, tail, order, take(4), target.at[tail], ROWS, ROWS
            )
            for order, tail in zip(THIRD_ORDERS, THIRDS, strict=True)
        ]
        for source, target in ((gate_part, gate_out), (up_part, up_out))
    )
    downs = [
        scatter_stream(
            links,
            slot(),
            source,
            rest_of(FFN_DIMS, order[0]),
            (),
            order[1:],
            take(2),
            down_out.at[tail],
            ROWS,
            16,
        )
        for source, order, tail in zip((down_a, down_b), FFN_ORDERS, HALVES, strict=True)
    ]
    step(outs)
    step(rows)
    step(downs)
    step(gates)
    blocks, row = key_blocks()
    first = jnp.concatenate([first_ref[...]] * GROUP, axis=1)
    spread = slot_matrix(out_last.shape[0])
    for i in range(4):
        part = mm(grad_slots[:, 512 * i : 512 * (i + 1)], spread, (1, 1))
        for j in range(3):
            h = 3 * i + j
            one = part[:, head(j)]
            gs[h // GROUP, (h % GROUP) * TOK : (h % GROUP + 1) * TOK, :] = one.astype(BF)
            both = (one * attended[:, head(h)]).T
            delta[h // GROUP : h // GROUP + 1, head(h % GROUP)] = jnp.sum(
                both, axis=0, keepdims=True
            )
            qs[h // GROUP, (h % GROUP) * TOK : (h % GROUP + 1) * TOK, :] = queries[:, head(h)]

    def clear(b, carry):
        at = (lax.div(b, 2), pl.ds(lax.rem(b, 2) * 2, 2))
        kv_grad[at] = jnp.zeros((2, 2, TOK, 512), BF)
        return carry

    lax.fori_loop(blocks, 8, clear, 0)
    step(outs)
    step(rows)
    cos, sin = cosine[...], sine[...]
    grad_all(kv, qs, gs, lse, delta, first, row, blocks, query_grad, kv_grad)
    keys = []
    for half, order in enumerate(KV_ORDERS):
        tail = (slice(None), slice(256 * half, 256 * (half + 1)))
        keys.append(
            scatter_stream(
                links, None, kv_grad, KV_DIMS, tail, order, take(6), kv_out.at[half], TOK, 64
            )
        )
    step(keys)
    for g in range(KVH):
        for i in range(GROUP):
            one = query_grad[g, :, head(i)].T * SCALE
            qkv_grad[:, head(GROUP * g + i)] = (one * cos - turned(one) * sin).astype(BF)
    step(outs)
    step(ups[1:2])
    stored = []

    def weight_terms(j):
        if j >= 2:
            stored[j - 2].wait()
        part = qkv_grad[:, 512 * j : 512 * (j + 1)]
        lhs = jnp.concatenate(
            [part[:, head(i)].astype(F32).T.astype(BF) for i in range(4)], axis=0
        )
        for i in range(3):
            cols = slice(512 * i, 512 * (i + 1))
            grad = mm(lhs, normed_one[:, cols], (1, 0)).astype(BF)
            staged[j % 2, :, :, :, :, cols] = grad.reshape(4, 4, 2, 16, 512)
        c = pltpu.make_async_copy(staged.at[j % 2], qkv_part.at[j // 2, j % 2], slot())
        c.start()
        stored.append(c)

    def input_terms(j):
        fetched[j].wait()
        part = qkv_grad[:, 512 * j : 512 * (j + 1)]
        for i in range(3):
            cols = slice(512 * i, 512 * (i + 1))
            term = mm(part, weight[j % 2, :, cols], (1, 0))
            if j == 0:
                total[:, cols] = term
            else:
                total[:, cols] += term

    for j in range(3):
        weight_terms(j)
        input_terms(j)
        if j < 2:
            fetched.append(fetch(j + 2))
    step(keys)
    step(outs)
    step(keys)
    step(gates)
    step(ups[:1])
    step(ups[2:])
    step(outs)
    for axis in ("c", "x", "y", "z"):
        for k in REACH[axis]:
            pl.semaphore_signal(
                free,
                inc=1,
                device_id=device_id(peer(me, axis, k)),
                device_id_type=pl.DeviceIdType.MESH,
            )
    step(keys)
    for g in range(KVH):
        one = kv_out[0, :, head(g)]
        qkv_grad[:, head(H + g)] = (one * cos - turned(one) * sin).astype(BF)
        qkv_grad[:, head(H + 2 + g)] = kv_out[1, :, head(g)].astype(BF)
    weight_terms(3)
    for c in stored[2:]:
        c.wait()
    pl.semaphore_wait(free, 10)
    qkvs = [
        scatter_stream(links, slot(), qkv_part, AXES, tail, order, part, qkv_out.at[tail], 16, 16)
        for order, tail, part in zip(ALL_ORDERS, THIRDS, shared, strict=True)
    ]
    step(qkvs)
    input_terms(3)
    whole = tokens[...].astype(F32)
    factor = lax.rsqrt(jnp.sum(whole * whole, axis=1, keepdims=True) / D + norm_eps)
    grad = total[...]
    gain_one_grad = jnp.sum(grad * whole * factor, axis=0, keepdims=True)
    bias_grad = jnp.sum(qkv_grad[...].astype(F32), axis=0, keepdims=True)
    line = lax.broadcasted_iota(jnp.int32, (128, 16, 128), 1)
    blocks_grad = jnp.zeros((128, 16, 128), F32)
    for i, (one, width) in enumerate(
        ((gain_one_grad, 12), (gain_two_grad[0:1], 12), (bias_grad, 16))
    ):
        blocks_grad = jnp.where(line == i, collect_row(one, 0, width)[:, None, :], blocks_grad)
    small[...] = blocks_grad.astype(BF).reshape(lead_of(AXES) + (16, 128))
    smalls = [
        scatter_stream(links, None, small, AXES, (), ALL_ORDERS[0], take(8), small_out, 16, 16)
    ]
    step(smalls)
    step(ups[1:2])
    step(qkvs)
    step(smalls)
    step(ups[:1])
    step(ups[2:])
    scaled = grad * gains[0:1]
    mean = jnp.sum(scaled * whole, axis=1, keepdims=True) / D
    input_grad[...] = middle_grad[...] + factor * scaled - whole * (factor * factor * factor * mean)
    step(rows)
    layer_out[...] = (middle[...] + ffn_total[...]).astype(BF)
    step(downs)
    step(gates)
    step(qkvs)
    step(smalls)
    step(ups)
    step(qkvs)
    step(smalls)
    out_last[...] = out_out[0 : out_last.shape[0]]
    units = gate_last.shape[0]
    gate_last[...] = gate_out[0:units]
    down_last[...] = down_out[0:units]
    up_last[...] = up_out[0:units]
    step(qkvs)
    step(smalls)


def back(inputs, parts, w_qkv, out_rows, units):
    copies = count_scatter(KV_ORDERS) + 2 * count_scatter(ALL_ORDERS)
    copies += count_scatter(ALL_ORDERS[:1]) + count_scatter([("c", "x")])
    copies += 2 * count_scatter(THIRD_ORDERS) + count_scatter(LAST_STAGE)
    every = lead_of(AXES) + (16, D)
    scratch = []
    for order in ALL_ORDERS:
        scratch += scatter_scratch(AXES, order, 16, 512)
    scratch += scatter_scratch(ROW_DIMS, ("c", "x"), TOK, D)
    for _ in range(2):
        for order in THIRD_ORDERS:
            scratch += scatter_scratch(FFN_DIMS, order, ROWS, 512)
    for order in FFN_ORDERS:
        scratch += scatter_scratch(rest_of(FFN_DIMS, order[0]), order[1:], ROWS, 768)
    for order in KV_ORDERS:
        scratch += scatter_scratch(KV_DIMS, order, TOK, 256)
    scratch += scatter_scratch(AXES, ALL_ORDERS[0], 16, 128)
    ffn = jax.ShapeDtypeStruct((units, D), F32)
    return pl.pallas_call(
        back_kernel,
        out_shape=(
            jax.ShapeDtypeStruct((TOK, D), BF),
            jax.ShapeDtypeStruct((TOK, D), F32),
            jax.ShapeDtypeStruct((16, D), F32),
            jax.ShapeDtypeStruct((16, 128), F32),
            jax.ShapeDtypeStruct((out_rows, D), F32),
            ffn,
            ffn,
            ffn,
            jax.ShapeDtypeStruct(every, BF),
        ),
        in_specs=[VMEM] * 14 + [ANY] * 7,
        out_specs=(VMEM,) * 8 + (ANY,),
        scratch_shapes=[
            pltpu.VMEM((KVH, GQ, HD), BF),
            pltpu.VMEM((KVH, GQ, HD), BF),
            pltpu.VMEM((8, GQ), F32),
            pltpu.VMEM((KVH, HD, GQ), F32),
            pltpu.VMEM(lead_of(KV_DIMS) + (TOK, 512), BF),
            pltpu.VMEM((2, TOK, 256), F32),
            pltpu.VMEM((TOK, 2048), BF),
            pltpu.VMEM((2, 512, D), BF),
            pltpu.VMEM((2, 4, 4, 2, 16, D), BF),
            pltpu.VMEM(lead_of(AXES) + (16, 128), BF),
            pltpu.VMEM((TOK, D), F32),
            pltpu.VMEM((16, D), F32),
            pltpu.VMEM((ROWS, D), F32),
            pltpu.VMEM((ROWS, D), F32),
            pltpu.VMEM((ROWS, D), F32),
            pltpu.SemaphoreType.REGULAR,
            pltpu.SemaphoreType.DMA((copies,)),
            pltpu.SemaphoreType.DMA((copies,)),
            pltpu.SemaphoreType.DMA((38,)),
        ]
        + scratch,
        compiler_params=pltpu.CompilerParams(
            collective_id=5, has_side_effects=True, vmem_limit_bytes=63 * 2**20
        ),
    )(*inputs, *parts, w_qkv)


def results_kernel(*refs):
    small, sources, gain_grads, bias_grad = refs[0], refs[1:8], refs[8], refs[9]
    targets = refs[10:17]
    for src, dst in zip(sources, targets, strict=True):
        dst = dst.at[0] if len(dst.shape) == 3 else dst
        dst[...] = src[...]
    gain_grads[...] = small[0:2, 0 : gain_grads.shape[1]]
    bias_grad[...] = small[2:3, 0 : bias_grad.shape[1]]


def results(small, arrays, gains, features):
    shapes = [(1,) + a.shape if a.shape[0] == TOK else a.shape for a in arrays]
    return pl.pallas_call(
        results_kernel,
        out_shape=(
            jax.ShapeDtypeStruct((2, gains), F32),
            jax.ShapeDtypeStruct((1, features), F32),
            *(jax.ShapeDtypeStruct(n, a.dtype) for n, a in zip(shapes, arrays, strict=True)),
        ),
        in_specs=[VMEM] * 8,
        out_specs=(VMEM,) * 9,
    )(small, *arrays)


def positions_of(documents):
    index = jnp.arange(documents.shape[0], dtype=jnp.int32)
    kinds = jnp.arange(doc_kinds, dtype=jnp.int32)
    counts = jnp.sum((documents[None, :] == kinds[:, None]).astype(jnp.int32), axis=1)
    starts = jnp.cumsum(counts) - counts
    first = jnp.sum(jnp.where(documents[:, None] == kinds[None, :], starts[None, :], 0), axis=1)
    return index - first


def rope_tables(position):
    half = HD // 2
    inverse = rope_base ** (-(jnp.arange(half, dtype=jnp.float32) * 2.0 / HD))
    angle = position.astype(jnp.float32)[:, None] * inverse[None, :]
    angle = jnp.concatenate([angle, angle], axis=1)
    return (jnp.cos(angle), jnp.sin(angle))


def dot(a, b, dims):
    return lax.dot_general(a, b, ((dims[:1], dims[1:]), ((), ())), preferred_element_type=F32)


def local(
    tokens_in,
    qkv_weight,
    qkv_bias,
    out_weight,
    norm_gains,
    gate_weight,
    up_weight,
    down_weight,
    doc_ids,
    cotangent,
):
    block_index = lax.axis_index("y") * 8 + lax.axis_index("x") * 2 + lax.axis_index("zh")
    documents = doc_ids[0]
    cot_low = cotangent[0]

    small = jnp.concatenate([qkv_bias, norm_gains.reshape(-1)])[None]
    small = jnp.pad(small, ((0, 15), (0, 128 - small.shape[1])))
    units, out_rows = gate_weight.shape[0], out_weight.shape[0]
    first_row = block_index * TOK
    my_pos = lax.dynamic_slice_in_dim(positions_of(documents), first_row, TOK, 0)
    cosine, sine = rope_tables(my_pos)
    sine = jnp.concatenate([-sine[:, : HD // 2], sine[:, HD // 2 :]], axis=1)
    first = first_row + jnp.arange(TOK, dtype=jnp.int32) - my_pos
    first = first[None]

    (
        normed_one,
        gains,
        queries,
        attended,
        slots,
        lse,
        middle,
        kv,
        w_qkv,
        w_out,
        w_gate,
        w_up,
        w_down,
        cot_rows,
        rows_two,
    ) = front(
        tokens_in[0],
        cosine,
        sine,
        first,
        small,
        out_weight,
        gate_weight,
        up_weight,
        down_weight,
        cot_low,
        qkv_weight,
    )
    w_qkv = w_qkv.reshape(2048, D)
    w_out = w_out.reshape(2048, D)
    w_gate, w_up, w_down = (w.reshape(-1, D) for w in (w_gate, w_up, w_down))
    cot_rows, rows_two = cot_rows.reshape(-1, D), rows_two.reshape(-1, D)

    gate = dot(w_gate, rows_two, (1, 1))
    upward = dot(w_up, rows_two, (1, 1))
    hidden_grad = dot(w_down, cot_rows, (1, 1))
    sigma = jax.nn.sigmoid(gate)
    hidden = (gate * sigma * upward).astype(BF)
    gate_grad = (hidden_grad * upward * sigma * (1.0 + gate * (1.0 - sigma))).astype(BF)
    upward_grad = (hidden_grad * gate * sigma).astype(BF)
    ffn_part = dot(hidden, w_down, (0, 0)).astype(BF)
    grad_part = (dot(gate_grad, w_gate, (0, 0)) + dot(upward_grad, w_up, (0, 0))).astype(BF)
    rows_lead = lead_of(ROW_DIMS) + (TOK, D)
    middle_grad, gain_two_grad, grad_slots, down_a, down_b, gate_part, up_part, out_part = scatter_rows(
        (middle, cot_low, gains, slots),
        grad_part.reshape(rows_lead),
        rows_two,
        cot_rows,
        hidden,
        gate_grad,
        upward_grad,
        w_out,
    )
    layer_out, input_grad, qkv_sum, small_sum, out_sum, gate_sum, up_sum, down_sum, _ = back(
        (
            kv,
            queries,
            attended,
            grad_slots,
            lse,
            first,
            cosine,
            sine,
            tokens_in[0],
            normed_one,
            gains,
            middle,
            middle_grad,
            gain_two_grad,
        ),
        (gate_part, up_part, down_a, down_b, out_part, ffn_part.reshape(rows_lead)),
        w_qkv,
        out_rows,
        units,
    )
    gain_grads, bias_grad, *arrays = results(
        small_sum,
        (layer_out, input_grad, qkv_sum, out_sum, gate_sum, up_sum, down_sum),
        norm_gains.shape[1],
        qkv_bias.shape[0],
    )
    return (*arrays[:3], bias_grad[0], arrays[3], gain_grads, *arrays[4:])


def solution(mesh):
    fine = Mesh(mesh.devices.reshape(tuple(SIZE[a] for a in AXES)), AXES)
    dp, ctx = ("zl", "c"), ("y", "x", "zh")
    in_specs = (
        P(dp, ctx, None),
        P(AXES, None),
        P(AXES),
        P(AXES, None),
        P(None, AXES),
        P(AXES, None),
        P(AXES, None),
        P(AXES, None),
        P(dp, None),
        P(dp, ctx, None),
    )
    out_specs = (
        P(dp, ctx, None),
        P(dp, ctx, None),
        P(AXES, None),
        P(AXES),
        P(AXES, None),
        P(None, AXES),
        P(AXES, None),
        P(AXES, None),
        P(AXES, None),
    )
    return jax.shard_map(local, mesh=fine, in_specs=in_specs, out_specs=out_specs, check_vma=False)
```

```python
import math

import jax
import jax.numpy as jnp
from jax import lax
from jax.experimental import pallas as pl
from jax.experimental.pallas import tpu as pltpu
from jax.sharding import Mesh
from jax.sharding import PartitionSpec as P

H = 12
KVH = 2
HD = 128
HQ = 1536
D = 1536
TOK = 128
ROWS = 80

norm_eps = 1e-06
rope_base = 1000000.0

AXES = ("zl", "c", "y", "x", "zh")
SIZE = {"zl": 2, "c": 2, "y": 4, "x": 4, "zh": 2}
PARTS_OF = {"z": ("zl", "zh"), "x": ("x",), "y": ("y",), "c": ("c",), "zh": ("zh",)}
REACH = {"z": (1, 2, 3), "x": (1, 2, 3), "y": (1, 2, 3), "c": (1,), "zh": (1,)}
BF = jnp.bfloat16
F32 = jnp.float32
ANY = pl.BlockSpec(memory_space=pl.ANY)
VMEM = pl.BlockSpec(memory_space=pltpu.VMEM)


def here():
    return {a: lax.axis_index(a) for a in AXES}


def peer(me, axis, k):
    to = dict(me)
    if axis == "z":
        z = lax.rem(me["zh"] * 2 + me["zl"] + k, 4)
        to["zl"], to["zh"] = lax.rem(z, 2), lax.div(z, 2)
    else:
        to[axis] = lax.rem(me[axis] + k, SIZE[axis])
    return to


def device_id(at):
    return tuple(at[a] for a in AXES)


def place(dims, at, whole, tail=()):
    return tuple(slice(None) if d in whole else at[d] for d in dims) + tuple(tail)


class Links:
    def __init__(self, me, send, recv):
        self.me, self.send, self.recv, self.used = me, send, recv, 0

    def copy(self, src, dst, axis, k):
        i = self.used
        self.used += 1
        c = pltpu.make_async_remote_copy(
            src_ref=src,
            dst_ref=dst,
            send_sem=self.send.at[i],
            recv_sem=self.recv.at[i],
            device_id=device_id(peer(self.me, axis, k)),
            device_id_type=pl.DeviceIdType.MESH,
        )
        c.start()
        return c


def greet(me, axes):
    barrier = pltpu.get_barrier_semaphore()
    count = 0
    for axis in axes:
        for k in REACH[axis]:
            pl.semaphore_signal(
                barrier,
                inc=1,
                device_id=device_id(peer(me, axis, k)),
                device_id_type=pl.DeviceIdType.MESH,
            )
            count += 1
    pl.semaphore_wait(barrier, count)


def halves_of(tail, cols):
    rows = tail[:-1] if tail else (slice(None),)
    start = tail[-1].start if tail else 0
    cut = cols // 2
    return tuple(rows + (slice(start + cut * i, start + cut * (i + 1)),) for i in range(2))


def gather_stream(links, block, buf, dims, tail, order):
    me = links.me
    whole = ()
    cols = block.shape[-1]
    for n, axis in enumerate(order):
        direct = axis.endswith("!")
        axis = axis.rstrip("!")
        mine = place(dims, me, whole, tail)
        src = block if n == 0 else buf.at[mine]
        ring = len(REACH[axis]) == 3 and not direct
        near = (1, 3) if ring else REACH[axis]
        copies = [links.copy(src, buf.at[mine], axis, k) for k in near]
        yield
        for c in copies:
            c.wait()
        if ring:
            copies = []
            for k, half in zip(near, halves_of(tail, cols), strict=True):
                theirs = buf.at[place(dims, peer(me, axis, 4 - k), whole, half)]
                copies.append(links.copy(theirs, theirs, axis, k))
            yield
            for c in copies:
                c.wait()
        whole = whole + PARTS_OF[axis]


def run_streams(streams):
    live = list(streams)
    while live:
        live = [s for s in live if next(s, live) is not live]


def step(streams):
    for s in streams:
        next(s, None)


def count_gather(orders):
    return sum({"c": 1, "zh": 1}.get(a, 3 if "!" in a else 4) for order in orders for a in order)


def count_scatter(orders):
    return sum(4 if "~" in a else len(REACH[a]) for order in orders for a in order)


THIRDS = tuple((slice(None), slice(512 * i, 512 * (i + 1))) for i in range(3))
ORDERS = (("x", "y", "z"), ("y", "z", "x"), ("z", "x", "y"))


def cut_at(column):
    return ((slice(None), slice(0, column)), (slice(None), slice(column, D)))


HALVES = cut_at(768)
GATHER_CUTS = (1024, 768, 1024)
THIRD_ORDERS = (("y", "z"), ("z", "y"), ("z", "y"))
FFN_ORDERS = (("y", "z"), ("z", "y"))
FFN_DIMS = ("zl", "y", "zh")
ROW_DIMS = ("x", "c")
KV_DIMS = ("y", "x", "zh")


def lead_of(dims):
    return tuple(SIZE[d] for d in dims)


def rest_of(dims, axis):
    return tuple(d for d in dims if d not in PARTS_OF[axis])


def scatter_scratch(dims, order, rows, cols):
    shapes = []
    for axis in order:
        ring = axis.endswith("~")
        axis = axis.rstrip("~")
        dims = rest_of(dims, axis)
        block = lead_of(dims) + (rows, cols)
        shapes.append(pltpu.VMEM((2 if ring else len(REACH[axis]),) + block, BF))
        shapes.append(pltpu.VMEM(block, BF))
        if ring:
            shapes.append(pltpu.VMEM((2,) + lead_of(dims) + (rows, cols // 2), BF))
            shapes.append(pltpu.VMEM((2,) + block, BF))
    return shapes


def block_index(i, lead, rows, step):
    per = rows // step
    block, row = lax.div(i, per), lax.rem(i, per)
    fine = lead[-1:] == (2,)
    index = []
    for n in reversed(lead[:-1] if fine else lead):
        index.append(lax.rem(block, n))
        block = lax.div(block, n)
    at = tuple(reversed(index)) + ((slice(None),) if fine else ())
    return at + (pl.ds(pl.multiple_of(row * step, step), step),)


def step_count(lead, rows, step):
    count = rows // step
    for n in lead[:-1] if lead[-1:] == (2,) else lead:
        count *= n
    return count


def sum_blocks(own, arrived, out, lead, rows, step):
    parts = arrived.shape[0]

    def body(i, carry):
        at = block_index(i, lead, rows, step)
        total = own[at].astype(F32)
        for p in range(parts):
            total = total + arrived[(p,) + at].astype(F32)
        out[at] = total.astype(out.dtype)
        return carry

    lax.fori_loop(0, step_count(lead, rows, step), body, 0)


def add_blocks(total, part, lead, rows, step, cols):
    def body(i, carry):
        at = block_index(i, lead, rows, step)
        whole = total[at + (cols,)].astype(F32) + part[at + (slice(None),)].astype(F32)
        total[at + (cols,)] = whole.astype(BF)
        return carry

    lax.fori_loop(0, step_count(lead, rows, step), body, 0)


def scatter_stream(links, local, source, dims, tail, order, scratch, out, rows, step):
    me = links.me
    now = None
    scratch = list(scratch)
    for n, axis in enumerate(order):
        ring = axis.endswith("~")
        axis = axis.rstrip("~")
        arrived, own = scratch.pop(0), scratch.pop(0)
        gone = PARTS_OF[axis]
        keep = tuple(d for d in dims if d not in gone)
        lead = lead_of(keep)
        end = tail if n == 0 else ()
        base = source if n == 0 else now
        staged = n == 0 and local is not None
        held = base.at[place(dims, me, keep, end)]
        fetched = []

        def stage(src, dst, sem):
            fetched.append(pltpu.make_async_copy(src, dst, sem))
            fetched[-1].start()

        if ring:
            passed, onward = scratch.pop(0), scratch.pop(0)
            cut = passed.shape[-1]
            copies = []
            for i, k in enumerate((1, 3)):
                half = halves_of(end, 2 * cut)[i]
                src = base.at[place(dims, peer(me, axis, 2), keep, half)]
                copies.append(links.copy(src, passed.at[i], axis, k))
                src = base.at[place(dims, peer(me, axis, k), keep, end)]
                if staged:
                    stage(src, onward.at[i], local.at[i])
            if staged:
                stage(held, own, local.at[2])
                held = own
            yield
            for c in fetched + copies:
                c.wait()
            copies = []
            for i, k in enumerate((1, 3)):
                cols = pl.ds(cut * i, cut)
                to = onward.at[i]
                add_blocks(to, passed.at[i], lead, rows, step, cols)
                copies.append(links.copy(to, arrived.at[i], axis, k))
        else:
            copies = []
            for k in REACH[axis]:
                src = base.at[place(dims, peer(me, axis, k), keep, end)]
                copies.append(links.copy(src, arrived.at[k - 1], axis, k))
            if staged:
                stage(held, own, local)
                held = own
        yield
        for c in ([] if ring else fetched) + copies:
            c.wait()
        target = out if n == len(order) - 1 else own
        sum_blocks(held, arrived, target, lead, rows, step)
        now, dims = own, keep


FIRST_STAGE = (("y~",), ("z~",))
LAST_STAGE = (("z",), ("y",))
KV_ORDERS = (("y", "x", "zh"), ("x", "y", "zh"))
ALL_ORDERS = tuple(("c",) + o for o in ORDERS)


def rows_scatter_kernel(*refs):
    middle, cot, gains, slots = refs[:4]
    rows, tokens, cots, hidden, gate, up, w_out = refs[4:11]
    middle_grad, gain_two_grad, grad_slots, sum_a, sum_b = refs[11:16]
    gate_part, up_part, out_part = refs[16:19]
    out, weight, tokens_v, cots_v, lhs, part, down, out_v, send, recv, local = refs[19:30]
    scratch = refs[30:]
    me = here()
    links = Links(me, send, recv)
    used = [0]

    def move(src, dst):
        used[0] += 1
        c = pltpu.make_async_copy(src, dst, local.at[used[0] - 1])
        c.start()
        return c

    first = [move(hidden, lhs.at[0]), move(cots, cots_v)]
    second = [move(gate, lhs.at[1]), move(tokens, tokens_v)]
    fetched = move(w_out, weight)
    greet(me, ("x", "y", "z", "c"))
    streams = [
        scatter_stream(links, local.at[20], rows, ROW_DIMS, (), ("c", "x"), scratch[8:], out, TOK, 16)
    ]
    step(streams)

    def product(left, right, result):
        def body(i, carry):
            at = pl.ds(pl.multiple_of(i * 4 * ROWS, 4 * ROWS), 4 * ROWS)
            for j in range(3):
                cols = slice(512 * j, 512 * (j + 1))
                block = mm(left[at], right[:, cols], (1, 0)).astype(BF)
                result[lax.div(i, 2), pl.ds(lax.rem(i, 2) * 2, 2), :, :, cols] = block.reshape(
                    2, 2, ROWS, 512
                )
            return carry

        lax.fori_loop(0, 4, body, 0)

    for c in first:
        c.wait()
    product(lhs.at[0], cots_v, down)
    step(streams)
    weights = [
        scatter_stream(
            links,
            local.at[pl.ds(21 + 3 * i, 3)],
            down,
            FFN_DIMS,
            HALVES[i],
            FIRST_STAGE[i],
            scratch[4 * i : 4 * i + 4],
            (sum_a, sum_b)[i],
            ROWS,
            16,
        )
        for i in range(2)
    ]
    step(weights)
    third = move(up, lhs.at[0])
    for c in second:
        c.wait()
    product(lhs.at[1], tokens_v, part.at[0])
    stored = [move(part.at[0], gate_part)]
    step(weights)
    third.wait()
    product(lhs.at[0], tokens_v, part.at[1])
    stored.append(move(part.at[1], up_part))
    turned_slots = jnp.concatenate(
        [slots[:, head(i)].astype(F32).T.astype(BF) for i in range(16)], axis=0
    )
    step(streams)
    grad = out[...]
    mid = middle[...]
    factor = lax.rsqrt(jnp.sum(mid * mid, axis=1, keepdims=True) / D + norm_eps)
    gain_two_grad[...] = jnp.sum(grad * mid * factor, axis=0, keepdims=True)
    scaled = grad * gains[8:9]
    mean = jnp.sum(scaled * mid, axis=1, keepdims=True) / D
    total = cot[...].astype(F32) + factor * scaled - mid * (factor * factor * factor * mean)
    middle_grad[...] = total
    branch = total.astype(BF)
    fetched.wait()
    for i in range(4):
        grad_slots[:, 512 * i : 512 * (i + 1)] = mm(
            branch, weight[512 * i : 512 * (i + 1)], (1, 1)
        ).astype(BF)
    for i in range(4):
        for j in range(3):
            cols = slice(512 * j, 512 * (j + 1))
            block = mm(turned_slots[512 * i : 512 * (i + 1)], branch[:, cols], (1, 0))
            out_v[i // 2, i % 2, :, :, :, :, cols] = block.astype(BF).reshape(4, 4, 2, 16, 512)
        stored.append(move(out_v.at[i // 2, i % 2], out_part.at[i // 2, i % 2]))
    step(weights)
    for c in stored:
        c.wait()


def scatter_rows(own, rows, tokens, cots, hidden, gate, up, w_out):
    copies = count_scatter([("c", "x")]) + count_scatter(FIRST_STAGE)
    lead = lead_of(FFN_DIMS) + (ROWS, D)
    every = lead_of(AXES) + (16, D)
    scratch, sums = [], []
    for order in FIRST_STAGE:
        scratch += scatter_scratch(FFN_DIMS, order, ROWS, 768)
        rest = rest_of(FFN_DIMS, order[0].rstrip("~"))
        sums.append(jax.ShapeDtypeStruct(lead_of(rest) + (ROWS, 768), BF))
    part = jax.ShapeDtypeStruct(lead, BF)
    return pl.pallas_call(
        rows_scatter_kernel,
        out_shape=(
            jax.ShapeDtypeStruct((TOK, D), F32),
            jax.ShapeDtypeStruct((1, D), F32),
            jax.ShapeDtypeStruct((TOK, 2048), BF),
            *sums,
            part,
            part,
            jax.ShapeDtypeStruct(every, BF),
        ),
        in_specs=[VMEM] * 4 + [ANY] * 7,
        out_specs=(VMEM,) * 5 + (ANY,) * 3,
        scratch_shapes=[
            pltpu.VMEM((TOK, D), F32),
            pltpu.VMEM((2048, D), BF),
            pltpu.VMEM(tokens.shape, BF),
            pltpu.VMEM(cots.shape, BF),
            pltpu.VMEM((2,) + hidden.shape, BF),
            pltpu.VMEM((2,) + lead, BF),
            pltpu.VMEM(lead, BF),
            pltpu.VMEM(every, BF),
            pltpu.SemaphoreType.DMA((copies,)),
            pltpu.SemaphoreType.DMA((copies,)),
            pltpu.SemaphoreType.DMA((27,)),
        ]
        + scratch
        + scatter_scratch(ROW_DIMS, ("c", "x"), TOK, D),
        compiler_params=pltpu.CompilerParams(
            collective_id=4, has_side_effects=True, vmem_limit_bytes=63 * 2**20
        ),
    )(*own, rows, tokens, cots, hidden, gate, up, w_out)


GROUP = H // KVH
GQ = GROUP * TOK
KEYS = 512
SCALE = HD**-0.5
TO_LOG2 = SCALE * math.log2(math.e)


def head(h):
    return slice(128 * h, 128 * (h + 1))


def turned(v):
    return pltpu.roll(v, 64, 1)


def key_blocks():
    ctx = lax.axis_index("y") * 8 + lax.axis_index("x") * 2 + lax.axis_index("zh")
    return lax.div(ctx, 4) + 1, ctx * TOK


def key_block_of(ref, b, cols):
    return ref[lax.div(b, 2), pl.ds(lax.rem(b, 2) * 2, 2), :, :, cols].reshape(KEYS, HD)


def allowed_keys(b, first, row):
    key = b * KEYS + lax.broadcasted_iota(jnp.int32, (KEYS, GQ), 0)
    query = row + lax.rem(lax.broadcasted_iota(jnp.int32, (1, GQ), 1), TOK)
    return (key <= query) & (key >= first)


def over_key_blocks(blocks, body):
    def at_edge(i, carry):
        body(i * (blocks - 1), True)
        return carry

    def between(b, carry):
        body(b, False)
        return carry

    lax.fori_loop(0, jnp.minimum(blocks, 2), at_edge, 0)
    lax.fori_loop(1, blocks - 1, between, 0)


def mm(a, b, contract):
    return lax.dot_general(
        a, b, ((contract[:1], contract[1:]), ((), ())), preferred_element_type=F32
    )


def attend_all(kv, qs, first, row, blocks, acc, stats):
    acc[...] = jnp.zeros_like(acc)
    stats[:, 0:1] = jnp.full((KVH, 1, GQ), -1e30, F32)
    stats[:, 1:2] = jnp.zeros((KVH, 1, GQ), F32)

    def body(b, edge):
        allowed = allowed_keys(b, first, row) if edge else None
        later = jnp.where(first > b * KEYS, -1e30, 0.0)
        for g in range(KVH):
            keys = key_block_of(kv, b, head(g))
            values = key_block_of(kv, b, head(2 + g))
            raw = mm(keys, qs[g], (1, 1)) * TO_LOG2
            raw = jnp.where(allowed, raw, -1e30) if edge else raw + later
            old = stats[g, 0:1]
            top = jnp.maximum(old, jnp.max(raw, axis=0, keepdims=True))
            probs = jnp.exp2(raw - top)
            shrink = jnp.exp2(old - top)
            stats[g, 0:1] = top
            stats[g, 1:2] = stats[g, 1:2] * shrink + jnp.sum(probs, axis=0, keepdims=True)
            acc[g] = acc[g] * shrink + mm(values.T, probs.astype(BF), (1, 0))

    over_key_blocks(blocks, body)


QKV_ORDERS = (("x!", "y!", "z!", "c"), ("y!", "z!", "x!", "c"), ("z!", "x!", "y!", "c"))
OUT_ORDERS = (("y!", "z!", "x", "c"), ("x!", "y!", "z", "c"))
KEY_ORDERS = (("zh", "x!", "y"), ("zh", "y!", "x"))
ROW_ORDER = ("x", "c")


def spread_row(blocks, offset, width, count):
    f = lax.broadcasted_iota(jnp.int32, (1, count), 1).astype(F32)
    block = jnp.floor((f + 0.5) * (1.0 / width))
    lane = offset + f - block * width
    index = lax.broadcasted_iota(jnp.int32, (128, count), 0).astype(F32)
    pick = (index == lane).astype(BF)
    spread = mm(blocks, pick, (1, 0))
    return jnp.sum(jnp.where(index == block, spread, 0.0), axis=0, keepdims=True)


def slot_matrix(out_rows):
    feature = lax.broadcasted_iota(jnp.int32, (384, 512), 0).astype(F32)
    slot = lax.broadcasted_iota(jnp.int32, (384, 512), 1).astype(F32)
    block = jnp.floor((feature + 0.5) * (1.0 / out_rows))
    return (slot == feature + block * (16 - out_rows)).astype(BF)


def position_tables(inverse, documents, cosine, sine, first_ref):
    _, start = key_blocks()
    ids = documents[...]
    counts = [jnp.sum((ids == k).astype(jnp.int32), axis=1, keepdims=True) for k in range(2)]
    mine = documents[:, pl.ds(pl.multiple_of(start, TOK), TOK)]
    first = jnp.where(mine == 0, 0, jnp.where(mine == 1, counts[0], counts[0] + counts[1]))
    first_ref[...] = first
    lane = lax.broadcasted_iota(jnp.int32, (1, TOK), 1)
    position = (start + lane - first).astype(F32)
    angle = jnp.broadcast_to(position, (TOK, TOK)).T * inverse[...]
    cosine[...] = jnp.cos(angle)
    sine[...] = jnp.where(lane < HD // 2, -jnp.sin(angle), jnp.sin(angle))


def front_kernel(*refs):
    tokens, inverse, documents, small, out_in, gate_in, up_in, down_in, cot = refs[:9]
    qkv_block = refs[9]
    normed_one, gains, queries, attended, slots, lse, middle = refs[10:17]
    cosine, sine, first_ref = refs[17:20]
    kv_hbm, qkv_hbm, out_hbm, gate_all, up_all, down_all, cot_all, rows_all = refs[20:28]
    small_all, w_qkv, w_out, kv, out_block, gate, up, down = refs[28:36]
    qkv, block, qs, acc, stats, normed, send, recv, local = refs[36:]
    me = here()
    links = Links(me, send, recv)
    own = []

    def keep(src, dst):
        own.append(pltpu.make_async_copy(src, dst, local.at[len(own)]))
        own[-1].start()
        return own[-1]

    first_copies = [
        keep(qkv_block, w_qkv.at[place(AXES, me, ())]),
        keep(small, small_all.at[place(AXES, me, ())]),
        keep(cot, cot_all.at[place(ROW_DIMS, me, ())]),
    ]
    out_rows = out_in.shape[0]
    out_block[0:out_rows] = out_in[...]
    out_block[out_rows:16] = jnp.zeros((16 - out_rows, D), BF)
    first_copies.append(keep(out_block, w_out.at[place(AXES, me, ())]))
    units = gate_in.shape[0]
    ffn = ((gate_in, gate, gate_all), (up_in, up, up_all), (down_in, down, down_all))
    for a, b, c in ffn:
        b[0:units] = a[...]
        b[units:ROWS] = jnp.zeros((ROWS - units, D), BF)
        first_copies.append(keep(b, c.at[place(FFN_DIMS, me, ())]))
    greet(me, ("x", "y", "z", "c", "zh"))
    qkvs = [
        gather_stream(links, qkv_block.at[tail], w_qkv, AXES, tail, order)
        for order, tail in zip(QKV_ORDERS, THIRDS, strict=True)
    ]
    qkvs.append(gather_stream(links, small, small_all, AXES, (), QKV_ORDERS[1]))
    outs = [
        gather_stream(links, out_block.at[tail], w_out, AXES, tail, order)
        for order, tail in zip(OUT_ORDERS, HALVES, strict=True)
    ]
    by_y, by_z = (
        [
            gather_stream(links, a.at[cut_at(column)[i]], b, FFN_DIMS, cut_at(column)[i], order)
            for (_, a, b), column in zip(ffn, GATHER_CUTS, strict=True)
        ]
        for i, order in enumerate(FFN_ORDERS)
    )
    cots = [gather_stream(links, cot, cot_all, ROW_DIMS, (), ROW_ORDER)]
    step(qkvs)
    step(outs)
    whole = tokens[...].astype(F32)
    factor = lax.rsqrt(jnp.sum(whole * whole, axis=1, keepdims=True) / D + norm_eps)
    first_copies[0].wait()
    first_copies[1].wait()
    step(qkvs)
    position_tables(inverse, documents, cosine, sine, first_ref)
    for c in first_copies[2:]:
        c.wait()
    step(outs)
    step(qkvs)
    step(by_y)
    step(qkvs)
    step(outs)
    step(qkvs)
    saved = [keep(w_qkv, qkv_hbm)]
    row = lax.broadcasted_iota(jnp.int32, (128, 2048), 0)
    entry = lax.broadcasted_iota(jnp.int32, (128, 2048), 1)
    blocks = mm((entry == row * 16).astype(BF), small_all[...].reshape(2048, 128), (1, 0)).astype(BF)
    bias = spread_row(blocks, 0, 16, 2048)
    gain = spread_row(blocks, 16, 12, D)
    gains[0:8] = jnp.broadcast_to(gain, (8, D))
    gain_two = spread_row(blocks, 28, 12, D)
    gains[8:16] = jnp.broadcast_to(gain_two, (8, D))
    normed_one[...] = (tokens[...].astype(F32) * factor * gain).astype(BF)
    cos, sin = cosine[...], sine[...]

    def project(j):
        part = w_qkv[j // 4, (j // 2) % 2, 2 * (j % 2) : 2 * (j % 2) + 2].reshape(256, D)
        return mm(normed_one[...], part, (1, 1)) + bias[:, 256 * j : 256 * (j + 1)]

    part = project(6)
    for g in range(KVH):
        one = part[:, head(g)]
        block[:, head(g)] = (one * cos + turned(one) * sin).astype(BF)
    block[:, 256:512] = project(7).astype(BF)
    mine = keep(block, kv.at[place(KV_DIMS, me, ())])
    keys = []
    for half, order in enumerate(KEY_ORDERS):
        tail = (slice(None), slice(256 * half, 256 * (half + 1)))
        keys.append(gather_stream(links, block.at[tail], kv, KV_DIMS, tail, order))
    step(keys)
    step(by_y)
    step(outs)
    step(by_z)
    mine.wait()
    for j in range(3):
        qkv[:, 256 * j : 256 * (j + 1)] = project(j)
    step(keys)
    for j in range(3, 6):
        qkv[:, 256 * j : 256 * (j + 1)] = project(j)
    step(by_z)
    step(by_y)
    step(keys)
    step(outs)
    for h in range(H):
        one = qkv[:, head(h)]
        rotated = (one * cos + turned(one) * sin).astype(BF)
        queries[:, head(h)] = rotated
        qs[h // GROUP, (h % GROUP) * TOK : (h % GROUP + 1) * TOK, :] = rotated
    step(keys)
    step(by_z)
    step(cots)
    step(keys)
    saved.append(keep(kv, kv_hbm))
    count, start = key_blocks()
    first = jnp.concatenate([first_ref[...]] * GROUP, axis=1)
    attend_all(kv, qs, first, start, count, acc, stats)
    for g in range(KVH):
        total = stats[g, 1:2]
        lse[g] = jnp.broadcast_to(stats[g, 0:1] + jnp.log2(total), (8, GQ))
        for i in range(GROUP):
            attended[:, head(GROUP * g + i)] = (acc[g, :, head(i)] / total[:, head(i)]).T
    step(cots)
    spread = slot_matrix(out_rows)
    for i in range(4):
        part = attended[:, 384 * i : 384 * (i + 1)].astype(BF)
        slots[:, 512 * i : 512 * (i + 1)] = mm(part, spread, (1, 0)).astype(BF)
    step(outs)
    saved.append(keep(w_out, out_hbm))
    square = jnp.zeros((TOK, 1), F32)
    for i in range(3):
        cols = slice(512 * i, 512 * (i + 1))
        part = w_out[:, :, :, :, :, :, cols].reshape(2048, 512)
        part = tokens[:, cols].astype(F32) + mm(slots[...], part, (1, 0))
        middle[:, cols] = part
        square = square + jnp.sum(part * part, axis=1, keepdims=True)
    factor = lax.rsqrt(square / D + norm_eps)
    normed[...] = (middle[...] * factor * gains[8:9]).astype(BF)
    mine = keep(normed, rows_all.at[place(ROW_DIMS, me, ())])
    rows = [gather_stream(links, normed, rows_all, ROW_DIMS, (), ROW_ORDER)]
    step(rows)
    step(by_y)
    step(by_z)
    step(cots)
    mine.wait()
    step(rows)
    step(rows)
    step(cots)
    step(rows)
    step(by_y)
    step(by_z)
    for c in saved:
        c.wait()


def front(tokens, inverse, documents, small, out_weight, gate, up, down, cot, qkv_weight):
    every = lead_of(AXES) + (16, D)
    kv = lead_of(KV_DIMS) + (TOK, 512)
    ffn = jax.ShapeDtypeStruct(lead_of(FFN_DIMS) + (ROWS, D), BF)
    rows = jax.ShapeDtypeStruct(lead_of(ROW_DIMS) + (TOK, D), BF)
    copies = count_gather(QKV_ORDERS + QKV_ORDERS[:1] + OUT_ORDERS + (ROW_ORDER, ROW_ORDER))
    copies += count_gather(KEY_ORDERS + 3 * FFN_ORDERS)
    return pl.pallas_call(
        front_kernel,
        out_shape=(
            jax.ShapeDtypeStruct((TOK, D), BF),
            jax.ShapeDtypeStruct((16, D), F32),
            jax.ShapeDtypeStruct((TOK, HQ), BF),
            jax.ShapeDtypeStruct((TOK, HQ), F32),
            jax.ShapeDtypeStruct((TOK, 2048), BF),
            jax.ShapeDtypeStruct((KVH, 8, GQ), F32),
            jax.ShapeDtypeStruct((TOK, D), F32),
            jax.ShapeDtypeStruct((TOK, HD), F32),
            jax.ShapeDtypeStruct((TOK, HD), F32),
            jax.ShapeDtypeStruct((1, TOK), jnp.int32),
            jax.ShapeDtypeStruct(kv, BF),
            jax.ShapeDtypeStruct(every, BF),
            jax.ShapeDtypeStruct(every, BF),
            ffn,
            ffn,
            ffn,
            rows,
            rows,
        ),
        in_specs=[VMEM] * 9 + [ANY],
        out_specs=(VMEM,) * 10 + (ANY,) * 8,
        scratch_shapes=[
            pltpu.VMEM(lead_of(AXES) + (16, 128), BF),
            pltpu.VMEM(every, BF),
            pltpu.VMEM(every, BF),
            pltpu.VMEM(kv, BF),
            pltpu.VMEM((16, D), BF),
            pltpu.VMEM((ROWS, D), BF),
            pltpu.VMEM((ROWS, D), BF),
            pltpu.VMEM((ROWS, D), BF),
            pltpu.VMEM((TOK, HQ), F32),
            pltpu.VMEM((TOK, 512), BF),
            pltpu.VMEM((KVH, GQ, HD), BF),
            pltpu.VMEM((KVH, HD, GQ), F32),
            pltpu.VMEM((KVH, 8, GQ), F32),
            pltpu.VMEM((TOK, D), BF),
            pltpu.SemaphoreType.DMA((copies,)),
            pltpu.SemaphoreType.DMA((copies,)),
            pltpu.SemaphoreType.DMA((12,)),
        ],
        compiler_params=pltpu.CompilerParams(
            collective_id=2, has_side_effects=True, vmem_limit_bytes=56 * 2**20
        ),
    )(tokens, inverse, documents, small, out_weight, gate, up, down, cot, qkv_weight)


def grad_all(kv, qs, gs, lse, delta, first, row, blocks, query_grad, kv_grad):
    query_grad[...] = jnp.zeros_like(query_grad)

    def body(b, edge):
        at = (lax.div(b, 2), pl.ds(lax.rem(b, 2) * 2, 2), slice(None), slice(None))
        allowed = allowed_keys(b, first, row) if edge else None
        later = jnp.where(first > b * KEYS, 1e30, 0.0)
        for g in range(KVH):
            keys = key_block_of(kv, b, head(g))
            values = key_block_of(kv, b, head(2 + g))
            raw = mm(keys, qs[g], (1, 1)) * TO_LOG2
            if edge:
                probs = jnp.where(allowed, jnp.exp2(raw - lse[g, 0:1]), 0.0)
            else:
                probs = jnp.exp2(raw - (lse[g, 0:1] + later))
            prob_grad = mm(values, gs[g], (1, 1))
            score_grad = (probs * (prob_grad - delta[g : g + 1])).astype(BF)
            key_term = mm(score_grad, qs[g], (1, 0)) * SCALE
            value_term = mm(probs.astype(BF), gs[g], (1, 0))
            kv_grad[at + (head(g),)] = key_term.astype(BF).reshape(2, 2, TOK, HD)
            kv_grad[at + (head(2 + g),)] = value_term.astype(BF).reshape(2, 2, TOK, HD)
            query_grad[g] += mm(keys.T, score_grad, (1, 0))

    over_key_blocks(blocks, body)


def collect_row(row, offset, width):
    count = row.shape[1]
    f = lax.broadcasted_iota(jnp.int32, (1, count), 1).astype(F32)
    block = jnp.floor((f + 0.5) * (1.0 / width))
    lane = offset + f - block * width
    index = lax.broadcasted_iota(jnp.int32, (128, count), 0).astype(F32)
    spread = jnp.where(index == block, row, 0.0).astype(BF)
    return mm(spread, (index == lane).astype(BF), (1, 1))


def back_kernel(*refs):
    kv, queries, attended, grad_slots, lse, first_ref, cosine, sine = refs[:8]
    tokens, normed_one, gains, middle, middle_grad, gain_two_grad = refs[8:14]
    gate_part, up_part, down_a, down_b, out_part, ffn_rows, w_qkv = refs[14:21]
    layer_out, input_grad, qkv_out, small_out, out_last, gate_last, up_last, down_last = refs[21:29]
    qkv_part = refs[29]
    qs, gs, delta, query_grad, kv_grad, kv_out, qkv_grad, weight, staged = refs[30:39]
    small, ffn_total, out_out, gate_out, up_out, down_out, free, send, recv, local = refs[39:49]
    scratch = list(refs[49:])
    total = input_grad

    def take(n):
        return [scratch.pop(0) for _ in range(n)]

    me = here()
    links = Links(me, send, recv)
    used = [0]

    def slot():
        used[0] += 1
        return local.at[used[0] - 1]

    def fetch(j):
        c = pltpu.make_async_copy(w_qkv.at[pl.ds(512 * j, 512)], weight.at[j % 2], slot())
        c.start()
        return c

    fetched = [fetch(0), fetch(1)]
    greet(me, ("zh", "x", "y", "z", "c"))
    shared = [take(8) for _ in THIRDS]
    outs = [
        scatter_stream(links, slot(), out_part, AXES, tail, order, part, out_out.at[tail], 16, 16)
        for order, tail, part in zip(ALL_ORDERS, THIRDS, shared, strict=True)
    ]
    rows = [
        scatter_stream(
            links, slot(), ffn_rows, ROW_DIMS, (), ("c", "x"), take(4), ffn_total, TOK, 16
        )
    ]
    gates, ups = (
        [
            scatter_stream(
                links, slot(), source, FFN_DIMS, tail, order, take(4), target.at[tail], ROWS, ROWS
            )
            for order, tail in zip(THIRD_ORDERS, THIRDS, strict=True)
        ]
        for source, target in ((gate_part, gate_out), (up_part, up_out))
    )
    downs = [
        scatter_stream(
            links,
            slot(),
            source,
            rest_of(FFN_DIMS, order[0]),
            (),
            order[1:],
            take(2),
            down_out.at[tail],
            ROWS,
            16,
        )
        for source, order, tail in zip((down_a, down_b), FFN_ORDERS, HALVES, strict=True)
    ]
    step(outs)
    step(rows)
    step(downs)
    blocks, row = key_blocks()
    first = jnp.concatenate([first_ref[...]] * GROUP, axis=1)
    spread = slot_matrix(out_last.shape[0])
    for i in range(4):
        part = mm(grad_slots[:, 512 * i : 512 * (i + 1)], spread, (1, 1))
        for j in range(3):
            h = 3 * i + j
            one = part[:, head(j)]
            gs[h // GROUP, (h % GROUP) * TOK : (h % GROUP + 1) * TOK, :] = one.astype(BF)
            both = (one * attended[:, head(h)]).T
            delta[h // GROUP : h // GROUP + 1, head(h % GROUP)] = jnp.sum(
                both, axis=0, keepdims=True
            )
            qs[h // GROUP, (h % GROUP) * TOK : (h % GROUP + 1) * TOK, :] = queries[:, head(h)]

    def clear(b, carry):
        at = (lax.div(b, 2), pl.ds(lax.rem(b, 2) * 2, 2))
        kv_grad[at] = jnp.zeros((2, 2, TOK, 512), BF)
        return carry

    lax.fori_loop(blocks, 8, clear, 0)
    step(outs)
    step(gates)
    cos, sin = cosine[...], sine[...]
    grad_all(kv, qs, gs, lse, delta, first, row, blocks, query_grad, kv_grad)
    keys = []
    for half, order in enumerate(KV_ORDERS):
        tail = (slice(None), slice(256 * half, 256 * (half + 1)))
        keys.append(
            scatter_stream(
                links, None, kv_grad, KV_DIMS, tail, order, take(6), kv_out.at[half], TOK, 64
            )
        )
    step(outs)
    step(keys)
    for g in range(KVH):
        for i in range(GROUP):
            one = query_grad[g, :, head(i)].T * SCALE
            qkv_grad[:, head(GROUP * g + i)] = (one * cos - turned(one) * sin).astype(BF)
    step(ups[1:2])
    stored = []

    def weight_terms(j):
        if j >= 2:
            stored[j - 2].wait()
        part = qkv_grad[:, 512 * j : 512 * (j + 1)]
        lhs = jnp.concatenate(
            [part[:, head(i)].astype(F32).T.astype(BF) for i in range(4)], axis=0
        )
        for i in range(3):
            cols = slice(512 * i, 512 * (i + 1))
            grad = mm(lhs, normed_one[:, cols], (1, 0)).astype(BF)
            staged[j % 2, :, :, :, :, cols] = grad.reshape(4, 4, 2, 16, 512)
        c = pltpu.make_async_copy(staged.at[j % 2], qkv_part.at[j // 2, j % 2], slot())
        c.start()
        stored.append(c)

    def input_terms(j):
        fetched[j].wait()
        part = qkv_grad[:, 512 * j : 512 * (j + 1)]
        for i in range(3):
            cols = slice(512 * i, 512 * (i + 1))
            term = mm(part, weight[j % 2, :, cols], (1, 0))
            if j == 0:
                total[:, cols] = term
            else:
                total[:, cols] += term

    for j in range(3):
        weight_terms(j)
        input_terms(j)
        if j < 2:
            fetched.append(fetch(j + 2))
    step(keys)
    step(outs)
    step(rows)
    step(keys)
    step(gates)
    step(ups[:1])
    step(ups[2:])
    step(outs)
    for axis in ("c", "x", "y", "z"):
        for k in REACH[axis]:
            pl.semaphore_signal(
                free,
                inc=1,
                device_id=device_id(peer(me, axis, k)),
                device_id_type=pl.DeviceIdType.MESH,
            )
    step(keys)
    for g in range(KVH):
        one = kv_out[0, :, head(g)]
        qkv_grad[:, head(H + g)] = (one * cos - turned(one) * sin).astype(BF)
        qkv_grad[:, head(H + 2 + g)] = kv_out[1, :, head(g)].astype(BF)
    weight_terms(3)
    for c in stored[2:]:
        c.wait()
    pl.semaphore_wait(free, 10)
    qkvs = [
        scatter_stream(links, slot(), qkv_part, AXES, tail, order, part, qkv_out.at[tail], 16, 16)
        for order, tail, part in zip(ALL_ORDERS, THIRDS, shared, strict=True)
    ]
    step(qkvs)
    input_terms(3)
    whole = tokens[...].astype(F32)
    factor = lax.rsqrt(jnp.sum(whole * whole, axis=1, keepdims=True) / D + norm_eps)
    grad = total[...]
    gain_one_grad = jnp.sum(grad * whole * factor, axis=0, keepdims=True)
    bias_grad = jnp.sum(qkv_grad[...].astype(F32), axis=0, keepdims=True)
    line = lax.broadcasted_iota(jnp.int32, (128, 16, 128), 1)
    blocks_grad = jnp.zeros((128, 16, 128), F32)
    for i, (one, width) in enumerate(
        ((gain_one_grad, 12), (gain_two_grad[0:1], 12), (bias_grad, 16))
    ):
        blocks_grad = jnp.where(line == i, collect_row(one, 0, width)[:, None, :], blocks_grad)
    small[...] = blocks_grad.astype(BF).reshape(lead_of(AXES) + (16, 128))
    smalls = [
        scatter_stream(links, None, small, AXES, (), ALL_ORDERS[0], take(8), small_out, 16, 16)
    ]
    step(smalls)
    step(ups[1:2])
    step(qkvs)
    step(smalls)
    step(ups[:1])
    step(ups[2:])
    scaled = grad * gains[0:1]
    mean = jnp.sum(scaled * whole, axis=1, keepdims=True) / D
    input_grad[...] = middle_grad[...] + factor * scaled - whole * (factor * factor * factor * mean)
    step(rows)
    layer_out[...] = (middle[...] + ffn_total[...]).astype(BF)
    step(downs)
    step(gates)
    step(qkvs)
    step(smalls)
    step(ups)
    step(qkvs)
    step(smalls)
    out_last[...] = out_out[0 : out_last.shape[0]]
    units = gate_last.shape[0]
    gate_last[...] = gate_out[0:units]
    down_last[...] = down_out[0:units]
    up_last[...] = up_out[0:units]
    step(qkvs)
    step(smalls)


def back(inputs, parts, w_qkv, out_rows, units):
    copies = count_scatter(KV_ORDERS) + 2 * count_scatter(ALL_ORDERS)
    copies += count_scatter(ALL_ORDERS[:1]) + count_scatter([("c", "x")])
    copies += 2 * count_scatter(THIRD_ORDERS) + count_scatter(LAST_STAGE)
    every = lead_of(AXES) + (16, D)
    scratch = []
    for order in ALL_ORDERS:
        scratch += scatter_scratch(AXES, order, 16, 512)
    scratch += scatter_scratch(ROW_DIMS, ("c", "x"), TOK, D)
    for _ in range(2):
        for order in THIRD_ORDERS:
            scratch += scatter_scratch(FFN_DIMS, order, ROWS, 512)
    for order in FFN_ORDERS:
        scratch += scatter_scratch(rest_of(FFN_DIMS, order[0]), order[1:], ROWS, 768)
    for order in KV_ORDERS:
        scratch += scatter_scratch(KV_DIMS, order, TOK, 256)
    scratch += scatter_scratch(AXES, ALL_ORDERS[0], 16, 128)
    ffn = jax.ShapeDtypeStruct((units, D), F32)
    return pl.pallas_call(
        back_kernel,
        out_shape=(
            jax.ShapeDtypeStruct((TOK, D), BF),
            jax.ShapeDtypeStruct((TOK, D), F32),
            jax.ShapeDtypeStruct((16, D), F32),
            jax.ShapeDtypeStruct((16, 128), F32),
            jax.ShapeDtypeStruct((out_rows, D), F32),
            ffn,
            ffn,
            ffn,
            jax.ShapeDtypeStruct(every, BF),
        ),
        in_specs=[VMEM] * 14 + [ANY] * 7,
        out_specs=(VMEM,) * 8 + (ANY,),
        scratch_shapes=[
            pltpu.VMEM((KVH, GQ, HD), BF),
            pltpu.VMEM((KVH, GQ, HD), BF),
            pltpu.VMEM((8, GQ), F32),
            pltpu.VMEM((KVH, HD, GQ), F32),
            pltpu.VMEM(lead_of(KV_DIMS) + (TOK, 512), BF),
            pltpu.VMEM((2, TOK, 256), F32),
            pltpu.VMEM((TOK, 2048), BF),
            pltpu.VMEM((2, 512, D), BF),
            pltpu.VMEM((2, 4, 4, 2, 16, D), BF),
            pltpu.VMEM(lead_of(AXES) + (16, 128), BF),
            pltpu.VMEM((TOK, D), F32),
            pltpu.VMEM((16, D), F32),
            pltpu.VMEM((ROWS, D), F32),
            pltpu.VMEM((ROWS, D), F32),
            pltpu.VMEM((ROWS, D), F32),
            pltpu.SemaphoreType.REGULAR,
            pltpu.SemaphoreType.DMA((copies,)),
            pltpu.SemaphoreType.DMA((copies,)),
            pltpu.SemaphoreType.DMA((38,)),
        ]
        + scratch,
        compiler_params=pltpu.CompilerParams(
            collective_id=5, has_side_effects=True, vmem_limit_bytes=63 * 2**20
        ),
    )(*inputs, *parts, w_qkv)


def results_kernel(*refs):
    small, sources, gain_grads, bias_grad = refs[0], refs[1:8], refs[8], refs[9]
    targets = refs[10:17]
    for src, dst in zip(sources, targets, strict=True):
        dst = dst.at[0] if len(dst.shape) == 3 else dst
        dst[...] = src[...]
    gain_grads[...] = small[0:2, 0 : gain_grads.shape[1]]
    bias_grad[...] = small[2:3, 0 : bias_grad.shape[1]]


def results(small, arrays, gains, features):
    shapes = [(1,) + a.shape if a.shape[0] == TOK else a.shape for a in arrays]
    return pl.pallas_call(
        results_kernel,
        out_shape=(
            jax.ShapeDtypeStruct((2, gains), F32),
            jax.ShapeDtypeStruct((1, features), F32),
            *(jax.ShapeDtypeStruct(n, a.dtype) for n, a in zip(shapes, arrays, strict=True)),
        ),
        in_specs=[VMEM] * 8,
        out_specs=(VMEM,) * 9,
    )(small, *arrays)


def dot(a, b, dims):
    return lax.dot_general(a, b, ((dims[:1], dims[1:]), ((), ())), preferred_element_type=F32)


def local(
    tokens_in,
    qkv_weight,
    qkv_bias,
    out_weight,
    norm_gains,
    gate_weight,
    up_weight,
    down_weight,
    doc_ids,
    cotangent,
):
    cot_low = cotangent[0]

    small = jnp.concatenate([qkv_bias, norm_gains.reshape(-1)])[None]
    small = jnp.pad(small, ((0, 15), (0, 128 - small.shape[1])))
    units, out_rows = gate_weight.shape[0], out_weight.shape[0]
    inverse = rope_base ** (-(jnp.arange(HD // 2, dtype=jnp.float32) * 2.0 / HD))
    inverse = jnp.concatenate([inverse, inverse])[None]
    (
        normed_one,
        gains,
        queries,
        attended,
        slots,
        lse,
        middle,
        cosine,
        sine,
        first,
        kv,
        w_qkv,
        w_out,
        w_gate,
        w_up,
        w_down,
        cot_rows,
        rows_two,
    ) = front(
        tokens_in[0],
        inverse,
        doc_ids,
        small,
        out_weight,
        gate_weight,
        up_weight,
        down_weight,
        cot_low,
        qkv_weight,
    )
    w_qkv = w_qkv.reshape(2048, D)
    w_out = w_out.reshape(2048, D)
    w_gate, w_up, w_down = (w.reshape(-1, D) for w in (w_gate, w_up, w_down))
    cot_rows, rows_two = cot_rows.reshape(-1, D), rows_two.reshape(-1, D)

    gate = dot(w_gate, rows_two, (1, 1)).astype(BF)
    upward = dot(w_up, rows_two, (1, 1)).astype(BF)
    gate, upward = (v.astype(F32) for v in lax.optimization_barrier((gate, upward)))
    hidden_grad = dot(w_down, cot_rows, (1, 1))
    sigma = jax.nn.sigmoid(gate)
    hidden = (gate * sigma * upward).astype(BF)
    gate_grad = (hidden_grad * upward * sigma * (1.0 + gate * (1.0 - sigma))).astype(BF)
    upward_grad = (hidden_grad * gate * sigma).astype(BF)
    ffn_part = dot(hidden, w_down, (0, 0)).astype(BF)
    grad_part = (dot(gate_grad, w_gate, (0, 0)) + dot(upward_grad, w_up, (0, 0))).astype(BF)
    rows_lead = lead_of(ROW_DIMS) + (TOK, D)
    middle_grad, gain_two_grad, grad_slots, down_a, down_b, gate_part, up_part, out_part = scatter_rows(
        (middle, cot_low, gains, slots),
        grad_part.reshape(rows_lead),
        rows_two,
        cot_rows,
        hidden,
        gate_grad,
        upward_grad,
        w_out,
    )
    layer_out, input_grad, qkv_sum, small_sum, out_sum, gate_sum, up_sum, down_sum, _ = back(
        (
            kv,
            queries,
            attended,
            grad_slots,
            lse,
            first,
            cosine,
            sine,
            tokens_in[0],
            normed_one,
            gains,
            middle,
            middle_grad,
            gain_two_grad,
        ),
        (gate_part, up_part, down_a, down_b, out_part, ffn_part.reshape(rows_lead)),
        w_qkv,
        out_rows,
        units,
    )
    gain_grads, bias_grad, *arrays = results(
        small_sum,
        (layer_out, input_grad, qkv_sum, out_sum, gate_sum, up_sum, down_sum),
        norm_gains.shape[1],
        qkv_bias.shape[0],
    )
    return (*arrays[:3], bias_grad[0], arrays[3], gain_grads, *arrays[4:])


def solution(mesh):
    fine = Mesh(mesh.devices.reshape(tuple(SIZE[a] for a in AXES)), AXES)
    dp, ctx = ("zl", "c"), ("y", "x", "zh")
    in_specs = (
        P(dp, ctx, None),
        P(AXES, None),
        P(AXES),
        P(AXES, None),
        P(None, AXES),
        P(AXES, None),
        P(AXES, None),
        P(AXES, None),
        P(dp, None),
        P(dp, ctx, None),
    )
    out_specs = (
        P(dp, ctx, None),
        P(dp, ctx, None),
        P(AXES, None),
        P(AXES),
        P(AXES, None),
        P(None, AXES),
        P(AXES, None),
        P(AXES, None),
        P(AXES, None),
    )
    return jax.shard_map(local, mesh=fine, in_specs=in_specs, out_specs=out_specs, check_vma=False)
```

```python
import math

import jax
import jax.numpy as jnp
from jax import lax
from jax.experimental import pallas as pl
from jax.experimental.pallas import tpu as pltpu
from jax.sharding import Mesh
from jax.sharding import PartitionSpec as P

H = 12
KVH = 2
HD = 128
HQ = 1536
D = 1536
TOK = 128
ROWS = 80

norm_eps = 1e-06
rope_base = 1000000.0

AXES = ("zl", "c", "y", "x", "zh")
SIZE = {"zl": 2, "c": 2, "y": 4, "x": 4, "zh": 2}
PARTS_OF = {"z": ("zl", "zh"), "x": ("x",), "y": ("y",), "c": ("c",), "zh": ("zh",)}
REACH = {"z": (1, 2, 3), "x": (1, 2, 3), "y": (1, 2, 3), "c": (1,), "zh": (1,)}
BF = jnp.bfloat16
F32 = jnp.float32
ANY = pl.BlockSpec(memory_space=pl.ANY)
VMEM = pl.BlockSpec(memory_space=pltpu.VMEM)


def here():
    return {a: lax.axis_index(a) for a in AXES}


def peer(me, axis, k):
    to = dict(me)
    if axis == "z":
        z = lax.rem(me["zh"] * 2 + me["zl"] + k, 4)
        to["zl"], to["zh"] = lax.rem(z, 2), lax.div(z, 2)
    else:
        to[axis] = lax.rem(me[axis] + k, SIZE[axis])
    return to


def device_id(at):
    return tuple(at[a] for a in AXES)


def place(dims, at, whole, tail=()):
    return tuple(slice(None) if d in whole else at[d] for d in dims) + tuple(tail)


class Links:
    def __init__(self, me, send, recv):
        self.me, self.send, self.recv, self.used = me, send, recv, 0

    def copy(self, src, dst, axis, k):
        i = self.used
        self.used += 1
        c = pltpu.make_async_remote_copy(
            src_ref=src,
            dst_ref=dst,
            send_sem=self.send.at[i],
            recv_sem=self.recv.at[i],
            device_id=device_id(peer(self.me, axis, k)),
            device_id_type=pl.DeviceIdType.MESH,
        )
        c.start()
        return c


def greet(me, axes):
    barrier = pltpu.get_barrier_semaphore()
    count = 0
    for axis in axes:
        for k in REACH[axis]:
            pl.semaphore_signal(
                barrier,
                inc=1,
                device_id=device_id(peer(me, axis, k)),
                device_id_type=pl.DeviceIdType.MESH,
            )
            count += 1
    pl.semaphore_wait(barrier, count)


def halves_of(tail, cols):
    rows = tail[:-1] if tail else (slice(None),)
    start = tail[-1].start if tail else 0
    cut = cols // 2
    return tuple(rows + (slice(start + cut * i, start + cut * (i + 1)),) for i in range(2))


def gather_stream(links, block, buf, dims, tail, order):
    me = links.me
    whole = ()
    cols = block.shape[-1]
    for n, axis in enumerate(order):
        direct = axis.endswith("!")
        axis = axis.rstrip("!")
        mine = place(dims, me, whole, tail)
        src = block if n == 0 else buf.at[mine]
        ring = len(REACH[axis]) == 3 and not direct
        near = (1, 3) if ring else REACH[axis]
        copies = [links.copy(src, buf.at[mine], axis, k) for k in near]
        yield
        for c in copies:
            c.wait()
        if ring:
            copies = []
            for k, half in zip(near, halves_of(tail, cols), strict=True):
                theirs = buf.at[place(dims, peer(me, axis, 4 - k), whole, half)]
                copies.append(links.copy(theirs, theirs, axis, k))
            yield
            for c in copies:
                c.wait()
        whole = whole + PARTS_OF[axis]


def run_streams(streams):
    live = list(streams)
    while live:
        live = [s for s in live if next(s, live) is not live]


def step(streams):
    for s in streams:
        next(s, None)


def count_gather(orders):
    return sum({"c": 1, "zh": 1}.get(a, 3 if "!" in a else 4) for order in orders for a in order)


def count_scatter(orders):
    return sum(4 if "~" in a else len(REACH[a]) for order in orders for a in order)


THIRDS = tuple((slice(None), slice(512 * i, 512 * (i + 1))) for i in range(3))
ORDERS = (("x", "y", "z"), ("y", "z", "x"), ("z", "x", "y"))


def cut_at(column):
    return ((slice(None), slice(0, column)), (slice(None), slice(column, D)))


HALVES = cut_at(768)
GATHER_CUTS = (1024, 768, 1024)
THIRD_ORDERS = (("y", "z"), ("z", "y"), ("z", "y"))
FFN_ORDERS = (("y", "z"), ("z", "y"))
FFN_DIMS = ("zl", "y", "zh")
ROW_DIMS = ("x", "c")
KV_DIMS = ("y", "x", "zh")


def lead_of(dims):
    return tuple(SIZE[d] for d in dims)


def rest_of(dims, axis):
    return tuple(d for d in dims if d not in PARTS_OF[axis])


def scatter_scratch(dims, order, rows, cols):
    shapes = []
    for axis in order:
        ring = axis.endswith("~")
        axis = axis.rstrip("~")
        dims = rest_of(dims, axis)
        block = lead_of(dims) + (rows, cols)
        shapes.append(pltpu.VMEM((2 if ring else len(REACH[axis]),) + block, BF))
        shapes.append(pltpu.VMEM(block, BF))
        if ring:
            shapes.append(pltpu.VMEM((2,) + lead_of(dims) + (rows, cols // 2), BF))
            shapes.append(pltpu.VMEM((2,) + block, BF))
    return shapes


def block_index(i, lead, rows, step):
    per = rows // step
    block, row = lax.div(i, per), lax.rem(i, per)
    fine = lead[-1:] == (2,)
    index = []
    for n in reversed(lead[:-1] if fine else lead):
        index.append(lax.rem(block, n))
        block = lax.div(block, n)
    at = tuple(reversed(index)) + ((slice(None),) if fine else ())
    return at + (pl.ds(pl.multiple_of(row * step, step), step),)


def step_count(lead, rows, step):
    count = rows // step
    for n in lead[:-1] if lead[-1:] == (2,) else lead:
        count *= n
    return count


def sum_blocks(own, arrived, out, lead, rows, step):
    parts = arrived.shape[0]

    def body(i, carry):
        at = block_index(i, lead, rows, step)
        total = own[at].astype(F32)
        for p in range(parts):
            total = total + arrived[(p,) + at].astype(F32)
        out[at] = total.astype(out.dtype)
        return carry

    lax.fori_loop(0, step_count(lead, rows, step), body, 0)


def add_blocks(total, part, lead, rows, step, cols):
    def body(i, carry):
        at = block_index(i, lead, rows, step)
        whole = total[at + (cols,)].astype(F32) + part[at + (slice(None),)].astype(F32)
        total[at + (cols,)] = whole.astype(BF)
        return carry

    lax.fori_loop(0, step_count(lead, rows, step), body, 0)


def scatter_stream(links, local, source, dims, tail, order, scratch, out, rows, step):
    me = links.me
    now = None
    scratch = list(scratch)
    for n, axis in enumerate(order):
        ring = axis.endswith("~")
        axis = axis.rstrip("~")
        arrived, own = scratch.pop(0), scratch.pop(0)
        gone = PARTS_OF[axis]
        keep = tuple(d for d in dims if d not in gone)
        lead = lead_of(keep)
        end = tail if n == 0 else ()
        base = source if n == 0 else now
        staged = n == 0 and local is not None
        held = base.at[place(dims, me, keep, end)]
        fetched = []

        def stage(src, dst, sem):
            fetched.append(pltpu.make_async_copy(src, dst, sem))
            fetched[-1].start()

        if ring:
            passed, onward = scratch.pop(0), scratch.pop(0)
            cut = passed.shape[-1]
            copies = []
            for i, k in enumerate((1, 3)):
                half = halves_of(end, 2 * cut)[i]
                src = base.at[place(dims, peer(me, axis, 2), keep, half)]
                copies.append(links.copy(src, passed.at[i], axis, k))
                src = base.at[place(dims, peer(me, axis, k), keep, end)]
                if staged:
                    stage(src, onward.at[i], local.at[i])
            if staged:
                stage(held, own, local.at[2])
                held = own
            yield
            for c in fetched + copies:
                c.wait()
            copies = []
            for i, k in enumerate((1, 3)):
                cols = pl.ds(cut * i, cut)
                to = onward.at[i]
                add_blocks(to, passed.at[i], lead, rows, step, cols)
                copies.append(links.copy(to, arrived.at[i], axis, k))
        else:
            copies = []
            for k in REACH[axis]:
                src = base.at[place(dims, peer(me, axis, k), keep, end)]
                copies.append(links.copy(src, arrived.at[k - 1], axis, k))
            if staged:
                stage(held, own, local)
                held = own
        yield
        for c in ([] if ring else fetched) + copies:
            c.wait()
        target = out if n == len(order) - 1 else own
        sum_blocks(held, arrived, target, lead, rows, step)
        now, dims = own, keep


FIRST_STAGE = (("y~",), ("z~",))
LAST_STAGE = (("z",), ("y",))
KV_ORDERS = (("y", "x", "zh"), ("x", "y", "zh"))
ALL_ORDERS = tuple(("c",) + o for o in ORDERS)


def rows_scatter_kernel(*refs):
    middle, cot, gains, slots = refs[:4]
    rows, tokens, cots, hidden, gate, up, w_out = refs[4:11]
    middle_grad, gain_two_grad, grad_slots, sum_a, sum_b = refs[11:16]
    gate_part, up_part, out_part = refs[16:19]
    out, weight, tokens_v, cots_v, lhs, part, down, out_v, send, recv, local = refs[19:30]
    scratch = refs[30:]
    me = here()
    links = Links(me, send, recv)
    used = [0]

    def move(src, dst):
        used[0] += 1
        c = pltpu.make_async_copy(src, dst, local.at[used[0] - 1])
        c.start()
        return c

    first = [move(hidden, lhs.at[0]), move(cots, cots_v)]
    second = [move(gate, lhs.at[1]), move(tokens, tokens_v)]
    fetched = move(w_out, weight)
    greet(me, ("x", "y", "z", "c"))
    streams = [
        scatter_stream(links, local.at[20], rows, ROW_DIMS, (), ("c", "x"), scratch[8:], out, TOK, 16)
    ]
    step(streams)

    def product(left, right, result):
        def body(i, carry):
            at = pl.ds(pl.multiple_of(i * 4 * ROWS, 4 * ROWS), 4 * ROWS)
            for j in range(3):
                cols = slice(512 * j, 512 * (j + 1))
                block = mm(left[at], right[:, cols], (1, 0)).astype(BF)
                result[lax.div(i, 2), pl.ds(lax.rem(i, 2) * 2, 2), :, :, cols] = block.reshape(
                    2, 2, ROWS, 512
                )
            return carry

        lax.fori_loop(0, 4, body, 0)

    for c in first:
        c.wait()
    product(lhs.at[0], cots_v, down)
    step(streams)
    weights = [
        scatter_stream(
            links,
            local.at[pl.ds(21 + 3 * i, 3)],
            down,
            FFN_DIMS,
            HALVES[i],
            FIRST_STAGE[i],
            scratch[4 * i : 4 * i + 4],
            (sum_a, sum_b)[i],
            ROWS,
            16,
        )
        for i in range(2)
    ]
    step(weights)
    third = move(up, lhs.at[0])
    for c in second:
        c.wait()
    product(lhs.at[1], tokens_v, part.at[0])
    stored = [move(part.at[0], gate_part)]
    step(weights)
    third.wait()
    product(lhs.at[0], tokens_v, part.at[1])
    stored.append(move(part.at[1], up_part))
    turned_slots = jnp.concatenate(
        [slots[:, head(i)].astype(F32).T.astype(BF) for i in range(16)], axis=0
    )
    step(streams)
    grad = out[...]
    mid = middle[...]
    factor = lax.rsqrt(jnp.sum(mid * mid, axis=1, keepdims=True) / D + norm_eps)
    gain_two_grad[...] = jnp.sum(grad * mid * factor, axis=0, keepdims=True)
    scaled = grad * gains[8:9]
    mean = jnp.sum(scaled * mid, axis=1, keepdims=True) / D
    total = cot[...].astype(F32) + factor * scaled - mid * (factor * factor * factor * mean)
    middle_grad[...] = total
    branch = total.astype(BF)
    fetched.wait()
    for i in range(4):
        grad_slots[:, 512 * i : 512 * (i + 1)] = mm(
            branch, weight[512 * i : 512 * (i + 1)], (1, 1)
        ).astype(BF)
    for i in range(4):
        for j in range(3):
            cols = slice(512 * j, 512 * (j + 1))
            block = mm(turned_slots[512 * i : 512 * (i + 1)], branch[:, cols], (1, 0))
            out_v[i // 2, i % 2, :, :, :, :, cols] = block.astype(BF).reshape(4, 4, 2, 16, 512)
        stored.append(move(out_v.at[i // 2, i % 2], out_part.at[i // 2, i % 2]))
    step(weights)
    for c in stored:
        c.wait()


def scatter_rows(own, rows, tokens, cots, hidden, gate, up, w_out):
    copies = count_scatter([("c", "x")]) + count_scatter(FIRST_STAGE)
    lead = lead_of(FFN_DIMS) + (ROWS, D)
    every = lead_of(AXES) + (16, D)
    scratch, sums = [], []
    for order in FIRST_STAGE:
        scratch += scatter_scratch(FFN_DIMS, order, ROWS, 768)
        rest = rest_of(FFN_DIMS, order[0].rstrip("~"))
        sums.append(jax.ShapeDtypeStruct(lead_of(rest) + (ROWS, 768), BF))
    part = jax.ShapeDtypeStruct(lead, BF)
    return pl.pallas_call(
        rows_scatter_kernel,
        out_shape=(
            jax.ShapeDtypeStruct((TOK, D), F32),
            jax.ShapeDtypeStruct((1, D), F32),
            jax.ShapeDtypeStruct((TOK, 2048), BF),
            *sums,
            part,
            part,
            jax.ShapeDtypeStruct(every, BF),
        ),
        in_specs=[VMEM] * 4 + [ANY] * 7,
        out_specs=(VMEM,) * 5 + (ANY,) * 3,
        scratch_shapes=[
            pltpu.VMEM((TOK, D), F32),
            pltpu.VMEM((2048, D), BF),
            pltpu.VMEM(tokens.shape, BF),
            pltpu.VMEM(cots.shape, BF),
            pltpu.VMEM((2,) + hidden.shape, BF),
            pltpu.VMEM((2,) + lead, BF),
            pltpu.VMEM(lead, BF),
            pltpu.VMEM(every, BF),
            pltpu.SemaphoreType.DMA((copies,)),
            pltpu.SemaphoreType.DMA((copies,)),
            pltpu.SemaphoreType.DMA((27,)),
        ]
        + scratch
        + scatter_scratch(ROW_DIMS, ("c", "x"), TOK, D),
        compiler_params=pltpu.CompilerParams(
            collective_id=4, has_side_effects=True, vmem_limit_bytes=63 * 2**20
        ),
    )(*own, rows, tokens, cots, hidden, gate, up, w_out)


GROUP = H // KVH
GQ = GROUP * TOK
KEYS = 512
SCALE = HD**-0.5
TO_LOG2 = SCALE * math.log2(math.e)


def head(h):
    return slice(128 * h, 128 * (h + 1))


def turned(v):
    return pltpu.roll(v, 64, 1)


def key_blocks():
    ctx = lax.axis_index("y") * 8 + lax.axis_index("x") * 2 + lax.axis_index("zh")
    return lax.div(ctx, 4) + 1, ctx * TOK


def key_block_of(ref, b, cols):
    return ref[lax.div(b, 2), pl.ds(lax.rem(b, 2) * 2, 2), :, :, cols].reshape(KEYS, HD)


def allowed_keys(b, first, row):
    key = b * KEYS + lax.broadcasted_iota(jnp.int32, (KEYS, GQ), 0)
    query = row + lax.rem(lax.broadcasted_iota(jnp.int32, (1, GQ), 1), TOK)
    return (key <= query) & (key >= first)


def over_key_blocks(blocks, body):
    def at_edge(i, carry):
        body(i * (blocks - 1), True)
        return carry

    def between(b, carry):
        body(b, False)
        return carry

    lax.fori_loop(0, jnp.minimum(blocks, 2), at_edge, 0)
    lax.fori_loop(1, blocks - 1, between, 0)


def mm(a, b, contract):
    return lax.dot_general(
        a, b, ((contract[:1], contract[1:]), ((), ())), preferred_element_type=F32
    )


def attend_all(kv, qs, first, row, blocks, acc, stats):
    acc[...] = jnp.zeros_like(acc)
    stats[:, 0:1] = jnp.full((KVH, 1, GQ), -1e30, F32)
    stats[:, 1:2] = jnp.zeros((KVH, 1, GQ), F32)

    def body(b, edge):
        allowed = allowed_keys(b, first, row) if edge else None
        later = jnp.where(first > b * KEYS, -1e30, 0.0)
        for g in range(KVH):
            keys = key_block_of(kv, b, head(g))
            values = key_block_of(kv, b, head(2 + g))
            raw = mm(keys, qs[g], (1, 1)) * TO_LOG2
            raw = jnp.where(allowed, raw, -1e30) if edge else raw + later
            old = stats[g, 0:1]
            top = jnp.maximum(old, jnp.max(raw, axis=0, keepdims=True))
            probs = jnp.exp2(raw - top)
            shrink = jnp.exp2(old - top)
            stats[g, 0:1] = top
            stats[g, 1:2] = stats[g, 1:2] * shrink + jnp.sum(probs, axis=0, keepdims=True)
            acc[g] = acc[g] * shrink + mm(values.T, probs.astype(BF), (1, 0))

    over_key_blocks(blocks, body)


QKV_ORDERS = (("x!", "y!", "z!", "c"), ("y!", "z!", "x!", "c"), ("z!", "x!", "y!", "c"))
OUT_ORDERS = (("y!", "z!", "x", "c"), ("x!", "y!", "z", "c"))
KEY_ORDERS = (("zh", "x!", "y"), ("zh", "y!", "x"))
ROW_ORDER = ("x", "c")


def spread_row(blocks, offset, width, count):
    f = lax.broadcasted_iota(jnp.int32, (1, count), 1).astype(F32)
    block = jnp.floor((f + 0.5) * (1.0 / width))
    lane = offset + f - block * width
    index = lax.broadcasted_iota(jnp.int32, (128, count), 0).astype(F32)
    pick = (index == lane).astype(BF)
    spread = mm(blocks, pick, (1, 0))
    return jnp.sum(jnp.where(index == block, spread, 0.0), axis=0, keepdims=True)


def slot_matrix(out_rows):
    feature = lax.broadcasted_iota(jnp.int32, (384, 512), 0).astype(F32)
    slot = lax.broadcasted_iota(jnp.int32, (384, 512), 1).astype(F32)
    block = jnp.floor((feature + 0.5) * (1.0 / out_rows))
    return (slot == feature + block * (16 - out_rows)).astype(BF)


def position_tables(inverse, documents, cosine, sine, first_ref):
    _, start = key_blocks()
    ids = documents[...]
    counts = [jnp.sum((ids == k).astype(jnp.int32), axis=1, keepdims=True) for k in range(2)]
    mine = documents[:, pl.ds(pl.multiple_of(start, TOK), TOK)]
    first = jnp.where(mine == 0, 0, jnp.where(mine == 1, counts[0], counts[0] + counts[1]))
    first_ref[...] = first
    lane = lax.broadcasted_iota(jnp.int32, (1, TOK), 1)
    position = (start + lane - first).astype(F32)
    angle = jnp.broadcast_to(position, (TOK, TOK)).T * inverse[...]
    cosine[...] = jnp.cos(angle)
    sine[...] = jnp.where(lane < HD // 2, -jnp.sin(angle), jnp.sin(angle))


def front_kernel(*refs):
    tokens, inverse, documents, small, out_in, gate_in, up_in, down_in, cot = refs[:9]
    qkv_block = refs[9]
    normed_one, gains, queries, attended, slots, lse, middle = refs[10:17]
    cosine, sine, first_ref = refs[17:20]
    kv_hbm, qkv_hbm, out_hbm, gate_all, up_all, down_all, cot_all, rows_all = refs[20:28]
    small_all, w_qkv, w_out, kv, out_block, gate, up, down = refs[28:36]
    padded, qkv, block, qs, acc, stats, normed, send, recv, local = refs[36:]
    me = here()
    links = Links(me, send, recv)
    own = []

    def keep(src, dst):
        own.append(pltpu.make_async_copy(src, dst, local.at[len(own)]))
        own[-1].start()
        return own[-1]

    first_copies = [
        keep(qkv_block, w_qkv.at[place(AXES, me, ())]),
        keep(small, small_all.at[place(AXES, me, ())]),
        keep(cot, cot_all.at[place(ROW_DIMS, me, ())]),
    ]
    ffn = ((gate_in, gate, gate_all), (up_in, up, up_all), (down_in, down, down_all))
    out_rows = out_in.shape[0]

    def pad_rows(source, target):
        padded[...] = jnp.zeros_like(padded)
        padded[0 : source.shape[0]] = source[...].astype(F32)
        target[...] = padded[0 : target.shape[0]].astype(BF)

    greet(me, ("x", "y", "z", "c", "zh"))
    qkvs = [
        gather_stream(links, qkv_block.at[tail], w_qkv, AXES, tail, order)
        for order, tail in zip(QKV_ORDERS, THIRDS, strict=True)
    ]
    qkvs.append(gather_stream(links, small, small_all, AXES, (), QKV_ORDERS[1]))
    outs = [
        gather_stream(links, out_block.at[tail], w_out, AXES, tail, order)
        for order, tail in zip(OUT_ORDERS, HALVES, strict=True)
    ]
    by_y, by_z = (
        [
            gather_stream(links, a.at[cut_at(column)[i]], b, FFN_DIMS, cut_at(column)[i], order)
            for (_, a, b), column in zip(ffn, GATHER_CUTS, strict=True)
        ]
        for i, order in enumerate(FFN_ORDERS)
    )
    cots = [gather_stream(links, cot, cot_all, ROW_DIMS, (), ROW_ORDER)]
    step(qkvs)
    pad_rows(out_in, out_block)
    first_copies.append(keep(out_block, w_out.at[place(AXES, me, ())]))
    step(outs)
    for a, b, c in ffn:
        pad_rows(a, b)
        first_copies.append(keep(b, c.at[place(FFN_DIMS, me, ())]))
    whole = tokens[...].astype(F32)
    factor = lax.rsqrt(jnp.sum(whole * whole, axis=1, keepdims=True) / D + norm_eps)
    first_copies[0].wait()
    first_copies[1].wait()
    step(qkvs)
    position_tables(inverse, documents, cosine, sine, first_ref)
    for c in first_copies[2:]:
        c.wait()
    step(outs)
    step(qkvs)
    step(by_y)
    step(qkvs)
    step(outs)
    step(qkvs)
    saved = [keep(w_qkv, qkv_hbm)]
    row = lax.broadcasted_iota(jnp.int32, (128, 2048), 0)
    entry = lax.broadcasted_iota(jnp.int32, (128, 2048), 1)
    blocks = mm((entry == row * 16).astype(BF), small_all[...].reshape(2048, 128), (1, 0)).astype(BF)
    bias = spread_row(blocks, 0, 16, 2048)
    gain = spread_row(blocks, 16, 12, D)
    gains[0:8] = jnp.broadcast_to(gain, (8, D))
    gain_two = spread_row(blocks, 28, 12, D)
    gains[8:16] = jnp.broadcast_to(gain_two, (8, D))
    normed_one[...] = (tokens[...].astype(F32) * factor * gain).astype(BF)
    cos, sin = cosine[...], sine[...]

    def project(j):
        part = w_qkv[j // 4, (j // 2) % 2, 2 * (j % 2) : 2 * (j % 2) + 2].reshape(256, D)
        return mm(normed_one[...], part, (1, 1)) + bias[:, 256 * j : 256 * (j + 1)]

    part = project(6)
    for g in range(KVH):
        one = part[:, head(g)]
        block[:, head(g)] = (one * cos + turned(one) * sin).astype(BF)
    block[:, 256:512] = project(7).astype(BF)
    mine = keep(block, kv.at[place(KV_DIMS, me, ())])
    keys = []
    for half, order in enumerate(KEY_ORDERS):
        tail = (slice(None), slice(256 * half, 256 * (half + 1)))
        keys.append(gather_stream(links, block.at[tail], kv, KV_DIMS, tail, order))
    step(keys)
    step(by_y)
    step(outs)
    step(by_z)
    mine.wait()
    for j in range(3):
        qkv[:, 256 * j : 256 * (j + 1)] = project(j)
    step(keys)
    for j in range(3, 6):
        qkv[:, 256 * j : 256 * (j + 1)] = project(j)
    step(by_z)
    step(by_y)
    step(keys)
    step(outs)
    for h in range(H):
        one = qkv[:, head(h)]
        rotated = (one * cos + turned(one) * sin).astype(BF)
        queries[:, head(h)] = rotated
        qs[h // GROUP, (h % GROUP) * TOK : (h % GROUP + 1) * TOK, :] = rotated
    step(keys)
    step(by_z)
    step(cots)
    step(keys)
    saved.append(keep(kv, kv_hbm))
    count, start = key_blocks()
    first = jnp.concatenate([first_ref[...]] * GROUP, axis=1)
    attend_all(kv, qs, first, start, count, acc, stats)
    for g in range(KVH):
        total = stats[g, 1:2]
        lse[g] = jnp.broadcast_to(stats[g, 0:1] + jnp.log2(total), (8, GQ))
        for i in range(GROUP):
            attended[:, head(GROUP * g + i)] = (acc[g, :, head(i)] / total[:, head(i)]).T
    step(cots)
    spread = slot_matrix(out_rows)
    for i in range(4):
        part = attended[:, 384 * i : 384 * (i + 1)].astype(BF)
        slots[:, 512 * i : 512 * (i + 1)] = mm(part, spread, (1, 0)).astype(BF)
    step(outs)
    saved.append(keep(w_out, out_hbm))
    square = jnp.zeros((TOK, 1), F32)
    for i in range(3):
        cols = slice(512 * i, 512 * (i + 1))
        part = w_out[:, :, :, :, :, :, cols].reshape(2048, 512)
        part = tokens[:, cols].astype(F32) + mm(slots[...], part, (1, 0))
        middle[:, cols] = part
        square = square + jnp.sum(part * part, axis=1, keepdims=True)
    factor = lax.rsqrt(square / D + norm_eps)
    normed[...] = (middle[...] * factor * gains[8:9]).astype(BF)
    mine = keep(normed, rows_all.at[place(ROW_DIMS, me, ())])
    rows = [gather_stream(links, normed, rows_all, ROW_DIMS, (), ROW_ORDER)]
    step(rows)
    step(by_y)
    step(by_z)
    step(cots)
    mine.wait()
    step(rows)
    step(rows)
    step(cots)
    step(rows)
    step(by_y)
    step(by_z)
    for c in saved:
        c.wait()


def front(tokens, inverse, documents, small, out_weight, gate, up, down, cot, qkv_weight):
    every = lead_of(AXES) + (16, D)
    kv = lead_of(KV_DIMS) + (TOK, 512)
    ffn = jax.ShapeDtypeStruct(lead_of(FFN_DIMS) + (ROWS, D), BF)
    rows = jax.ShapeDtypeStruct(lead_of(ROW_DIMS) + (TOK, D), BF)
    copies = count_gather(QKV_ORDERS + QKV_ORDERS[:1] + OUT_ORDERS + (ROW_ORDER, ROW_ORDER))
    copies += count_gather(KEY_ORDERS + 3 * FFN_ORDERS)
    return pl.pallas_call(
        front_kernel,
        out_shape=(
            jax.ShapeDtypeStruct((TOK, D), BF),
            jax.ShapeDtypeStruct((16, D), F32),
            jax.ShapeDtypeStruct((TOK, HQ), BF),
            jax.ShapeDtypeStruct((TOK, HQ), F32),
            jax.ShapeDtypeStruct((TOK, 2048), BF),
            jax.ShapeDtypeStruct((KVH, 8, GQ), F32),
            jax.ShapeDtypeStruct((TOK, D), F32),
            jax.ShapeDtypeStruct((TOK, HD), F32),
            jax.ShapeDtypeStruct((TOK, HD), F32),
            jax.ShapeDtypeStruct((1, TOK), jnp.int32),
            jax.ShapeDtypeStruct(kv, BF),
            jax.ShapeDtypeStruct(every, BF),
            jax.ShapeDtypeStruct(every, BF),
            ffn,
            ffn,
            ffn,
            rows,
            rows,
        ),
        in_specs=[VMEM] * 9 + [ANY],
        out_specs=(VMEM,) * 10 + (ANY,) * 8,
        scratch_shapes=[
            pltpu.VMEM(lead_of(AXES) + (16, 128), BF),
            pltpu.VMEM(every, BF),
            pltpu.VMEM(every, BF),
            pltpu.VMEM(kv, BF),
            pltpu.VMEM((16, D), BF),
            pltpu.VMEM((ROWS, D), BF),
            pltpu.VMEM((ROWS, D), BF),
            pltpu.VMEM((ROWS, D), BF),
            pltpu.VMEM((ROWS, D), F32),
            pltpu.VMEM((TOK, HQ), F32),
            pltpu.VMEM((TOK, 512), BF),
            pltpu.VMEM((KVH, GQ, HD), BF),
            pltpu.VMEM((KVH, HD, GQ), F32),
            pltpu.VMEM((KVH, 8, GQ), F32),
            pltpu.VMEM((TOK, D), BF),
            pltpu.SemaphoreType.DMA((copies,)),
            pltpu.SemaphoreType.DMA((copies,)),
            pltpu.SemaphoreType.DMA((12,)),
        ],
        compiler_params=pltpu.CompilerParams(
            collective_id=2, has_side_effects=True, vmem_limit_bytes=56 * 2**20
        ),
    )(tokens, inverse, documents, small, out_weight, gate, up, down, cot, qkv_weight)


def grad_all(kv, qs, gs, lse, delta, first, row, blocks, query_grad, kv_grad):
    query_grad[...] = jnp.zeros_like(query_grad)

    def body(b, edge):
        at = (lax.div(b, 2), pl.ds(lax.rem(b, 2) * 2, 2), slice(None), slice(None))
        allowed = allowed_keys(b, first, row) if edge else None
        later = jnp.where(first > b * KEYS, 1e30, 0.0)
        for g in range(KVH):
            keys = key_block_of(kv, b, head(g))
            values = key_block_of(kv, b, head(2 + g))
            raw = mm(keys, qs[g], (1, 1)) * TO_LOG2
            if edge:
                probs = jnp.where(allowed, jnp.exp2(raw - lse[g, 0:1]), 0.0)
            else:
                probs = jnp.exp2(raw - (lse[g, 0:1] + later))
            prob_grad = mm(values, gs[g], (1, 1))
            score_grad = (probs * (prob_grad - delta[g : g + 1])).astype(BF)
            key_term = mm(score_grad, qs[g], (1, 0)) * SCALE
            value_term = mm(probs.astype(BF), gs[g], (1, 0))
            kv_grad[at + (head(g),)] = key_term.astype(BF).reshape(2, 2, TOK, HD)
            kv_grad[at + (head(2 + g),)] = value_term.astype(BF).reshape(2, 2, TOK, HD)
            query_grad[g] += mm(keys.T, score_grad, (1, 0))

    over_key_blocks(blocks, body)


def collect_row(row, offset, width):
    count = row.shape[1]
    f = lax.broadcasted_iota(jnp.int32, (1, count), 1).astype(F32)
    block = jnp.floor((f + 0.5) * (1.0 / width))
    lane = offset + f - block * width
    index = lax.broadcasted_iota(jnp.int32, (128, count), 0).astype(F32)
    spread = jnp.where(index == block, row, 0.0).astype(BF)
    return mm(spread, (index == lane).astype(BF), (1, 1))


def back_kernel(*refs):
    kv, queries, attended, grad_slots, lse, first_ref, cosine, sine = refs[:8]
    tokens, normed_one, gains, middle, middle_grad, gain_two_grad = refs[8:14]
    gate_part, up_part, down_a, down_b, out_part, ffn_rows, w_qkv = refs[14:21]
    layer_out, input_grad, qkv_out, small_out, out_last, gate_last, up_last, down_last = refs[21:29]
    qkv_part = refs[29]
    qs, gs, delta, query_grad, kv_grad, kv_out, qkv_grad, weight, staged = refs[30:39]
    small, ffn_total, out_out, gate_out, up_out, down_out, free, send, recv, local = refs[39:49]
    scratch = list(refs[49:])
    total = input_grad

    def take(n):
        return [scratch.pop(0) for _ in range(n)]

    me = here()
    links = Links(me, send, recv)
    used = [0]

    def slot():
        used[0] += 1
        return local.at[used[0] - 1]

    def fetch(j):
        c = pltpu.make_async_copy(w_qkv.at[pl.ds(512 * j, 512)], weight.at[j % 2], slot())
        c.start()
        return c

    fetched = [fetch(0), fetch(1)]
    greet(me, ("zh", "x", "y", "z", "c"))
    shared = [take(8) for _ in THIRDS]
    outs = [
        scatter_stream(links, slot(), out_part, AXES, tail, order, part, out_out.at[tail], 16, 16)
        for order, tail, part in zip(ALL_ORDERS, THIRDS, shared, strict=True)
    ]
    rows = [
        scatter_stream(
            links, slot(), ffn_rows, ROW_DIMS, (), ("c", "x"), take(4), ffn_total, TOK, 16
        )
    ]
    gates, ups = (
        [
            scatter_stream(
                links, slot(), source, FFN_DIMS, tail, order, take(4), target.at[tail], ROWS, ROWS
            )
            for order, tail in zip(THIRD_ORDERS, THIRDS, strict=True)
        ]
        for source, target in ((gate_part, gate_out), (up_part, up_out))
    )
    downs = [
        scatter_stream(
            links,
            slot(),
            source,
            rest_of(FFN_DIMS, order[0]),
            (),
            order[1:],
            take(2),
            down_out.at[tail],
            ROWS,
            16,
        )
        for source, order, tail in zip((down_a, down_b), FFN_ORDERS, HALVES, strict=True)
    ]
    step(outs)
    step(rows)
    step(downs)
    blocks, row = key_blocks()
    first = jnp.concatenate([first_ref[...]] * GROUP, axis=1)
    spread = slot_matrix(out_last.shape[0])
    for i in range(4):
        part = mm(grad_slots[:, 512 * i : 512 * (i + 1)], spread, (1, 1))
        for j in range(3):
            h = 3 * i + j
            one = part[:, head(j)]
            gs[h // GROUP, (h % GROUP) * TOK : (h % GROUP + 1) * TOK, :] = one.astype(BF)
            both = (one * attended[:, head(h)]).T
            delta[h // GROUP : h // GROUP + 1, head(h % GROUP)] = jnp.sum(
                both, axis=0, keepdims=True
            )
            qs[h // GROUP, (h % GROUP) * TOK : (h % GROUP + 1) * TOK, :] = queries[:, head(h)]

    def clear(b, carry):
        at = (lax.div(b, 2), pl.ds(lax.rem(b, 2) * 2, 2))
        kv_grad[at] = jnp.zeros((2, 2, TOK, 512), BF)
        return carry

    lax.fori_loop(blocks, 8, clear, 0)
    step(outs)
    step(gates)
    cos, sin = cosine[...], sine[...]
    grad_all(kv, qs, gs, lse, delta, first, row, blocks, query_grad, kv_grad)
    keys = []
    for half, order in enumerate(KV_ORDERS):
        tail = (slice(None), slice(256 * half, 256 * (half + 1)))
        keys.append(
            scatter_stream(
                links, None, kv_grad, KV_DIMS, tail, order, take(6), kv_out.at[half], TOK, 64
            )
        )
    step(outs)
    step(keys)
    for g in range(KVH):
        for i in range(GROUP):
            one = query_grad[g, :, head(i)].T * SCALE
            qkv_grad[:, head(GROUP * g + i)] = (one * cos - turned(one) * sin).astype(BF)
    step(ups[1:2])
    stored = []

    def weight_terms(j):
        if j >= 2:
            stored[j - 2].wait()
        part = qkv_grad[:, 512 * j : 512 * (j + 1)]
        lhs = jnp.concatenate(
            [part[:, head(i)].astype(F32).T.astype(BF) for i in range(4)], axis=0
        )
        for i in range(3):
            cols = slice(512 * i, 512 * (i + 1))
            grad = mm(lhs, normed_one[:, cols], (1, 0)).astype(BF)
            staged[j % 2, :, :, :, :, cols] = grad.reshape(4, 4, 2, 16, 512)
        c = pltpu.make_async_copy(staged.at[j % 2], qkv_part.at[j // 2, j % 2], slot())
        c.start()
        stored.append(c)

    def input_terms(j):
        fetched[j].wait()
        part = qkv_grad[:, 512 * j : 512 * (j + 1)]
        for i in range(3):
            cols = slice(512 * i, 512 * (i + 1))
            term = mm(part, weight[j % 2, :, cols], (1, 0))
            if j == 0:
                total[:, cols] = term
            else:
                total[:, cols] += term

    for j in range(3):
        weight_terms(j)
        input_terms(j)
        if j < 2:
            fetched.append(fetch(j + 2))
    step(keys)
    step(outs)
    step(rows)
    step(keys)
    step(gates)
    step(ups[:1])
    step(ups[2:])
    step(outs)
    for axis in ("c", "x", "y", "z"):
        for k in REACH[axis]:
            pl.semaphore_signal(
                free,
                inc=1,
                device_id=device_id(peer(me, axis, k)),
                device_id_type=pl.DeviceIdType.MESH,
            )
    step(keys)
    for g in range(KVH):
        one = kv_out[0, :, head(g)]
        qkv_grad[:, head(H + g)] = (one * cos - turned(one) * sin).astype(BF)
        qkv_grad[:, head(H + 2 + g)] = kv_out[1, :, head(g)].astype(BF)
    weight_terms(3)
    for c in stored[2:]:
        c.wait()
    pl.semaphore_wait(free, 10)
    qkvs = [
        scatter_stream(links, slot(), qkv_part, AXES, tail, order, part, qkv_out.at[tail], 16, 16)
        for order, tail, part in zip(ALL_ORDERS, THIRDS, shared, strict=True)
    ]
    step(qkvs)
    input_terms(3)
    whole = tokens[...].astype(F32)
    factor = lax.rsqrt(jnp.sum(whole * whole, axis=1, keepdims=True) / D + norm_eps)
    grad = total[...]
    gain_one_grad = jnp.sum(grad * whole * factor, axis=0, keepdims=True)
    bias_grad = jnp.sum(qkv_grad[...].astype(F32), axis=0, keepdims=True)
    line = lax.broadcasted_iota(jnp.int32, (128, 16, 128), 1)
    blocks_grad = jnp.zeros((128, 16, 128), F32)
    for i, (one, width) in enumerate(
        ((gain_one_grad, 12), (gain_two_grad[0:1], 12), (bias_grad, 16))
    ):
        blocks_grad = jnp.where(line == i, collect_row(one, 0, width)[:, None, :], blocks_grad)
    small[...] = blocks_grad.astype(BF).reshape(lead_of(AXES) + (16, 128))
    smalls = [
        scatter_stream(links, None, small, AXES, (), ALL_ORDERS[0], take(8), small_out, 16, 16)
    ]
    step(smalls)
    step(ups[1:2])
    step(qkvs)
    step(smalls)
    step(ups[:1])
    step(ups[2:])
    scaled = grad * gains[0:1]
    mean = jnp.sum(scaled * whole, axis=1, keepdims=True) / D
    input_grad[...] = middle_grad[...] + factor * scaled - whole * (factor * factor * factor * mean)
    step(rows)
    layer_out[...] = (middle[...] + ffn_total[...]).astype(BF)
    step(downs)
    step(gates)
    step(qkvs)
    step(smalls)
    step(ups)
    step(qkvs)
    step(smalls)
    out_last[...] = out_out[0 : out_last.shape[0]]
    units = gate_last.shape[0]
    gate_last[...] = gate_out[0:units]
    down_last[...] = down_out[0:units]
    up_last[...] = up_out[0:units]
    step(qkvs)
    step(smalls)


def back(inputs, parts, w_qkv, out_rows, units):
    copies = count_scatter(KV_ORDERS) + 2 * count_scatter(ALL_ORDERS)
    copies += count_scatter(ALL_ORDERS[:1]) + count_scatter([("c", "x")])
    copies += 2 * count_scatter(THIRD_ORDERS) + count_scatter(LAST_STAGE)
    every = lead_of(AXES) + (16, D)
    scratch = []
    for order in ALL_ORDERS:
        scratch += scatter_scratch(AXES, order, 16, 512)
    scratch += scatter_scratch(ROW_DIMS, ("c", "x"), TOK, D)
    for _ in range(2):
        for order in THIRD_ORDERS:
            scratch += scatter_scratch(FFN_DIMS, order, ROWS, 512)
    for order in FFN_ORDERS:
        scratch += scatter_scratch(rest_of(FFN_DIMS, order[0]), order[1:], ROWS, 768)
    for order in KV_ORDERS:
        scratch += scatter_scratch(KV_DIMS, order, TOK, 256)
    scratch += scatter_scratch(AXES, ALL_ORDERS[0], 16, 128)
    ffn = jax.ShapeDtypeStruct((units, D), F32)
    return pl.pallas_call(
        back_kernel,
        out_shape=(
            jax.ShapeDtypeStruct((TOK, D), BF),
            jax.ShapeDtypeStruct((TOK, D), F32),
            jax.ShapeDtypeStruct((16, D), F32),
            jax.ShapeDtypeStruct((16, 128), F32),
            jax.ShapeDtypeStruct((out_rows, D), F32),
            ffn,
            ffn,
            ffn,
            jax.ShapeDtypeStruct(every, BF),
        ),
        in_specs=[VMEM] * 14 + [ANY] * 7,
        out_specs=(VMEM,) * 8 + (ANY,),
        scratch_shapes=[
            pltpu.VMEM((KVH, GQ, HD), BF),
            pltpu.VMEM((KVH, GQ, HD), BF),
            pltpu.VMEM((8, GQ), F32),
            pltpu.VMEM((KVH, HD, GQ), F32),
            pltpu.VMEM(lead_of(KV_DIMS) + (TOK, 512), BF),
            pltpu.VMEM((2, TOK, 256), F32),
            pltpu.VMEM((TOK, 2048), BF),
            pltpu.VMEM((2, 512, D), BF),
            pltpu.VMEM((2, 4, 4, 2, 16, D), BF),
            pltpu.VMEM(lead_of(AXES) + (16, 128), BF),
            pltpu.VMEM((TOK, D), F32),
            pltpu.VMEM((16, D), F32),
            pltpu.VMEM((ROWS, D), F32),
            pltpu.VMEM((ROWS, D), F32),
            pltpu.VMEM((ROWS, D), F32),
            pltpu.SemaphoreType.REGULAR,
            pltpu.SemaphoreType.DMA((copies,)),
            pltpu.SemaphoreType.DMA((copies,)),
            pltpu.SemaphoreType.DMA((38,)),
        ]
        + scratch,
        compiler_params=pltpu.CompilerParams(
            collective_id=5, has_side_effects=True, vmem_limit_bytes=63 * 2**20
        ),
    )(*inputs, *parts, w_qkv)


def results_kernel(*refs):
    small, sources, gain_grads, bias_grad = refs[0], refs[1:8], refs[8], refs[9]
    targets = refs[10:17]
    for src, dst in zip(sources, targets, strict=True):
        dst = dst.at[0] if len(dst.shape) == 3 else dst
        dst[...] = src[...]
    gain_grads[...] = small[0:2, 0 : gain_grads.shape[1]]
    bias_grad[...] = small[2:3, 0 : bias_grad.shape[1]]


def results(small, arrays, gains, features):
    shapes = [(1,) + a.shape if a.shape[0] == TOK else a.shape for a in arrays]
    return pl.pallas_call(
        results_kernel,
        out_shape=(
            jax.ShapeDtypeStruct((2, gains), F32),
            jax.ShapeDtypeStruct((1, features), F32),
            *(jax.ShapeDtypeStruct(n, a.dtype) for n, a in zip(shapes, arrays, strict=True)),
        ),
        in_specs=[VMEM] * 8,
        out_specs=(VMEM,) * 9,
    )(small, *arrays)


def dot(a, b, dims):
    return lax.dot_general(a, b, ((dims[:1], dims[1:]), ((), ())), preferred_element_type=F32)


def local(
    tokens_in,
    qkv_weight,
    qkv_bias,
    out_weight,
    norm_gains,
    gate_weight,
    up_weight,
    down_weight,
    doc_ids,
    cotangent,
):
    cot_low = cotangent[0]

    small = jnp.concatenate([qkv_bias, norm_gains.reshape(-1)])[None]
    small = jnp.pad(small, ((0, 15), (0, 128 - small.shape[1])))
    units, out_rows = gate_weight.shape[0], out_weight.shape[0]
    inverse = rope_base ** (-(jnp.arange(HD // 2, dtype=jnp.float32) * 2.0 / HD))
    inverse = jnp.concatenate([inverse, inverse])[None]
    (
        normed_one,
        gains,
        queries,
        attended,
        slots,
        lse,
        middle,
        cosine,
        sine,
        first,
        kv,
        w_qkv,
        w_out,
        w_gate,
        w_up,
        w_down,
        cot_rows,
        rows_two,
    ) = front(
        tokens_in[0],
        inverse,
        doc_ids,
        small,
        out_weight,
        gate_weight,
        up_weight,
        down_weight,
        cot_low,
        qkv_weight,
    )
    w_qkv = w_qkv.reshape(2048, D)
    w_out = w_out.reshape(2048, D)
    w_gate, w_up, w_down = (w.reshape(-1, D) for w in (w_gate, w_up, w_down))
    cot_rows, rows_two = cot_rows.reshape(-1, D), rows_two.reshape(-1, D)

    gate = dot(w_gate, rows_two, (1, 1)).astype(BF)
    upward = dot(w_up, rows_two, (1, 1)).astype(BF)
    gate, upward = (v.astype(F32) for v in lax.optimization_barrier((gate, upward)))
    hidden_grad = dot(w_down, cot_rows, (1, 1))
    sigma = jax.nn.sigmoid(gate)
    hidden = (gate * sigma * upward).astype(BF)
    gate_grad = (hidden_grad * upward * sigma * (1.0 + gate * (1.0 - sigma))).astype(BF)
    upward_grad = (hidden_grad * gate * sigma).astype(BF)
    ffn_part = dot(hidden, w_down, (0, 0)).astype(BF)
    grad_part = (dot(gate_grad, w_gate, (0, 0)) + dot(upward_grad, w_up, (0, 0))).astype(BF)
    rows_lead = lead_of(ROW_DIMS) + (TOK, D)
    middle_grad, gain_two_grad, grad_slots, down_a, down_b, gate_part, up_part, out_part = scatter_rows(
        (middle, cot_low, gains, slots),
        grad_part.reshape(rows_lead),
        rows_two,
        cot_rows,
        hidden,
        gate_grad,
        upward_grad,
        w_out,
    )
    layer_out, input_grad, qkv_sum, small_sum, out_sum, gate_sum, up_sum, down_sum, _ = back(
        (
            kv,
            queries,
            attended,
            grad_slots,
            lse,
            first,
            cosine,
            sine,
            tokens_in[0],
            normed_one,
            gains,
            middle,
            middle_grad,
            gain_two_grad,
        ),
        (gate_part, up_part, down_a, down_b, out_part, ffn_part.reshape(rows_lead)),
        w_qkv,
        out_rows,
        units,
    )
    gain_grads, bias_grad, *arrays = results(
        small_sum,
        (layer_out, input_grad, qkv_sum, out_sum, gate_sum, up_sum, down_sum),
        norm_gains.shape[1],
        qkv_bias.shape[0],
    )
    return (*arrays[:3], bias_grad[0], arrays[3], gain_grads, *arrays[4:])


def solution(mesh):
    fine = Mesh(mesh.devices.reshape(tuple(SIZE[a] for a in AXES)), AXES)
    dp, ctx = ("zl", "c"), ("y", "x", "zh")
    in_specs = (
        P(dp, ctx, None),
        P(AXES, None),
        P(AXES),
        P(AXES, None),
        P(None, AXES),
        P(AXES, None),
        P(AXES, None),
        P(AXES, None),
        P(dp, None),
        P(dp, ctx, None),
    )
    out_specs = (
        P(dp, ctx, None),
        P(dp, ctx, None),
        P(AXES, None),
        P(AXES),
        P(AXES, None),
        P(None, AXES),
        P(AXES, None),
        P(AXES, None),
        P(AXES, None),
    )
    return jax.shard_map(local, mesh=fine, in_specs=in_specs, out_specs=out_specs, check_vma=False)
```
